32 devices in a mesh: groups: 2 (over x), tm: 8 (over z, y), space: 2 (over core).
Axes of the slice: x: 2, y: 2, z: 4, core: 2. Of those that a mesh axis runs over, the one named last changes fastest.
Arguments:
- grad_out: bfloat16 [112, 128, 1024], P(('groups', 'tm'), 'space'), parts along dimension 0, may hold values from -6 to 6
- time_q: bfloat16 [112, 128, 1024], P(('groups', 'tm'), 'space'), parts along dimension 0, may hold values from -7 to 7
- time_k: bfloat16 [112, 128, 1024], P(('groups', 'tm'), 'space'), parts along dimension 0, may hold values from -7 to 7
- time_v: bfloat16 [112, 128, 1024], P(('groups', 'tm'), 'space'), parts along dimension 0, may hold values from -6 to 6
- space_q: bfloat16 [112, 128, 1024], P(('groups', 'tm'), 'space'), parts along dimension 0, may hold values from -7 to 7
- space_k: bfloat16 [112, 128, 1024], P(('groups', 'tm'), 'space'), parts along dimension 0, may hold values from -7 to 7
- space_v: bfloat16 [112, 128, 1024], P(('groups', 'tm'), 'space'), parts along dimension 0, may hold values from -6 to 6
- time_wo: bfloat16 [1024, 1024], P(('tm', 'space')), may hold values from -0.1875 to 0.1875
- space_wo: bfloat16 [1024, 1024], P(('tm', 'space')), may hold values from -0.1875 to 0.1875
Outputs:
- time_dq: bfloat16 [112, 128, 1024], P(('groups', 'tm'), 'space'), parts along dimension 0
- time_dk: bfloat16 [112, 128, 1024], P(('groups', 'tm'), 'space'), parts along dimension 0
- time_dv: bfloat16 [112, 128, 1024], P(('groups', 'tm'), 'space'), parts along dimension 0
- space_dq: bfloat16 [112, 128, 1024], P(('groups', 'tm'), 'space'), parts along dimension 0
- space_dk: bfloat16 [112, 128, 1024], P(('groups', 'tm'), 'space'), parts along dimension 0
- space_dv: bfloat16 [112, 128, 1024], P(('groups', 'tm'), 'space'), parts along dimension 0
The draws below stay inside these ranges and needn't reach their ends.
There are 2 independent parts, one for each index of `groups`. The reference program is written for one: setup_inputs(seed, part) draws one part's arguments, and reference() takes and returns one part's arrays. A program takes and returns all parts, laid end to end along the dimension named above; an argument that names none is the same for every part. Nothing has to cross between parts.
All inputs are finite; a program needn't handle non-finite values.
Results may differ from the reference program's by a relative error of at most 0.011.
Values may be sent and summed in bfloat16 or wider, within the bound.
No kernel may reach another device: no remote copies, remote signals or barrier semaphores. Data moves between devices by JAX's collectives and lax.ppermute only.
A program may use at most 128 MiB of HBM per device.

```python
import math
import jax
import jax.numpy as jnp
from jax import lax

D = 1024
HEADS = 16
HEAD_DIM = 64
FRAMES = 56
PATCHES = 128


def drawn_values(key):
    return jnp.clip(jax.random.normal(key, (FRAMES, PATCHES, D), jnp.float32), -6.0, 6.0)


def draw_time_q(key, part):
    key = jax.random.fold_in(key, 1)
    drawn = drawn_values(key)
    return drawn.astype(jnp.bfloat16)


def draw_time_k(key, part):
    key = jax.random.fold_in(key, 2)
    drawn = drawn_values(key)
    return drawn.astype(jnp.bfloat16)


def draw_space_q(key, part):
    key = jax.random.fold_in(key, 3)
    drawn = drawn_values(key)
    return drawn.astype(jnp.bfloat16)


def draw_space_k(key, part):
    key = jax.random.fold_in(key, 4)
    drawn = drawn_values(key)
    return drawn.astype(jnp.bfloat16)


def block_levels(own_key, extent, shards, smallest, high):
    factor_of, own = 1.0, jax.random.fold_in(own_key, 6)
    for dim, parts in shards:
        steps = jnp.exp(jax.random.uniform(jax.random.fold_in(own, dim), (parts,), jnp.float32, smallest / len(shards), high / len(shards)))
        factor_of = factor_of * jnp.repeat(steps, extent[dim] // parts).reshape([-1 if axis == dim else 1 for axis in range(len(extent))])
    return factor_of


def normal_values(stream_key, extent, spread, most, pieces=(), kind=jnp.bfloat16):
    values = spread * jax.random.normal(stream_key, extent, jnp.float32)
    if pieces:
        values = values * block_levels(stream_key, extent, pieces, -0.22, 0.18)
    return jnp.clip(values, -most, most).astype(kind)


def setup_inputs(seed: int = 0, part: int = 0) -> dict:
    streams_of = jax.random.split(jax.random.key(seed), 10)
    part_splits = jax.random.split(jax.random.fold_in(streams_of[9], part), 10)
    grad_out = normal_values(part_splits[0], (FRAMES, PATCHES, D), 1.0, 6.0, ((0, 8), (1, 2)))
    time_q = draw_time_q(jax.random.fold_in(jax.random.fold_in(streams_of[9], part), 71), part)
    time_k = draw_time_k(jax.random.fold_in(jax.random.fold_in(streams_of[9], part), 71), part)
    time_v = normal_values(part_splits[3], (FRAMES, PATCHES, D), 1.0, 6.0, ((0, 8), (1, 2)))
    space_q = draw_space_q(jax.random.fold_in(jax.random.fold_in(streams_of[9], part), 71), part)
    space_k = draw_space_k(jax.random.fold_in(jax.random.fold_in(streams_of[9], part), 71), part)
    space_v = normal_values(part_splits[6], (FRAMES, PATCHES, D), 1.0, 6.0, ((0, 8), (1, 2)))
    time_wo = normal_values(streams_of[7], (D, D), D ** -0.5, 0.1875, ((0, 16),))
    space_wo = normal_values(streams_of[8], (D, D), D ** -0.5, 0.1875, ((0, 16),))
    return dict(grad_out=grad_out, time_q=time_q, time_k=time_k, time_v=time_v, space_q=space_q, space_k=space_k, space_v=space_v, time_wo=time_wo, space_wo=space_wo)


def attend_back(query, keys, values, out_grad, layout):
    key_layout = layout.replace('s', 't')
    batch_letters = ''.join([letter for letter in layout if letter not in 'se'])
    score_layout = batch_letters + 'st'
    score_scale = 1.0 / math.sqrt(query.shape[-1])
    query_wide = query.astype(jnp.float32)
    keys_wide = keys.astype(jnp.float32)
    values_wide = values.astype(jnp.float32)
    grad_wide = out_grad.astype(jnp.float32)
    scores = jnp.einsum(layout + ',' + key_layout + '->' + score_layout, query_wide, keys_wide) * score_scale
    row_max = lax.optimization_barrier(jnp.max(scores, axis=-1, keepdims=True))
    expo = jnp.exp(scores - row_max)
    probs = expo / lax.optimization_barrier(jnp.sum(expo, axis=-1, keepdims=True))
    probs_low = lax.optimization_barrier(probs.astype(jnp.bfloat16)).astype(jnp.float32)
    grad_values = jnp.einsum(score_layout + ',' + layout + '->' + key_layout, probs_low, grad_wide)
    dprob = jnp.einsum(layout + ',' + key_layout + '->' + score_layout, grad_wide, values_wide)
    delta = lax.optimization_barrier(jnp.sum(probs * dprob, axis=-1, keepdims=True))
    dscore = lax.optimization_barrier((probs * (dprob - delta)).astype(jnp.bfloat16)).astype(jnp.float32)
    grad_query = score_scale * jnp.einsum(score_layout + ',' + key_layout + '->' + layout, dscore, keys_wide)
    grad_keys = score_scale * jnp.einsum(score_layout + ',' + layout + '->' + key_layout, dscore, query_wide)
    return (grad_query, grad_keys, grad_values)

def run_block(inputs):
    query, keys, values, out_grad = inputs
    results = attend_back(query, keys, values, out_grad, 'sbe')
    return (results[0].astype(jnp.bfloat16), results[1].astype(jnp.bfloat16), results[2].astype(jnp.bfloat16))

def reference(grad_out, time_q, time_k, time_v, space_q, space_k, space_v, time_wo, space_wo):
    tok_rows = grad_out.reshape(FRAMES * PATCHES, D)

    def project(weight_matrix):
        product = jnp.dot(tok_rows, weight_matrix.T, preferred_element_type=jnp.float32)
        return product.astype(jnp.bfloat16).reshape(FRAMES, PATCHES, HEADS, HEAD_DIM)

    def heads_view(tensor):
        return tensor.reshape(FRAMES, PATCHES, HEADS, HEAD_DIM)
    time_grad = project(time_wo)
    space_grad = project(space_wo)
    moved = tuple([jnp.moveaxis(tensor, 1, 0) for tensor in (heads_view(time_q), heads_view(time_k), heads_view(time_v), time_grad)])
    time_out = lax.map(run_block, moved)
    time_out = [jnp.moveaxis(tensor, 0, 1).reshape(FRAMES, PATCHES, D) for tensor in time_out]
    space_out = lax.map(run_block, (heads_view(space_q), heads_view(space_k), heads_view(space_v), space_grad))
    space_out = [tensor.reshape(FRAMES, PATCHES, D) for tensor in space_out]
    return (time_out[0], time_out[1], time_out[2], space_out[0], space_out[1], space_out[2])
```

```python
import functools
import math

import jax
import jax.numpy as jnp
from jax import lax
from jax.experimental import pallas as pl
from jax.experimental.pallas import tpu as pltpu
from jax.sharding import PartitionSpec as P

HEAD_DIM = 64
PAIR = 2 * HEAD_DIM
F32 = jnp.float32
BF16 = jnp.bfloat16
SCALE = 1.0 / math.sqrt(HEAD_DIM)


def dot(left, right, contract):
    return lax.dot_general(left, right, (contract, ((), ())), preferred_element_type=F32)


def pair_back(query, keys, values, out_grad):
    rows = query.shape[0]
    lane = lax.broadcasted_iota(jnp.int32, (rows, PAIR), 1)
    first = lane < HEAD_DIM

    def stacked(tensor):
        zero = jnp.zeros_like(tensor)
        both = [jnp.where(first, tensor, zero), jnp.where(first, zero, tensor)]
        return jnp.concatenate(both, axis=0).astype(BF16)

    query2 = stacked(query)
    grad2 = stacked(out_grad)
    keys = keys.astype(BF16)
    values = values.astype(BF16)
    scores = dot(keys, query2, ((1,), (1,))) * SCALE
    expo = jnp.exp(scores - jnp.max(scores, axis=0, keepdims=True))
    probs = expo * (1.0 / jnp.sum(expo, axis=0, keepdims=True))
    dprob = dot(values, grad2, ((1,), (1,)))
    delta = jnp.sum(probs * dprob, axis=0, keepdims=True)
    dscore = (probs * (dprob - delta)).astype(BF16)
    grad_values = dot(probs.astype(BF16), grad2, ((1,), (0,)))
    grad_keys = dot(dscore, query2, ((1,), (0,))) * SCALE
    both = dot(dscore, keys, ((0,), (0,))) * SCALE
    grad_query = jnp.where(first, both[:rows], both[rows:])
    return grad_query, grad_keys, grad_values


def time_kernel(qkv_ref, grad_ref, out_ref, *scratch):
    sources, frames, patches, lanes = grad_ref.shape
    total = sources * frames
    held, results = scratch[:4], scratch[4:]
    for pair in range(lanes // PAIR):
        columns = slice(pair * PAIR, (pair + 1) * PAIR)
        for index in range(4):
            part = qkv_ref[:, index, :, :, columns] if index < 3 else grad_ref[:, :, :, columns]
            held[index][pair] = part.astype(F32).reshape(total * patches, PAIR)
        for patch in range(patches):
            rows = pl.ds(patch, total, stride=patches)
            done = pair_back(*[ref[pair, rows, :] for ref in held])
            for ref, value in zip(results, done):
                ref[pair, rows, :] = value
        for index in range(3):
            value = results[index][pair].reshape(sources, frames, patches, PAIR)
            out_ref[:, index, :, :, columns] = value.astype(BF16)


def time_kernel_wide(qkv_ref, grad_ref, out_ref):
    done = pair_back(*[qkv_ref[index, 0].astype(F32) for index in range(3)], grad_ref[0].astype(F32))
    for index in range(3):
        out_ref[index, 0] = done[index].astype(BF16)


def time_attention(qkv, grad):
    sources, _, frames, patches, width = qkv.shape
    total = sources * frames
    if patches % 8 == 0:
        lanes = 2 * PAIR
        return pl.pallas_call(
            time_kernel,
            grid=(width // lanes,),
            in_specs=[
                pl.BlockSpec((sources, 3, frames, patches, lanes), lambda i: (0, 0, 0, 0, i)),
                pl.BlockSpec((sources, frames, patches, lanes), lambda i: (0, 0, 0, i)),
            ],
            out_specs=pl.BlockSpec((sources, 3, frames, patches, lanes), lambda i: (0, 0, 0, 0, i)),
            out_shape=jax.ShapeDtypeStruct(qkv.shape, BF16),
            scratch_shapes=[pltpu.VMEM((lanes // PAIR, total * patches, PAIR), F32)] * 7,
            compiler_params=pltpu.CompilerParams(vmem_limit_bytes=40 * 2**20),
            name="time_attention",
        )(qkv, grad)
    qkv = qkv.transpose(1, 3, 0, 2, 4).reshape(3, patches, total, width)
    grad = grad.transpose(2, 0, 1, 3).reshape(patches, total, width)
    done = pl.pallas_call(
        time_kernel_wide,
        grid=(patches, width // PAIR),
        in_specs=[
            pl.BlockSpec((3, 1, total, PAIR), lambda p, i: (0, p, 0, i)),
            pl.BlockSpec((1, total, PAIR), lambda p, i: (p, 0, i)),
        ],
        out_specs=pl.BlockSpec((3, 1, total, PAIR), lambda p, i: (0, p, 0, i)),
        out_shape=jax.ShapeDtypeStruct(qkv.shape, BF16),
        compiler_params=pltpu.CompilerParams(vmem_limit_bytes=40 * 2**20),
        name="time_attention_wide",
    )(qkv, grad)
    done = done.reshape(3, patches, sources, frames, width)
    return done.transpose(2, 0, 3, 1, 4)


def space_kernel(core_ref, q_ref, k_ref, v_ref, g_ref, qkv_ref, grad_ref, *outs):
    own_outs, send_ref = outs[:3], outs[3]
    rows, lanes = q_ref.shape[1:]
    own = (q_ref, k_ref, v_ref, g_ref)
    for pair in range(lanes // PAIR):
        columns = slice(pair * PAIR, (pair + 1) * PAIR)
        operands = []
        for index in range(4):
            near = own[index][0, :, columns].astype(F32)
            far = (qkv_ref[index, 0] if index < 3 else grad_ref[0])[:, columns].astype(F32)
            operands.append(jnp.concatenate([near, far], axis=0))
        done = pair_back(*operands)
        for index in range(3):
            value = done[index].astype(BF16)
            own_outs[index][0, :, columns] = value[:rows]
            send_ref[index, 0, :, columns] = value[rows:]


def space_attention(core, query, keys, values, grad, far_qkv, far_grad):
    frames, rows, width = query.shape
    half = width // 2
    mine = pl.BlockSpec((1, rows, half), lambda f, core_ref: (f, 0, core_ref[0]))
    far = pl.BlockSpec((1, rows, half), lambda f, core_ref: (f, 0, 0))
    far3 = pl.BlockSpec((3, 1, rows, half), lambda f, core_ref: (0, f, 0, 0))
    own_shape = jax.ShapeDtypeStruct((frames, rows, half), BF16)
    return pl.pallas_call(
        space_kernel,
        grid_spec=pltpu.PrefetchScalarGridSpec(
            num_scalar_prefetch=1,
            grid=(frames,),
            in_specs=[mine] * 4 + [far3, far],
            out_specs=[far] * 3 + [far3],
        ),
        out_shape=[own_shape] * 3 + [jax.ShapeDtypeStruct((3, frames, rows, half), BF16)],
        compiler_params=pltpu.CompilerParams(vmem_limit_bytes=40 * 2**20),
        name="space_attention",
    )(core.reshape(1), query, keys, values, grad, far_qkv, far_grad)


def per_device(sizes, grad_out, time_q, time_k, time_v, space_q, space_k, space_v, time_wo, space_wo):
    frames, rows, width = grad_out.shape
    groups, tm, space = sizes
    patches = rows // tm
    half = width // 2
    core = lax.axis_index("space")
    swap = [(0, 1), (1, 0)]

    def to_patches(tensor):
        split = tensor.reshape(tensor.shape[:-2] + (tm, patches, width))
        return jnp.moveaxis(split, -3, 0)

    def exchanged(tensor):
        return lax.all_to_all(tensor, "tm", split_axis=0, concat_axis=0, tiled=True)

    time_qkv = exchanged(to_patches(jnp.stack([time_q, time_k, time_v])))

    both_wo = jnp.concatenate([time_wo, space_wo], axis=1)
    share = both_wo.shape[0] // groups
    if share * groups == both_wo.shape[0]:
        piece = lax.dynamic_slice_in_dim(both_wo, lax.axis_index("groups") * share, share, 0)
        whole = lax.all_gather(piece, ("tm", "space", "groups"), axis=0, tiled=True)
    else:
        whole = lax.all_gather(both_wo, ("tm", "space"), axis=0, tiled=True)

    def other_half(tensor):
        return lax.dynamic_slice_in_dim(tensor, (1 - core) * half, half, tensor.ndim - 1)

    far_qkv = lax.ppermute(jnp.stack([other_half(t) for t in (space_q, space_k, space_v)]), "space", swap)

    tokens = grad_out.reshape(frames * rows, width)
    time_grad = jnp.einsum("td,cd->tc", tokens, whole[:, :width], preferred_element_type=F32)
    time_grad = exchanged(to_patches(time_grad.astype(BF16).reshape(frames, rows, width)))
    space_grad = jnp.einsum("td,cd->tc", tokens, whole[:, width:], preferred_element_type=F32)
    space_grad = space_grad.astype(BF16).reshape(frames, rows, width)
    far_grad = lax.ppermute(other_half(space_grad), "space", swap)

    *own, send = space_attention(core, space_q, space_k, space_v, space_grad, far_qkv, far_grad)
    far = lax.ppermute(send, "space", swap)
    space_out = [
        jnp.where(
            core == 0,
            jnp.concatenate([own[index], far[index]], axis=-1),
            jnp.concatenate([far[index], own[index]], axis=-1),
        )
        for index in range(3)
    ]

    back = exchanged(time_attention(time_qkv, time_grad))
    time_out = [jnp.moveaxis(back[:, index], 0, 1).reshape(frames, rows, width) for index in range(3)]
    return (*time_out, *space_out)


def solution(mesh):
    tokens = P(("groups", "tm"), "space", None)
    weights = P(("tm", "space"), None)
    sizes = tuple(mesh.shape[name] for name in ("groups", "tm", "space"))
    return jax.shard_map(
        functools.partial(per_device, sizes),
        mesh=mesh,
        in_specs=(tokens,) * 7 + (weights,) * 2,
        out_specs=(tokens,) * 6,
        check_vma=False,
    )
```

```python
import functools
import math

import jax
import jax.numpy as jnp
from jax import lax
from jax.experimental import pallas as pl
from jax.experimental.pallas import tpu as pltpu
from jax.sharding import PartitionSpec as P

HEAD_DIM = 64
PAIR = 2 * HEAD_DIM
F32 = jnp.float32
BF16 = jnp.bfloat16
SCALE = 1.0 / math.sqrt(HEAD_DIM)


def dot(left, right, contract):
    return lax.dot_general(left, right, (contract, ((), ())), preferred_element_type=F32)


def pair_back(query, keys, values, out_grad):
    rows = query.shape[0]
    lane = lax.broadcasted_iota(jnp.int32, (rows, PAIR), 1)
    first = lane < HEAD_DIM

    def stacked(tensor):
        zero = jnp.zeros_like(tensor)
        both = [jnp.where(first, tensor, zero), jnp.where(first, zero, tensor)]
        return jnp.concatenate(both, axis=0).astype(BF16)

    query2 = stacked(query)
    grad2 = stacked(out_grad)
    keys = keys.astype(BF16)
    values = values.astype(BF16)
    scores = dot(keys, query2, ((1,), (1,))) * SCALE
    expo = jnp.exp(scores - jnp.max(scores, axis=0, keepdims=True))
    probs = expo * (1.0 / jnp.sum(expo, axis=0, keepdims=True))
    dprob = dot(values, grad2, ((1,), (1,)))
    delta = jnp.sum(probs * dprob, axis=0, keepdims=True)
    dscore = (probs * (dprob - delta)).astype(BF16)
    grad_values = dot(probs.astype(BF16), grad2, ((1,), (0,)))
    grad_keys = dot(dscore, query2, ((1,), (0,))) * SCALE
    both = dot(dscore, keys, ((0,), (0,))) * SCALE
    grad_query = jnp.where(first, both[:rows], both[rows:])
    return grad_query, grad_keys, grad_values


def time_kernel(qkv_ref, grad_ref, out_ref, *scratch):
    sources, frames, patches, lanes = grad_ref.shape
    total = sources * frames
    held, results = scratch[:4], scratch[4:]
    for pair in range(lanes // PAIR):
        columns = slice(pair * PAIR, (pair + 1) * PAIR)
        for index in range(4):
            part = qkv_ref[:, index, :, :, columns] if index < 3 else grad_ref[:, :, :, columns]
            held[index][pair] = part.astype(F32).reshape(total * patches, PAIR)
        for patch in range(patches):
            rows = pl.ds(patch, total, stride=patches)
            done = pair_back(*[ref[pair, rows, :] for ref in held])
            for ref, value in zip(results, done):
                ref[pair, rows, :] = value
        for index in range(3):
            value = results[index][pair].reshape(sources, frames, patches, PAIR)
            out_ref[:, index, :, :, columns] = value.astype(BF16)


def time_kernel_wide(qkv_ref, grad_ref, out_ref):
    done = pair_back(*[qkv_ref[index, 0].astype(F32) for index in range(3)], grad_ref[0].astype(F32))
    for index in range(3):
        out_ref[index, 0] = done[index].astype(BF16)


def time_attention(qkv, grad):
    sources, _, frames, patches, width = qkv.shape
    total = sources * frames
    if patches % 8 == 0:
        lanes = 2 * PAIR
        return pl.pallas_call(
            time_kernel,
            grid=(width // lanes,),
            in_specs=[
                pl.BlockSpec((sources, 3, frames, patches, lanes), lambda i: (0, 0, 0, 0, i)),
                pl.BlockSpec((sources, frames, patches, lanes), lambda i: (0, 0, 0, i)),
            ],
            out_specs=pl.BlockSpec((sources, 3, frames, patches, lanes), lambda i: (0, 0, 0, 0, i)),
            out_shape=jax.ShapeDtypeStruct(qkv.shape, BF16),
            scratch_shapes=[pltpu.VMEM((lanes // PAIR, total * patches, PAIR), F32)] * 7,
            compiler_params=pltpu.CompilerParams(vmem_limit_bytes=40 * 2**20),
            name="time_attention",
        )(qkv, grad)
    qkv = qkv.transpose(1, 3, 0, 2, 4).reshape(3, patches, total, width)
    grad = grad.transpose(2, 0, 1, 3).reshape(patches, total, width)
    done = pl.pallas_call(
        time_kernel_wide,
        grid=(patches, width // PAIR),
        in_specs=[
            pl.BlockSpec((3, 1, total, PAIR), lambda p, i: (0, p, 0, i)),
            pl.BlockSpec((1, total, PAIR), lambda p, i: (p, 0, i)),
        ],
        out_specs=pl.BlockSpec((3, 1, total, PAIR), lambda p, i: (0, p, 0, i)),
        out_shape=jax.ShapeDtypeStruct(qkv.shape, BF16),
        compiler_params=pltpu.CompilerParams(vmem_limit_bytes=40 * 2**20),
        name="time_attention_wide",
    )(qkv, grad)
    done = done.reshape(3, patches, sources, frames, width)
    return done.transpose(2, 0, 3, 1, 4)


def space_kernel(core_ref, q_ref, k_ref, v_ref, g_ref, qkv_ref, grad_ref, *outs):
    own_outs, send_ref = outs[:3], outs[3]
    rows, lanes = q_ref.shape[1:]
    own = (q_ref, k_ref, v_ref, g_ref)
    for pair in range(lanes // PAIR):
        columns = slice(pair * PAIR, (pair + 1) * PAIR)
        operands = []
        for index in range(4):
            near = own[index][0, :, columns].astype(F32)
            far = (qkv_ref[index, 0] if index < 3 else grad_ref[0])[:, columns].astype(F32)
            operands.append(jnp.concatenate([near, far], axis=0))
        done = pair_back(*operands)
        for index in range(3):
            value = done[index].astype(BF16)
            own_outs[index][0, :, columns] = value[:rows]
            send_ref[index, 0, :, columns] = value[rows:]


def space_attention(core, query, keys, values, grad, far_qkv, far_grad):
    frames, rows, width = query.shape
    half = width // 2
    mine = pl.BlockSpec((1, rows, half), lambda f, core_ref: (f, 0, core_ref[0]))
    far = pl.BlockSpec((1, rows, half), lambda f, core_ref: (f, 0, 0))
    far3 = pl.BlockSpec((3, 1, rows, half), lambda f, core_ref: (0, f, 0, 0))
    own_shape = jax.ShapeDtypeStruct((frames, rows, half), BF16)
    return pl.pallas_call(
        space_kernel,
        grid_spec=pltpu.PrefetchScalarGridSpec(
            num_scalar_prefetch=1,
            grid=(frames,),
            in_specs=[mine] * 3 + [far, far3, far],
            out_specs=[far] * 3 + [far3],
        ),
        out_shape=[own_shape] * 3 + [jax.ShapeDtypeStruct((3, frames, rows, half), BF16)],
        compiler_params=pltpu.CompilerParams(vmem_limit_bytes=40 * 2**20),
        name="space_attention",
    )(core.reshape(1), query, keys, values, grad, far_qkv, far_grad)


HBM = pl.BlockSpec(memory_space=pl.ANY)
SCALARS = pl.BlockSpec(memory_space=pltpu.SMEM)
WHOLE = pl.BlockSpec(memory_space=pltpu.VMEM)
BIG = pltpu.CompilerParams(vmem_limit_bytes=48 * 2**20)


def run_copies(sem, pairs):
    copies = [pltpu.make_async_copy(src, dst, sem) for src, dst in pairs]
    for copy in copies:
        copy.start()
    for copy in copies:
        copy.wait()


def packed(spots, parts, shape, place, name, after=()):
    def kernel(spots_ref, *refs):
        run_copies(refs[-1], place(spots_ref, refs[: len(parts)], refs[-2]))

    return pl.pallas_call(
        kernel,
        in_specs=[SCALARS] + [HBM] * (len(parts) + len(after)),
        out_specs=HBM,
        out_shape=jax.ShapeDtypeStruct(shape, BF16),
        scratch_shapes=[pltpu.SemaphoreType.DMA],
        name=name,
    )(spots, *parts, *after)


def load_weights(spots_ref, near_ref, far_ref, weights, sem, base):
    near_count = near_ref.shape[0]
    pairs = []
    for index in range(near_count):
        pairs.append((near_ref.at[index], weights.at[spots_ref[base + index]]))
        pairs.append((far_ref.at[index], weights.at[spots_ref[base + near_count + index]]))
    run_copies(sem, pairs)


def attend_pair(held, results, patches, total):
    for patch in range(patches):
        rows = pl.ds(patch, total, stride=patches)
        done = pair_back(*[ref[rows, :] for ref in held])
        for ref, value in zip(results, done):
            ref[rows, :] = value


def time_chunk(spots, base, blocks, near, far, late_grad, name):
    count = len(blocks)
    kinds, frames, patches, lanes = blocks[0].shape
    total, part = count * frames, frames * patches
    rows = total * patches
    first = late_grad is None
    width = 2 * lanes

    def kernel(spots_ref, *refs):
        refs = list(refs)
        block_refs = [refs.pop(0) for _ in range(count)]
        extra = [refs.pop(0) for _ in range(2 if first else 1)]
        out_refs = [refs.pop(0) for _ in range(count)]
        later_ref = refs.pop(0) if first else None
        held = [refs.pop(0) for _ in range(4)]
        results = [refs.pop(0) for _ in range(3)]
        if first:
            tokens, weights, sem = refs
            load_weights(spots_ref, extra[0], extra[1], weights, sem, base)
            for index, ref in enumerate(block_refs):
                at = slice(index * part, (index + 1) * part)
                for side in range(2):
                    value = ref[3 + side].astype(F32).reshape(part, lanes)
                    tokens[at, side * lanes : (side + 1) * lanes] = value.astype(BF16)
            features = weights.shape[0] * weights.shape[1]
            later = weights[weights.shape[0] // 2 :].reshape(features // 2, width)
            later_ref[...] = dot(tokens[...], later, ((1,), (1,))).astype(BF16)

        def one_pair(pair, carry):
            columns = pl.ds(pl.multiple_of(pair * PAIR, PAIR), PAIR)
            for index, ref in enumerate(block_refs):
                at = slice(index * part, (index + 1) * part)
                for kind in range(3):
                    held[kind][at, :] = ref[kind, :, :, columns].astype(F32).reshape(part, PAIR)
            if first:
                share = weights.shape[1]
                pieces = weights[pl.ds(pair * (PAIR // share), PAIR // share)].reshape(PAIR, width)
                held[3][...] = dot(tokens[...], pieces, ((1,), (1,))).astype(BF16).astype(F32)
            else:
                held[3][...] = extra[0][:, columns].astype(F32)
            attend_pair(held, results, patches, total)
            for index, ref in enumerate(out_refs):
                at = slice(index * part, (index + 1) * part)
                for kind in range(3):
                    value = results[kind][at, :].reshape(frames, patches, PAIR)
                    ref[kind, :, :, columns] = value.astype(BF16)
            return carry

        lax.fori_loop(0, lanes // PAIR, one_pair, 0)

    out_shapes = [jax.ShapeDtypeStruct((3, frames, patches, lanes), BF16)] * count
    scratch = [pltpu.VMEM((rows, PAIR), F32)] * 7
    if first:
        operands, specs = (near, far), [HBM, HBM]
        out_shapes = out_shapes + [jax.ShapeDtypeStruct((rows, lanes), BF16)]
        pieces = (2 * near.shape[0],) + near.shape[1:]
        scratch = scratch + [pltpu.VMEM((rows, width), BF16), pltpu.VMEM(pieces, BF16), pltpu.SemaphoreType.DMA]
    else:
        operands, specs = (late_grad,), [WHOLE]
    return pl.pallas_call(
        kernel,
        in_specs=[SCALARS] + [WHOLE] * count + specs,
        out_specs=[WHOLE] * len(out_shapes),
        out_shape=out_shapes,
        scratch_shapes=scratch,
        compiler_params=BIG,
        name=name,
    )(spots, *blocks, *operands)


def space_project(spots, base, core_at, tokens, near, far, after):
    frames, rows, width = tokens.shape
    half = width // 2

    def kernel(spots_ref, token_ref, near_ref, far_ref, after_ref, own_ref, send_ref, weights, sem):
        load_weights(spots_ref, near_ref, far_ref, weights, sem, base)
        flat = token_ref[...].reshape(frames * rows, width)
        pieces = weights.shape[0] // 2
        core = spots_ref[core_at]
        for ref, side in ((send_ref, 1 - core), (own_ref, core)):
            part = weights[pl.ds(side * pieces, pieces)].reshape(half, width)
            ref[...] = dot(flat, part, ((1,), (1,))).astype(BF16).reshape(frames, rows, half)

    pieces = (2 * near.shape[0],) + near.shape[1:]
    return pl.pallas_call(
        kernel,
        in_specs=[SCALARS, WHOLE, HBM, HBM, HBM],
        out_specs=[WHOLE, WHOLE],
        out_shape=[jax.ShapeDtypeStruct((frames, rows, half), BF16)] * 2,
        scratch_shapes=[pltpu.VMEM(pieces, BF16), pltpu.SemaphoreType.DMA],
        compiler_params=BIG,
        name="space_project",
    )(spots, tokens, near, far, after)


def placed(spots, blocks, outs, chunk, shape, name):
    count = len(blocks)
    lanes = blocks[0].shape[-1]
    kept = outs is not None

    def kernel(spots_ref, *refs):
        block_refs, sem, out_refs = refs[:count], refs[-1], refs[-4:-1]
        columns = pl.ds(chunk * lanes, lanes)
        pairs = []
        for index, ref in enumerate(block_refs):
            for kind in range(3):
                pairs.append((ref.at[kind], out_refs[kind].at[:, spots_ref[index], :, columns]))
        run_copies(sem, pairs)

    return pl.pallas_call(
        kernel,
        in_specs=[SCALARS] + [HBM] * (count + (3 if kept else 0)),
        out_specs=[HBM] * 3,
        out_shape=[jax.ShapeDtypeStruct(shape, BF16)] * 3,
        scratch_shapes=[pltpu.SemaphoreType.DMA],
        input_output_aliases={1 + count + kind: kind for kind in range(3)} if kept else {},
        name=name,
    )(spots, *blocks, *(outs or ()))


def per_device(sizes, grad_out, time_q, time_k, time_v, space_q, space_k, space_v, time_wo, space_wo):
    frames, rows, width = grad_out.shape
    groups, tm, space = sizes
    patches, half = rows // tm, width // 2
    group, me, core = (lax.axis_index(name) for name in ("groups", "tm", "space"))
    steps = tm // 2
    share = time_wo.shape[0] // groups
    swap = [(0, 1), (1, 0)]

    near_places = []
    for far_core in range(2):
        for hop in range(4):
            for step in range(steps):
                owner = (me ^ (2 * step) ^ (hop & 1)) * 2 + (core ^ far_core)
                near_places.append(owner * 2 + (group ^ (hop >> 1)))
    spots = jnp.stack([me ^ k for k in range(tm)] + near_places + [core, group]).astype(jnp.int32)
    base, core_at = tm, tm + len(near_places)
    group_at = core_at + 1

    def to_partner(tensor, k):
        return lax.ppermute(tensor, "tm", [(i, i ^ k) for i in range(tm)])

    def to_hop(tensor, hop):
        pairs = [
            (g * tm + t, (g ^ (hop >> 1)) * tm + (t ^ (hop & 1))) for g in range(groups) for t in range(tm)
        ]
        return lax.ppermute(tensor, ("groups", "tm"), pairs)

    piece = packed(
        spots,
        [tensor.reshape(groups, share, width) for tensor in (time_wo, space_wo)],
        (2, share, width),
        lambda at, parts, out: [(part.at[at[group_at]], out.at[i]) for i, part in enumerate(parts)],
        "own_piece",
    )
    stage1 = [piece] + [to_partner(piece, 2 * step) for step in range(1, steps)]

    split = [t.reshape(frames, tm, patches, width) for t in (time_q, time_k, time_v, grad_out)]
    order = sorted(range(tm), reverse=True)

    def payload(k, chunk, after=()):
        def place(at, parts, out):
            columns = pl.ds(chunk * half, half)
            pairs = [(part.at[:, at[k], :, columns], out.at[i]) for i, part in enumerate(parts[:3])]
            if chunk == 0:
                for side in range(2):
                    pairs.append((parts[3].at[:, at[k], :, pl.ds(side * half, half)], out.at[3 + side]))
            return pairs

        kinds = 5 if chunk == 0 else 3
        return packed(spots, split, (kinds, frames, patches, half), place, "payload", after)

    early, late = [None] * tm, [None] * tm
    for k in order:
        sent = payload(k, 0)
        early[k] = to_partner(sent, k) if k else sent

    def other_half(parts, shape, name):
        def place(at, refs, out):
            columns = pl.ds(pl.multiple_of((1 - at[core_at]) * half, half), half)
            return [(ref.at[:, :, columns], out.at[i]) for i, ref in enumerate(refs)]

        return packed(spots, parts, shape, place, name)

    far_qkv = lax.ppermute(
        other_half([space_q, space_k, space_v], (3, frames, rows, half), "space_payload"), "space", swap
    )

    def gathered(which):
        mine = packed(
            spots,
            stage1,
            (steps, share, width),
            lambda at, parts, out: [(part.at[which], out.at[i]) for i, part in enumerate(parts)],
            "stage_two",
        )
        quarters = [mine] + [to_hop(mine, hop) for hop in range(1, 4)]
        near = packed(
            spots,
            quarters,
            (4 * steps, share, width),
            lambda at, parts, out: [(part, out.at[pl.ds(i * steps, steps)]) for i, part in enumerate(parts)],
            "stage_three",
        )
        return near, lax.ppermute(near, "space", swap)

    time_near, time_far = gathered(0)
    space_near, space_far = gathered(1)

    for k in order:
        sent = payload(k, 1, (early[k],))
        late[k] = to_partner(sent, k) if k else sent

    *done, late_grad = time_chunk(spots, base, early, time_near, time_far, None, "time_first")
    back = [to_partner(done[k], k) if k else done[k] for k in range(tm)]

    own_grad, send_grad = space_project(spots, base, core_at, grad_out, space_near, space_far, done[0])
    far_grad = lax.ppermute(send_grad, "space", swap)
    *own, send = space_attention(core, space_q, space_k, space_v, own_grad, far_qkv, far_grad)
    far = lax.ppermute(send, "space", swap)
    space_out = [
        jnp.where(
            core == 0,
            jnp.concatenate([own[index], far[index]], axis=-1),
            jnp.concatenate([far[index], own[index]], axis=-1),
        )
        for index in range(3)
    ]

    done = time_chunk(spots, base, late, None, None, late_grad, "time_second")
    back2 = [to_partner(done[k], k) if k else done[k] for k in range(tm)]
    shape = (frames, tm, patches, width)
    outs = placed(spots, back, None, 0, shape, "place_first")
    outs = placed(spots, back2, outs, 1, shape, "place_second")
    time_out = [out.reshape(frames, rows, width) for out in outs]
    return (*time_out, *space_out)


def per_device_plain(sizes, grad_out, time_q, time_k, time_v, space_q, space_k, space_v, time_wo, space_wo):
    frames, rows, width = grad_out.shape
    groups, tm, space = sizes
    patches = rows // tm
    half = width // 2
    core = lax.axis_index("space")
    swap = [(0, 1), (1, 0)]

    def to_patches(tensor):
        split = tensor.reshape(tensor.shape[:-2] + (tm, patches, width))
        return jnp.moveaxis(split, -3, 0)

    def exchanged(tensor):
        return lax.all_to_all(tensor, "tm", split_axis=0, concat_axis=0, tiled=True)

    time_qkv = exchanged(to_patches(jnp.stack([time_q, time_k, time_v])))

    both_wo = jnp.concatenate([time_wo, space_wo], axis=1)
    share = both_wo.shape[0] // groups
    if share * groups == both_wo.shape[0]:
        piece = lax.dynamic_slice_in_dim(both_wo, lax.axis_index("groups") * share, share, 0)
        whole = lax.all_gather(piece, ("tm", "space", "groups"), axis=0, tiled=True)
    else:
        whole = lax.all_gather(both_wo, ("tm", "space"), axis=0, tiled=True)

    def other_half(tensor):
        return lax.dynamic_slice_in_dim(tensor, (1 - core) * half, half, tensor.ndim - 1)

    far_qkv = lax.ppermute(jnp.stack([other_half(t) for t in (space_q, space_k, space_v)]), "space", swap)

    tokens = grad_out.reshape(frames * rows, width)
    time_grad = jnp.einsum("td,cd->tc", tokens, whole[:, :width], preferred_element_type=F32)
    time_grad = exchanged(to_patches(time_grad.astype(BF16).reshape(frames, rows, width)))
    space_grad = jnp.einsum("td,cd->tc", tokens, whole[:, width:], preferred_element_type=F32)
    space_grad = space_grad.astype(BF16).reshape(frames, rows, width)
    far_grad = lax.ppermute(other_half(space_grad), "space", swap)

    own_grad = lax.dynamic_slice_in_dim(space_grad, core * half, half, 2)
    *own, send = space_attention(core, space_q, space_k, space_v, own_grad, far_qkv, far_grad)
    far = lax.ppermute(send, "space", swap)
    space_out = [
        jnp.where(
            core == 0,
            jnp.concatenate([own[index], far[index]], axis=-1),
            jnp.concatenate([far[index], own[index]], axis=-1),
        )
        for index in range(3)
    ]

    back = exchanged(time_attention(time_qkv, time_grad))
    time_out = [jnp.moveaxis(back[:, index], 0, 1).reshape(frames, rows, width) for index in range(3)]
    return (*time_out, *space_out)


def solution(mesh):
    tokens = P(("groups", "tm"), "space", None)
    weights = P(("tm", "space"), None)
    sizes = tuple(mesh.shape[name] for name in ("groups", "tm", "space"))
    groups, tm, space = sizes
    paired = groups == 2 and space == 2 and tm % 2 == 0 and tm & (tm - 1) == 0

    def body(*tensors):
        patches, rows = tensors[0].shape[1] // tm, tensors[-1].shape[0]
        fits = paired and patches % 8 == 0 and rows % (16 * groups) == 0
        return (per_device if fits else per_device_plain)(sizes, *tensors)

    return jax.shard_map(
        body,
        mesh=mesh,
        in_specs=(tokens,) * 7 + (weights,) * 2,
        out_specs=(tokens,) * 6,
        check_vma=False,
    )
```

```python
import functools
import math

import jax
import jax.numpy as jnp
from jax import lax
from jax.experimental import pallas as pl
from jax.experimental.pallas import tpu as pltpu
from jax.sharding import PartitionSpec as P

HEAD_DIM = 64
PAIR = 2 * HEAD_DIM
F32 = jnp.float32
BF16 = jnp.bfloat16
SCALE = 1.0 / math.sqrt(HEAD_DIM)


def dot(left, right, contract):
    return lax.dot_general(left, right, (contract, ((), ())), preferred_element_type=F32)


def pair_back(query, keys, values, out_grad):
    rows = query.shape[0]
    lane = lax.broadcasted_iota(jnp.int32, (rows, PAIR), 1)
    first = lane < HEAD_DIM

    def stacked(tensor):
        zero = jnp.zeros_like(tensor)
        both = [jnp.where(first, tensor, zero), jnp.where(first, zero, tensor)]
        return jnp.concatenate(both, axis=0).astype(BF16)

    query2 = stacked(query)
    grad2 = stacked(out_grad)
    keys = keys.astype(BF16)
    values = values.astype(BF16)
    scores = dot(keys, query2, ((1,), (1,))) * SCALE
    expo = jnp.exp(scores - jnp.max(scores, axis=0, keepdims=True))
    probs = expo * (1.0 / jnp.sum(expo, axis=0, keepdims=True))
    dprob = dot(values, grad2, ((1,), (1,)))
    delta = jnp.sum(probs * dprob, axis=0, keepdims=True)
    dscore = (probs * (dprob - delta)).astype(BF16)
    grad_values = dot(probs.astype(BF16), grad2, ((1,), (0,)))
    grad_keys = dot(dscore, query2, ((1,), (0,))) * SCALE
    both = dot(dscore, keys, ((0,), (0,))) * SCALE
    grad_query = jnp.where(first, both[:rows], both[rows:])
    return grad_query, grad_keys, grad_values


def time_kernel(qkv_ref, grad_ref, out_ref, *scratch):
    sources, frames, patches, lanes = grad_ref.shape
    total = sources * frames
    held, results = scratch[:4], scratch[4:]
    for pair in range(lanes // PAIR):
        columns = slice(pair * PAIR, (pair + 1) * PAIR)
        for index in range(4):
            part = qkv_ref[:, index, :, :, columns] if index < 3 else grad_ref[:, :, :, columns]
            held[index][pair] = part.astype(F32).reshape(total * patches, PAIR)
        for patch in range(patches):
            rows = pl.ds(patch, total, stride=patches)
            done = pair_back(*[ref[pair, rows, :] for ref in held])
            for ref, value in zip(results, done):
                ref[pair, rows, :] = value
        for index in range(3):
            value = results[index][pair].reshape(sources, frames, patches, PAIR)
            out_ref[:, index, :, :, columns] = value.astype(BF16)


def time_kernel_wide(qkv_ref, grad_ref, out_ref):
    done = pair_back(*[qkv_ref[index, 0].astype(F32) for index in range(3)], grad_ref[0].astype(F32))
    for index in range(3):
        out_ref[index, 0] = done[index].astype(BF16)


def time_attention(qkv, grad):
    sources, _, frames, patches, width = qkv.shape
    total = sources * frames
    if patches % 8 == 0:
        lanes = 2 * PAIR
        return pl.pallas_call(
            time_kernel,
            grid=(width // lanes,),
            in_specs=[
                pl.BlockSpec((sources, 3, frames, patches, lanes), lambda i: (0, 0, 0, 0, i)),
                pl.BlockSpec((sources, frames, patches, lanes), lambda i: (0, 0, 0, i)),
            ],
            out_specs=pl.BlockSpec((sources, 3, frames, patches, lanes), lambda i: (0, 0, 0, 0, i)),
            out_shape=jax.ShapeDtypeStruct(qkv.shape, BF16),
            scratch_shapes=[pltpu.VMEM((lanes // PAIR, total * patches, PAIR), F32)] * 7,
            compiler_params=pltpu.CompilerParams(vmem_limit_bytes=40 * 2**20),
            name="time_attention",
        )(qkv, grad)
    qkv = qkv.transpose(1, 3, 0, 2, 4).reshape(3, patches, total, width)
    grad = grad.transpose(2, 0, 1, 3).reshape(patches, total, width)
    done = pl.pallas_call(
        time_kernel_wide,
        grid=(patches, width // PAIR),
        in_specs=[
            pl.BlockSpec((3, 1, total, PAIR), lambda p, i: (0, p, 0, i)),
            pl.BlockSpec((1, total, PAIR), lambda p, i: (p, 0, i)),
        ],
        out_specs=pl.BlockSpec((3, 1, total, PAIR), lambda p, i: (0, p, 0, i)),
        out_shape=jax.ShapeDtypeStruct(qkv.shape, BF16),
        compiler_params=pltpu.CompilerParams(vmem_limit_bytes=40 * 2**20),
        name="time_attention_wide",
    )(qkv, grad)
    done = done.reshape(3, patches, sources, frames, width)
    return done.transpose(2, 0, 3, 1, 4)


def own_back(queries, keys, values, grads):
    rows = queries[0].shape[0]
    first = lax.broadcasted_iota(jnp.int32, (rows, PAIR), 1) < HEAD_DIM
    zero = jnp.zeros((rows, PAIR), F32)

    def stacked(parts):
        both = []
        for part in parts:
            both += [jnp.where(first, part, zero), jnp.where(first, zero, part)]
        return jnp.concatenate(both, axis=0).astype(BF16)

    query2, grad2 = stacked(queries), stacked(grads)
    keys = jnp.concatenate(keys, axis=0).astype(BF16)
    values = jnp.concatenate(values, axis=0).astype(BF16)
    scores = dot(keys, query2, ((1,), (1,))) * SCALE
    expo = jnp.exp(scores - jnp.max(scores, axis=0, keepdims=True))
    probs = expo * (1.0 / jnp.sum(expo, axis=0, keepdims=True))
    dprob = dot(values, grad2, ((1,), (1,)))
    delta = jnp.sum(probs * dprob, axis=0, keepdims=True)
    dscore = (probs * (dprob - delta)).astype(BF16)
    grad_values = dot(probs[:rows].astype(BF16), grad2, ((1,), (0,)))
    grad_keys = dot(dscore[:rows], query2, ((1,), (0,))) * SCALE
    both = dot(dscore[:, : 2 * rows], keys, ((0,), (0,))) * SCALE
    grad_query = jnp.where(first, both[:rows], both[rows:])
    return grad_query, grad_keys, grad_values


HBM = pl.BlockSpec(memory_space=pltpu.HBM)
SCALARS = pl.BlockSpec(memory_space=pltpu.SMEM)
BIG = pltpu.CompilerParams(vmem_limit_bytes=48 * 2**20)


def cost_of(microseconds):
    return pl.CostEstimate(flops=0, transcendentals=0, bytes_accessed=int(microseconds * 3_690_000))


def run_copies(sems, pairs):
    copies = [pltpu.make_async_copy(src, dst, sems.at[i]) for i, (src, dst) in enumerate(pairs)]
    for copy in copies:
        copy.start()
    return copies


def run_staged(pairs):
    count = len(pairs)

    def body(*scratch):
        stages, arrived, left = scratch[:count], scratch[count], scratch[count + 1]
        loads = run_copies(arrived, [(src, stage) for (src, _), stage in zip(pairs, stages)])
        stores = []
        for index, (load, (_, dst)) in enumerate(zip(loads, pairs)):
            load.wait()
            stores.append(pltpu.make_async_copy(stages[index], dst, left.at[index]))
            stores[-1].start()
        for store in stores:
            store.wait()

    sems = [pltpu.SemaphoreType.DMA((count,))] * 2
    pl.run_scoped(body, *[pltpu.VMEM(src.shape, BF16) for src, _ in pairs], *sems)


def moved(spots, parts, shapes, plan, name, after=(), kept=()):
    count = len(parts)

    def kernel(spots_ref, *refs):
        run_staged(plan(spots_ref, refs[:count], refs[len(refs) - len(shapes) :]))

    return pl.pallas_call(
        kernel,
        in_specs=[SCALARS] + [HBM] * (count + len(after) + len(kept)),
        out_specs=[HBM] * len(shapes),
        out_shape=[jax.ShapeDtypeStruct(shape, BF16) for shape in shapes],
        input_output_aliases={1 + count + len(after) + i: i for i in range(len(kept))},
        compiler_params=BIG,
        name=name,
    )(spots, *parts, *after, *kept)


def weight_copies(gathered_ref, weights):
    space, groups, tm = gathered_ref.shape[:3]
    return [
        (gathered_ref.at[s, g, t], weights.at[(t * space + s) * groups + g])
        for t in range(tm)
        for s in range(space)
        for g in range(groups)
    ]


def attend_pair(held, results, patches, total):
    for patch in range(patches):
        rows = pl.ds(patch, total, stride=patches)
        done = pair_back(*[ref[rows, :] for ref in held])
        for ref, value in zip(results, done):
            ref[rows, :] = value


def time_chunk(blocks, gathered, late_grad, name):
    count = len(blocks)
    first = late_grad is None
    _, frames, patches, lanes = blocks[0].shape
    total, part = count * frames, frames * patches
    rows, width = total * patches, 2 * lanes
    wide = [pltpu.VMEM(block.shape, BF16) for block in blocks]
    scratch = wide + [pltpu.VMEM((3, frames, patches, lanes), BF16)] * count
    scratch += [pltpu.VMEM((rows, PAIR), F32)] * 7
    if first:
        space, groups, tm, share = gathered.shape[:4]
        scratch += [pltpu.VMEM((rows, width), BF16), pltpu.VMEM((space * groups * tm, share, width), BF16)]
        operands = (gathered,)
        copied = count + space * groups * tm
    else:
        scratch += [pltpu.VMEM((rows, lanes), BF16)]
        operands = (late_grad,)
        copied = count + 1
    scratch += [pltpu.SemaphoreType.DMA((copied,)), pltpu.SemaphoreType.DMA((count,))]

    def kernel(*refs):
        refs = list(refs)

        def take(number):
            taken, refs[:number] = refs[:number], []
            return taken

        block_refs, extra_ref, out_refs = take(count), take(1)[0], take(count)
        later_ref = take(1)[0] if first else None
        blocks_in, results_out = take(count), take(count)
        held, results = take(4), take(3)
        grads = take(1)[0]
        weights = take(1)[0] if first else None
        arrived, left = refs
        pairs = list(zip(block_refs, blocks_in))
        pairs += weight_copies(extra_ref, weights) if first else [(extra_ref, grads)]
        for copy in run_copies(arrived, pairs):
            copy.wait()
        if first:
            for index, ref in enumerate(blocks_in):
                at = slice(index * part, (index + 1) * part)
                for side in range(2):
                    value = ref[3 + side].astype(F32).reshape(part, lanes)
                    grads[at, side * lanes : (side + 1) * lanes] = value.astype(BF16)

        def one_pair(pair, carry):
            columns = pl.ds(pl.multiple_of(pair * PAIR, PAIR), PAIR)
            for index, ref in enumerate(blocks_in):
                at = slice(index * part, (index + 1) * part)
                for kind in range(3):
                    held[kind][at, :] = ref[kind, :, :, columns].astype(F32).reshape(part, PAIR)
            if first:
                pieces = weights[pl.ds(pair * (PAIR // share), PAIR // share)].reshape(PAIR, width)
                held[3][...] = dot(grads[...], pieces, ((1,), (1,))).astype(BF16).astype(F32)
            else:
                held[3][...] = grads[:, columns].astype(F32)
            attend_pair(held, results, patches, total)
            for index, ref in enumerate(results_out):
                at = slice(index * part, (index + 1) * part)
                for kind in range(3):
                    value = results[kind][at, :].reshape(frames, patches, PAIR)
                    ref[kind, :, :, columns] = value.astype(BF16)
            return carry

        lax.fori_loop(0, lanes // PAIR, one_pair, 0)
        stores = run_copies(left, list(zip(results_out, out_refs)))
        if first:
            half = weights.shape[0] // 2
            later = weights[half:].reshape(lanes, width)
            later_ref[...] = dot(grads[...], later, ((1,), (1,))).astype(BF16)
        for store in stores:
            store.wait()

    out_shapes = [jax.ShapeDtypeStruct((3, frames, patches, lanes), BF16)] * count
    out_specs = [HBM] * count
    if first:
        out_shapes = out_shapes + [jax.ShapeDtypeStruct((rows, lanes), BF16)]
        out_specs = out_specs + [pl.BlockSpec(memory_space=pltpu.VMEM)]
    return pl.pallas_call(
        kernel,
        in_specs=[HBM] * (count + 1),
        out_specs=out_specs,
        out_shape=out_shapes,
        scratch_shapes=scratch,
        compiler_params=BIG,
        cost_estimate=cost_of(16 if first else 10),
        name=name,
    )(*blocks, *operands)


def space_attention(spots, core_at, own, far, own_tokens, far_tokens, weights_of, after=()):
    frames, rows, width = own_tokens.shape
    space, groups, tm, share = weights_of.shape[:4]
    pieces = space * groups * tm

    def kernel(spots_ref, *refs):
        own_refs, far_refs = refs[:3], refs[3:6]
        token_refs, gathered_ref = refs[6:8], refs[8]
        outs = refs[9 + len(after) : 12 + len(after)]
        weights, grads, sems = refs[12 + len(after) :]

        @pl.when(pl.program_id(0) == 0)
        def _():
            for copy in run_copies(sems, weight_copies(gathered_ref, weights)):
                copy.wait()
            whole = weights[...].reshape(width, width)
            for side in range(2):
                flat = (token_refs[0][...] if side == 0 else token_refs[1][0]).reshape(frames * rows, width)
                made = dot(flat, whole, ((1,), (1,))).astype(BF16)
                grads[side] = made.reshape(frames, rows, width)

        frame = pl.program_id(0)
        for pair in range(width // PAIR):
            columns = slice(pair * PAIR, (pair + 1) * PAIR)
            operands = [
                (near[0, :, columns].astype(F32), away[0, 0, :, columns].astype(F32))
                for near, away in zip(own_refs, far_refs)
            ]
            operands.append(tuple(grads[side, frame, :, columns].astype(F32) for side in range(2)))
            for out, value in zip(outs, own_back(*operands)):
                out[0, :, columns] = value.astype(BF16)

    near = pl.BlockSpec((1, rows, width), lambda f, spots_ref: (f, 0, 0))
    away = pl.BlockSpec((1, 1, rows, width), lambda f, spots_ref: (1 - spots_ref[core_at], f, 0, 0))
    near_all = pl.BlockSpec((frames, rows, width), lambda f, spots_ref: (0, 0, 0))
    away_all = pl.BlockSpec((1, frames, rows, width), lambda f, spots_ref: (1 - spots_ref[core_at], 0, 0, 0))
    return pl.pallas_call(
        kernel,
        grid_spec=pltpu.PrefetchScalarGridSpec(
            num_scalar_prefetch=1,
            grid=(frames,),
            in_specs=[near] * 3 + [away] * 3 + [near_all, away_all] + [HBM] * (1 + len(after)),
            out_specs=[near] * 3,
            scratch_shapes=[
                pltpu.VMEM((pieces, share, width), BF16),
                pltpu.VMEM((2, frames, rows, width), BF16),
                pltpu.SemaphoreType.DMA((pieces,)),
            ],
        ),
        out_shape=[jax.ShapeDtypeStruct((frames, rows, width), BF16)] * 3,
        compiler_params=BIG,
        cost_estimate=cost_of(20),
        name="space_attention",
    )(spots, *own, *far, own_tokens, far_tokens, weights_of, *after)


def per_device(sizes, grad_out, time_q, time_k, time_v, space_q, space_k, space_v, time_wo, space_wo):
    frames, rows, width = grad_out.shape
    groups, tm, space = sizes
    patches, half = rows // tm, width // 2
    group, me, core = (lax.axis_index(name) for name in ("groups", "tm", "space"))
    share = time_wo.shape[0] // groups
    spots = jnp.concatenate([me ^ jnp.arange(tm, dtype=jnp.int32), core.reshape(1)]).astype(jnp.int32)
    core_at = tm
    order = []
    for low in range(tm // 2):
        order += [tm // 2 - 1 - low, tm - 1 - low]

    def to_partner(tensor, k):
        return lax.ppermute(tensor, "tm", [(i, i ^ k) for i in range(tm)]) if k else tensor

    def cut(tensor):
        return lax.dynamic_slice_in_dim(tensor, group * share, share, 0)

    def gathered(piece):
        whole = lax.all_gather(piece, ("space", "groups", "tm"), axis=0, tiled=True)
        return whole.reshape(space, groups, tm, share, width)

    time_weights = gathered(cut(time_wo))

    split = [t.reshape(frames, tm, patches, width) for t in (time_q, time_k, time_v, grad_out)]

    def payloads(chunk, after=()):
        def plan(at, parts, outs):
            columns = pl.ds(chunk * half, half)
            pairs = []
            for k in order:
                pairs += [(part.at[:, at[k], :, columns], outs[k].at[i]) for i, part in enumerate(parts[:3])]
                if chunk == 0:
                    for side in range(2):
                        side_columns = pl.ds(side * half, half)
                        pairs.append((parts[3].at[:, at[k], :, side_columns], outs[k].at[3 + side]))
            return pairs

        kinds = 5 if chunk == 0 else 3
        shapes = [(kinds, frames, patches, half)] * tm
        return moved(spots, split[: 4 - chunk], shapes, plan, "payloads", after)

    def exchange(tensors):
        arrived = {k: to_partner(tensors[k], k) for k in order}
        return [arrived[k] for k in range(tm)]

    first_sent = payloads(0)
    early = exchange(first_sent)

    late = exchange(payloads(1, (first_sent[0],)))

    far = [lax.all_gather(tensor, "space", axis=0) for tensor in (space_q, space_k, space_v, grad_out)]
    space_weights = gathered(cut(space_wo))

    *done, late_grad = time_chunk(early, time_weights, None, "time_first")
    back = exchange(done)
    done = time_chunk(late, None, late_grad, "time_second")
    back2 = exchange(done)

    space_out = space_attention(
        spots,
        core_at,
        (space_q, space_k, space_v),
        far[:3],
        grad_out,
        far[3],
        space_weights,
        (late_grad,),
    )

    def place(chunk):
        def plan(at, refs, outs):
            columns = pl.ds(chunk * half, half)
            return [
                (ref.at[kind], outs[kind].at[:, at[k], :, columns])
                for k, ref in enumerate(refs)
                for kind in range(3)
            ]

        return plan

    shapes = [(frames, tm, patches, width)] * 3
    outs = moved(spots, back, shapes, place(0), "place_first")
    outs = moved(spots, back2, shapes, place(1), "place_second", space_out, outs)
    time_out = [out.reshape(frames, rows, width) for out in outs]
    return (*time_out, *space_out)


def per_device_plain(sizes, grad_out, time_q, time_k, time_v, space_q, space_k, space_v, time_wo, space_wo):
    frames, rows, width = grad_out.shape
    groups, tm, space = sizes
    patches = rows // tm
    core = lax.axis_index("space")
    spots = core.reshape(1).astype(jnp.int32)

    def to_patches(tensor):
        split = tensor.reshape(tensor.shape[:-2] + (tm, patches, width))
        return jnp.moveaxis(split, -3, 0)

    def exchanged(tensor):
        return lax.all_to_all(tensor, "tm", split_axis=0, concat_axis=0, tiled=True)

    time_qkv = exchanged(to_patches(jnp.stack([time_q, time_k, time_v])))

    both_wo = jnp.concatenate([time_wo, space_wo], axis=1)
    share = both_wo.shape[0] // groups
    if share * groups == both_wo.shape[0]:
        piece = lax.dynamic_slice_in_dim(both_wo, lax.axis_index("groups") * share, share, 0)
        whole = lax.all_gather(piece, ("tm", "space", "groups"), axis=0, tiled=True)
    else:
        whole = lax.all_gather(both_wo, ("tm", "space"), axis=0, tiled=True)

    far = [lax.all_gather(tensor, "space", axis=0) for tensor in (space_q, space_k, space_v, grad_out)]
    tokens = grad_out.reshape(frames * rows, width)
    time_grad = jnp.einsum("td,cd->tc", tokens, whole[:, :width], preferred_element_type=F32)
    time_grad = exchanged(to_patches(time_grad.astype(BF16).reshape(frames, rows, width)))
    pieces = whole[:, width:].reshape(tm, space, -1, 1, width)
    pieces = jnp.moveaxis(pieces.reshape(tm, space, 1, -1, width), 0, 2)
    space_out = space_attention(spots, 0, (space_q, space_k, space_v), far[:3], grad_out, far[3], pieces)

    back = exchanged(time_attention(time_qkv, time_grad))
    time_out = [jnp.moveaxis(back[:, index], 0, 1).reshape(frames, rows, width) for index in range(3)]
    return (*time_out, *space_out)


def solution(mesh):
    tokens = P(("groups", "tm"), "space", None)
    weights = P(("tm", "space"), None)
    sizes = tuple(mesh.shape[name] for name in ("groups", "tm", "space"))
    groups, tm, space = sizes
    paired = groups == 2 and space == 2 and tm % 2 == 0 and tm & (tm - 1) == 0

    def body(*tensors):
        patches, rows = tensors[0].shape[1] // tm, tensors[-1].shape[0]
        fits = paired and patches % 8 == 0 and rows % (16 * groups) == 0
        return (per_device if fits else per_device_plain)(sizes, *tensors)

    return jax.shard_map(
        body,
        mesh=mesh,
        in_specs=(tokens,) * 7 + (weights,) * 2,
        out_specs=(tokens,) * 6,
        check_vma=False,
    )
```

```python
import functools
import math

import jax
import jax.numpy as jnp
from jax import lax
from jax.experimental import pallas as pl
from jax.experimental.pallas import tpu as pltpu
from jax.sharding import PartitionSpec as P

HEAD_DIM = 64
PAIR = 2 * HEAD_DIM
F32 = jnp.float32
BF16 = jnp.bfloat16
SCALE = 1.0 / math.sqrt(HEAD_DIM)


def dot(left, right, contract):
    return lax.dot_general(left, right, (contract, ((), ())), preferred_element_type=F32)


def pair_back(query, keys, values, out_grad):
    rows = query.shape[0]
    lane = lax.broadcasted_iota(jnp.int32, (rows, PAIR), 1)
    first = lane < HEAD_DIM

    def stacked(tensor):
        zero = jnp.zeros_like(tensor)
        both = [jnp.where(first, tensor, zero), jnp.where(first, zero, tensor)]
        return jnp.concatenate(both, axis=0).astype(BF16)

    query2 = stacked(query)
    grad2 = stacked(out_grad)
    keys = keys.astype(BF16)
    values = values.astype(BF16)
    scores = dot(keys, query2, ((1,), (1,))) * SCALE
    expo = jnp.exp(scores - jnp.max(scores, axis=0, keepdims=True))
    probs = expo * (1.0 / jnp.sum(expo, axis=0, keepdims=True))
    dprob = dot(values, grad2, ((1,), (1,)))
    delta = jnp.sum(probs * dprob, axis=0, keepdims=True)
    dscore = (probs * (dprob - delta)).astype(BF16)
    grad_values = dot(probs.astype(BF16), grad2, ((1,), (0,)))
    grad_keys = dot(dscore, query2, ((1,), (0,))) * SCALE
    both = dot(dscore, keys, ((0,), (0,))) * SCALE
    grad_query = jnp.where(first, both[:rows], both[rows:])
    return grad_query, grad_keys, grad_values


def time_kernel(qkv_ref, grad_ref, out_ref, *scratch):
    sources, frames, patches, lanes = grad_ref.shape
    total = sources * frames
    held, results = scratch[:4], scratch[4:]
    for pair in range(lanes // PAIR):
        columns = slice(pair * PAIR, (pair + 1) * PAIR)
        for index in range(4):
            part = qkv_ref[:, index, :, :, columns] if index < 3 else grad_ref[:, :, :, columns]
            held[index][pair] = part.astype(F32).reshape(total * patches, PAIR)
        for patch in range(patches):
            rows = pl.ds(patch, total, stride=patches)
            done = pair_back(*[ref[pair, rows, :] for ref in held])
            for ref, value in zip(results, done):
                ref[pair, rows, :] = value
        for index in range(3):
            value = results[index][pair].reshape(sources, frames, patches, PAIR)
            out_ref[:, index, :, :, columns] = value.astype(BF16)


def time_kernel_wide(qkv_ref, grad_ref, out_ref):
    done = pair_back(*[qkv_ref[index, 0].astype(F32) for index in range(3)], grad_ref[0].astype(F32))
    for index in range(3):
        out_ref[index, 0] = done[index].astype(BF16)


def time_attention(qkv, grad):
    sources, _, frames, patches, width = qkv.shape
    total = sources * frames
    if patches % 8 == 0:
        lanes = 2 * PAIR
        return pl.pallas_call(
            time_kernel,
            grid=(width // lanes,),
            in_specs=[
                pl.BlockSpec((sources, 3, frames, patches, lanes), lambda i: (0, 0, 0, 0, i)),
                pl.BlockSpec((sources, frames, patches, lanes), lambda i: (0, 0, 0, i)),
            ],
            out_specs=pl.BlockSpec((sources, 3, frames, patches, lanes), lambda i: (0, 0, 0, 0, i)),
            out_shape=jax.ShapeDtypeStruct(qkv.shape, BF16),
            scratch_shapes=[pltpu.VMEM((lanes // PAIR, total * patches, PAIR), F32)] * 7,
            compiler_params=pltpu.CompilerParams(vmem_limit_bytes=40 * 2**20),
            name="time_attention",
        )(qkv, grad)
    qkv = qkv.transpose(1, 3, 0, 2, 4).reshape(3, patches, total, width)
    grad = grad.transpose(2, 0, 1, 3).reshape(patches, total, width)
    done = pl.pallas_call(
        time_kernel_wide,
        grid=(patches, width // PAIR),
        in_specs=[
            pl.BlockSpec((3, 1, total, PAIR), lambda p, i: (0, p, 0, i)),
            pl.BlockSpec((1, total, PAIR), lambda p, i: (p, 0, i)),
        ],
        out_specs=pl.BlockSpec((3, 1, total, PAIR), lambda p, i: (0, p, 0, i)),
        out_shape=jax.ShapeDtypeStruct(qkv.shape, BF16),
        compiler_params=pltpu.CompilerParams(vmem_limit_bytes=40 * 2**20),
        name="time_attention_wide",
    )(qkv, grad)
    done = done.reshape(3, patches, sources, frames, width)
    return done.transpose(2, 0, 3, 1, 4)


def own_back(queries, keys, values, grads):
    rows = queries[0].shape[0]
    first = lax.broadcasted_iota(jnp.int32, (rows, PAIR), 1) < HEAD_DIM
    zero = jnp.zeros((rows, PAIR), F32)

    def stacked(parts):
        both = []
        for part in parts:
            both += [jnp.where(first, part, zero), jnp.where(first, zero, part)]
        return jnp.concatenate(both, axis=0).astype(BF16)

    query2, grad2 = stacked(queries), stacked(grads)
    keys = jnp.concatenate(keys, axis=0).astype(BF16)
    values = jnp.concatenate(values, axis=0).astype(BF16)
    scores = dot(keys, query2, ((1,), (1,))) * SCALE
    expo = jnp.exp(scores - jnp.max(scores, axis=0, keepdims=True))
    probs = expo * (1.0 / jnp.sum(expo, axis=0, keepdims=True))
    dprob = dot(values, grad2, ((1,), (1,)))
    delta = jnp.sum(probs * dprob, axis=0, keepdims=True)
    dscore = (probs * (dprob - delta)).astype(BF16)
    grad_values = dot(probs[:rows].astype(BF16), grad2, ((1,), (0,)))
    grad_keys = dot(dscore[:rows], query2, ((1,), (0,))) * SCALE
    both = dot(dscore[:, : 2 * rows], keys, ((0,), (0,))) * SCALE
    grad_query = jnp.where(first, both[:rows], both[rows:])
    return grad_query, grad_keys, grad_values


HBM = pl.BlockSpec(memory_space=pltpu.HBM)
SCALARS = pl.BlockSpec(memory_space=pltpu.SMEM)
BIG = pltpu.CompilerParams(vmem_limit_bytes=48 * 2**20)


def cost_of(microseconds):
    return pl.CostEstimate(flops=0, transcendentals=0, bytes_accessed=int(microseconds * 3_690_000))


def run_copies(sems, pairs):
    copies = [pltpu.make_async_copy(src, dst, sems.at[i]) for i, (src, dst) in enumerate(pairs)]
    for copy in copies:
        copy.start()
    return copies


def run_staged(pairs):
    count = len(pairs)

    def body(*scratch):
        stages, arrived, left = scratch[:count], scratch[count], scratch[count + 1]
        loads = run_copies(arrived, [(src, stage) for (src, _), stage in zip(pairs, stages)])
        stores = []
        for index, (load, (_, dst)) in enumerate(zip(loads, pairs)):
            load.wait()
            stores.append(pltpu.make_async_copy(stages[index], dst, left.at[index]))
            stores[-1].start()
        for store in stores:
            store.wait()

    sems = [pltpu.SemaphoreType.DMA((count,))] * 2
    pl.run_scoped(body, *[pltpu.VMEM(src.shape, BF16) for src, _ in pairs], *sems)


def moved(spots, parts, shapes, plan, name, after=(), kept=()):
    count = len(parts)

    def kernel(spots_ref, *refs):
        run_staged(plan(spots_ref, refs[:count], refs[len(refs) - len(shapes) :]))

    return pl.pallas_call(
        kernel,
        in_specs=[SCALARS] + [HBM] * (count + len(after) + len(kept)),
        out_specs=[HBM] * len(shapes),
        out_shape=[jax.ShapeDtypeStruct(shape, BF16) for shape in shapes],
        input_output_aliases={1 + count + len(after) + i: i for i in range(len(kept))},
        compiler_params=BIG,
        name=name,
    )(spots, *parts, *after, *kept)


def weight_copies(gathered_ref, weights):
    space, groups, tm = gathered_ref.shape[:3]
    return [
        (gathered_ref.at[s, g, t], weights.at[(t * space + s) * groups + g])
        for t in range(tm)
        for s in range(space)
        for g in range(groups)
    ]


def attend_pair(held, results, patches, total):
    for patch in range(patches):
        rows = pl.ds(patch, total, stride=patches)
        done = pair_back(*[ref[rows, :] for ref in held])
        for ref, value in zip(results, done):
            ref[rows, :] = value


def time_chunk(blocks, token_blocks, gathered, late_grad, name, after=()):
    blocks = [*blocks, *token_blocks]
    first = late_grad is None
    count = len(blocks) // 2 if first else len(blocks)
    _, frames, patches, lanes = blocks[0].shape
    total, part = count * frames, frames * patches
    rows, width = total * patches, 2 * lanes
    wide = [pltpu.VMEM(block.shape, BF16) for block in blocks]
    scratch = wide + [pltpu.VMEM((3, frames, patches, lanes), BF16)] * count
    scratch += [pltpu.VMEM((rows, PAIR), F32)] * 7
    if first:
        space, groups, tm, share = gathered.shape[:4]
        scratch += [pltpu.VMEM((rows, width), BF16), pltpu.VMEM((space * groups * tm, share, width), BF16)]
        operands = (gathered,)
        copied = len(blocks) + space * groups * tm
    else:
        scratch += [pltpu.VMEM((rows, lanes), BF16)]
        operands = (late_grad,)
        copied = count + 1
    scratch += [pltpu.SemaphoreType.DMA((copied,)), pltpu.SemaphoreType.DMA((count,))]

    def kernel(*refs):
        refs = list(refs)

        def take(number):
            taken, refs[:number] = refs[:number], []
            return taken

        block_refs, extra_ref, _ = take(len(blocks)), take(1)[0], take(len(after))
        out_refs = take(count)
        later_ref = take(1)[0] if first else None
        blocks_in, results_out = take(len(blocks)), take(count)
        blocks_in, tokens_in = blocks_in[:count], blocks_in[count:]
        held, results = take(4), take(3)
        grads = take(1)[0]
        weights = take(1)[0] if first else None
        arrived, left = refs
        pairs = list(zip(block_refs, [*blocks_in, *tokens_in]))
        pairs += weight_copies(extra_ref, weights) if first else [(extra_ref, grads)]
        for copy in run_copies(arrived, pairs):
            copy.wait()
        if first:
            for index, ref in enumerate(tokens_in):
                value = ref[...].astype(F32).reshape(part, width)
                grads[index * part : (index + 1) * part, :] = value.astype(BF16)

        def one_pair(pair, carry):
            columns = pl.ds(pl.multiple_of(pair * PAIR, PAIR), PAIR)
            for index, ref in enumerate(blocks_in):
                at = slice(index * part, (index + 1) * part)
                for kind in range(3):
                    held[kind][at, :] = ref[kind, :, :, columns].astype(F32).reshape(part, PAIR)
            if first:
                pieces = weights[pl.ds(pair * (PAIR // share), PAIR // share)].reshape(PAIR, width)
                held[3][...] = dot(grads[...], pieces, ((1,), (1,))).astype(BF16).astype(F32)
            else:
                held[3][...] = grads[:, columns].astype(F32)
            attend_pair(held, results, patches, total)
            for index, ref in enumerate(results_out):
                at = slice(index * part, (index + 1) * part)
                for kind in range(3):
                    value = results[kind][at, :].reshape(frames, patches, PAIR)
                    ref[kind, :, :, columns] = value.astype(BF16)
            return carry

        lax.fori_loop(0, lanes // PAIR, one_pair, 0)
        stores = run_copies(left, list(zip(results_out, out_refs)))
        if first:
            half = weights.shape[0] // 2
            later = weights[half:].reshape(lanes, width)
            later_ref[...] = dot(grads[...], later, ((1,), (1,))).astype(BF16)
        for store in stores:
            store.wait()

    out_shapes = [jax.ShapeDtypeStruct((3, frames, patches, lanes), BF16)] * count
    out_specs = [HBM] * count
    if first:
        out_shapes = out_shapes + [jax.ShapeDtypeStruct((rows, lanes), BF16)]
        out_specs = out_specs + [pl.BlockSpec(memory_space=pltpu.VMEM)]
    return pl.pallas_call(
        kernel,
        in_specs=[HBM] * (len(blocks) + 1 + len(after)),
        out_specs=out_specs,
        out_shape=out_shapes,
        scratch_shapes=scratch,
        compiler_params=BIG,
        cost_estimate=cost_of(16 if first else 10),
        name=name,
    )(*blocks, *operands, *after)


def space_attention(own, far, own_tokens, weights_of, after=()):
    frames, rows, width = own_tokens.shape
    space, groups, tm, share = weights_of.shape[:4]
    pieces = space * groups * tm

    def kernel(*refs):
        own_refs, far_ref, own_token_ref, far_token_ref, gathered_ref = refs[:3], *refs[3:7]
        outs = refs[7 + len(after) : 10 + len(after)]
        weights, grads, sems = refs[10 + len(after) :]

        @pl.when(pl.program_id(0) == 0)
        def _():
            for copy in run_copies(sems, weight_copies(gathered_ref, weights)):
                copy.wait()
            whole = weights[...].reshape(width, width)
            for side in range(2):
                flat = (far_token_ref[0] if side else own_token_ref[...]).reshape(frames * rows, width)
                made = dot(flat, whole, ((1,), (1,))).astype(BF16)
                grads[side] = made.reshape(frames, rows, width)

        frame = pl.program_id(0)
        for pair in range(width // PAIR):
            columns = slice(pair * PAIR, (pair + 1) * PAIR)
            operands = [
                (near[0, :, columns].astype(F32), far_ref[index, 0, :, columns].astype(F32))
                for index, near in enumerate(own_refs)
            ]
            operands.append(tuple(grads[side, frame, :, columns].astype(F32) for side in range(2)))
            for out, value in zip(outs, own_back(*operands)):
                out[0, :, columns] = value.astype(BF16)

    near = pl.BlockSpec((1, rows, width), lambda f: (f, 0, 0))
    near_all = pl.BlockSpec((frames, rows, width), lambda f: (0, 0, 0))
    away = pl.BlockSpec((3, 1, rows, width), lambda f: (0, f, 0, 0))
    away_all = pl.BlockSpec((1, frames, rows, width), lambda f: (3, 0, 0, 0))
    return pl.pallas_call(
        kernel,
        grid_spec=pltpu.PrefetchScalarGridSpec(
            num_scalar_prefetch=0,
            grid=(frames,),
            in_specs=[near] * 3 + [away, near_all, away_all] + [HBM] * (1 + len(after)),
            out_specs=[near] * 3,
            scratch_shapes=[
                pltpu.VMEM((pieces, share, width), BF16),
                pltpu.VMEM((2, frames, rows, width), BF16),
                pltpu.SemaphoreType.DMA((pieces,)),
            ],
        ),
        out_shape=[jax.ShapeDtypeStruct((frames, rows, width), BF16)] * 3,
        compiler_params=BIG,
        cost_estimate=cost_of(20),
        name="space_attention",
    )(*own, far, own_tokens, far, weights_of, *after)


def per_device(sizes, grad_out, time_q, time_k, time_v, space_q, space_k, space_v, time_wo, space_wo):
    frames, rows, width = grad_out.shape
    groups, tm, space = sizes
    patches, half = rows // tm, width // 2
    group, me = lax.axis_index("groups"), lax.axis_index("tm")
    share = time_wo.shape[0] // groups
    spots = jnp.concatenate([me ^ jnp.arange(tm, dtype=jnp.int32), group.reshape(1)]).astype(jnp.int32)
    order = []
    for low in range(tm // 2):
        order += [tm // 2 - 1 - low, tm - 1 - low]

    def to_partner(tensor, k):
        return lax.ppermute(tensor, "tm", [(i, i ^ k) for i in range(tm)]) if k else tensor

    def moved_one(parts, shape, plan, name, after=()):
        return moved(spots, parts, [shape], lambda at, refs, outs: plan(at, refs, outs[0]), name, after)[0]

    piece = moved_one(
        [tensor.reshape(groups, share, width) for tensor in (time_wo, space_wo)],
        (2, share, width),
        lambda at, refs, out: [(ref.at[at[tm]], out.at[i]) for i, ref in enumerate(refs)],
        "own_piece",
    )
    columns = lax.all_gather(piece, "tm", axis=0)

    def gathered(column):
        whole = lax.all_gather(column, ("space", "groups"), axis=0, tiled=True)
        return whole.reshape(space, groups, tm, share, width)

    split = [t.reshape(frames, tm, patches, width) for t in (time_q, time_k, time_v, grad_out)]

    def token_plan(at, parts, outs):
        return [(parts[0].at[:, at[k]], outs[k]) for k in order]

    def payloads(chunk, after=()):
        def plan(at, parts, outs):
            columns = pl.ds(chunk * half, half)
            return [
                (part.at[:, at[k], :, columns], outs[k].at[i]) for k in order for i, part in enumerate(parts)
            ]

        return moved(spots, split[:3], [(3, frames, patches, half)] * tm, plan, "payloads", after)

    def exchange(tensors):
        arrived = {k: to_partner(tensors[k], k) for k in order}
        return [arrived[k] for k in range(tm)]

    sent_tokens = moved(spots, split[3:], [(frames, patches, width)] * tm, token_plan, "token_payloads", (piece,))
    tokens = exchange(sent_tokens)
    first_sent = payloads(0, (sent_tokens[0],))
    early = exchange(first_sent)
    second_sent = payloads(1, (first_sent[0],))
    late = exchange(second_sent)
    both_cores = moved_one(
        [space_q, space_k, space_v, grad_out],
        (4, frames, rows, width),
        lambda at, refs, out: [(ref, out.at[i]) for i, ref in enumerate(refs)],
        "space_payload",
        (first_sent[0],),
    )
    far = lax.ppermute(both_cores, "space", [(0, 1), (1, 0)])

    time_column, space_column = moved(
        spots,
        [columns],
        [(tm * share, width)] * 2,
        lambda at, refs, outs: [
            (refs[0].at[t, i], outs[i].at[pl.ds(t * share, share)]) for i in range(2) for t in range(tm)
        ],
        "columns",
        [tokens[k] for k in order if k],
    )
    time_weights, space_weights = gathered(time_column), gathered(space_column)

    *done, late_grad = time_chunk(early, tokens, time_weights, None, "time_first", (far,))
    back = exchange(done)
    done = time_chunk(late, (), None, late_grad, "time_second")
    back2 = exchange(done)

    def place(chunk):
        def plan(at, refs, outs):
            columns = pl.ds(chunk * half, half)
            return [
                (ref.at[kind], outs[kind].at[:, at[k], :, columns])
                for k, ref in enumerate(refs)
                for kind in range(3)
            ]

        return plan

    shapes = [(frames, tm, patches, width)] * 3
    outs = moved(spots, back, shapes, place(0), "place_first")
    space_out = space_attention(
        (space_q, space_k, space_v),
        far,
        grad_out,
        space_weights,
        (outs[0],),
    )
    outs = moved(spots, back2, shapes, place(1), "place_second", space_out, outs)
    time_out = [out.reshape(frames, rows, width) for out in outs]
    return (*time_out, *space_out)


def per_device_plain(sizes, grad_out, time_q, time_k, time_v, space_q, space_k, space_v, time_wo, space_wo):
    frames, rows, width = grad_out.shape
    groups, tm, space = sizes
    patches = rows // tm

    def to_patches(tensor):
        split = tensor.reshape(tensor.shape[:-2] + (tm, patches, width))
        return jnp.moveaxis(split, -3, 0)

    def exchanged(tensor):
        return lax.all_to_all(tensor, "tm", split_axis=0, concat_axis=0, tiled=True)

    time_qkv = exchanged(to_patches(jnp.stack([time_q, time_k, time_v])))

    both_wo = jnp.concatenate([time_wo, space_wo], axis=1)
    share = both_wo.shape[0] // groups
    if share * groups == both_wo.shape[0]:
        piece = lax.dynamic_slice_in_dim(both_wo, lax.axis_index("groups") * share, share, 0)
        whole = lax.all_gather(piece, ("tm", "space", "groups"), axis=0, tiled=True)
    else:
        whole = lax.all_gather(both_wo, ("tm", "space"), axis=0, tiled=True)

    swap = [(0, 1), (1, 0)]
    far = lax.ppermute(jnp.stack([space_q, space_k, space_v, grad_out]), "space", swap)
    tokens = grad_out.reshape(frames * rows, width)
    time_grad = jnp.einsum("td,cd->tc", tokens, whole[:, :width], preferred_element_type=F32)
    time_grad = exchanged(to_patches(time_grad.astype(BF16).reshape(frames, rows, width)))
    pieces = whole[:, width:].reshape(tm, space, -1, 1, width)
    pieces = jnp.moveaxis(pieces.reshape(tm, space, 1, -1, width), 0, 2)
    space_out = space_attention((space_q, space_k, space_v), far, grad_out, pieces)

    back = exchanged(time_attention(time_qkv, time_grad))
    time_out = [jnp.moveaxis(back[:, index], 0, 1).reshape(frames, rows, width) for index in range(3)]
    return (*time_out, *space_out)


def solution(mesh):
    tokens = P(("groups", "tm"), "space", None)
    weights = P(("tm", "space"), None)
    sizes = tuple(mesh.shape[name] for name in ("groups", "tm", "space"))
    groups, tm, space = sizes
    paired = groups == 2 and space == 2 and tm % 2 == 0 and tm & (tm - 1) == 0

    def body(*tensors):
        patches, rows = tensors[0].shape[1] // tm, tensors[-1].shape[0]
        fits = paired and patches % 8 == 0 and rows % (16 * groups) == 0
        return (per_device if fits else per_device_plain)(sizes, *tensors)

    return jax.shard_map(
        body,
        mesh=mesh,
        in_specs=(tokens,) * 7 + (weights,) * 2,
        out_specs=(tokens,) * 6,
        check_vma=False,
    )
```

```python
import functools
import math

import jax
import jax.numpy as jnp
from jax import lax
from jax.experimental import pallas as pl
from jax.experimental.pallas import tpu as pltpu
from jax.sharding import PartitionSpec as P

HEAD_DIM = 64
PAIR = 2 * HEAD_DIM
F32 = jnp.float32
BF16 = jnp.bfloat16
SCALE = 1.0 / math.sqrt(HEAD_DIM)


def dot(left, right, contract):
    return lax.dot_general(left, right, (contract, ((), ())), preferred_element_type=F32)


def pair_back(query, keys, values, out_grad):
    rows = query.shape[0]
    lane = lax.broadcasted_iota(jnp.int32, (rows, PAIR), 1)
    first = lane < HEAD_DIM

    def stacked(tensor):
        zero = jnp.zeros_like(tensor)
        both = [jnp.where(first, tensor, zero), jnp.where(first, zero, tensor)]
        return jnp.concatenate(both, axis=0).astype(BF16)

    query2 = stacked(query)
    grad2 = stacked(out_grad)
    keys = keys.astype(BF16)
    values = values.astype(BF16)
    scores = dot(keys, query2, ((1,), (1,))) * SCALE
    expo = jnp.exp(scores - jnp.max(scores, axis=0, keepdims=True))
    probs = expo * (1.0 / jnp.sum(expo, axis=0, keepdims=True))
    dprob = dot(values, grad2, ((1,), (1,)))
    delta = jnp.sum(probs * dprob, axis=0, keepdims=True)
    dscore = (probs * (dprob - delta)).astype(BF16)
    grad_values = dot(probs.astype(BF16), grad2, ((1,), (0,)))
    grad_keys = dot(dscore, query2, ((1,), (0,))) * SCALE
    both = dot(dscore, keys, ((0,), (0,))) * SCALE
    grad_query = jnp.where(first, both[:rows], both[rows:])
    return grad_query, grad_keys, grad_values


def time_kernel(qkv_ref, grad_ref, out_ref, *scratch):
    sources, frames, patches, lanes = grad_ref.shape
    total = sources * frames
    held, results = scratch[:4], scratch[4:]
    for pair in range(lanes // PAIR):
        columns = slice(pair * PAIR, (pair + 1) * PAIR)
        for index in range(4):
            part = qkv_ref[:, index, :, :, columns] if index < 3 else grad_ref[:, :, :, columns]
            held[index][pair] = part.astype(F32).reshape(total * patches, PAIR)
        for patch in range(patches):
            rows = pl.ds(patch, total, stride=patches)
            done = pair_back(*[ref[pair, rows, :] for ref in held])
            for ref, value in zip(results, done):
                ref[pair, rows, :] = value
        for index in range(3):
            value = results[index][pair].reshape(sources, frames, patches, PAIR)
            out_ref[:, index, :, :, columns] = value.astype(BF16)


def time_kernel_wide(qkv_ref, grad_ref, out_ref):
    done = pair_back(*[qkv_ref[index, 0].astype(F32) for index in range(3)], grad_ref[0].astype(F32))
    for index in range(3):
        out_ref[index, 0] = done[index].astype(BF16)


def time_attention(qkv, grad):
    sources, _, frames, patches, width = qkv.shape
    total = sources * frames
    if patches % 8 == 0:
        lanes = 2 * PAIR
        return pl.pallas_call(
            time_kernel,
            grid=(width // lanes,),
            in_specs=[
                pl.BlockSpec((sources, 3, frames, patches, lanes), lambda i: (0, 0, 0, 0, i)),
                pl.BlockSpec((sources, frames, patches, lanes), lambda i: (0, 0, 0, i)),
            ],
            out_specs=pl.BlockSpec((sources, 3, frames, patches, lanes), lambda i: (0, 0, 0, 0, i)),
            out_shape=jax.ShapeDtypeStruct(qkv.shape, BF16),
            scratch_shapes=[pltpu.VMEM((lanes // PAIR, total * patches, PAIR), F32)] * 7,
            compiler_params=pltpu.CompilerParams(vmem_limit_bytes=40 * 2**20),
            name="time_attention",
        )(qkv, grad)
    qkv = qkv.transpose(1, 3, 0, 2, 4).reshape(3, patches, total, width)
    grad = grad.transpose(2, 0, 1, 3).reshape(patches, total, width)
    done = pl.pallas_call(
        time_kernel_wide,
        grid=(patches, width // PAIR),
        in_specs=[
            pl.BlockSpec((3, 1, total, PAIR), lambda p, i: (0, p, 0, i)),
            pl.BlockSpec((1, total, PAIR), lambda p, i: (p, 0, i)),
        ],
        out_specs=pl.BlockSpec((3, 1, total, PAIR), lambda p, i: (0, p, 0, i)),
        out_shape=jax.ShapeDtypeStruct(qkv.shape, BF16),
        compiler_params=pltpu.CompilerParams(vmem_limit_bytes=40 * 2**20),
        name="time_attention_wide",
    )(qkv, grad)
    done = done.reshape(3, patches, sources, frames, width)
    return done.transpose(2, 0, 3, 1, 4)


def own_back(queries, keys, values, grads):
    rows = queries[0].shape[0]
    first = lax.broadcasted_iota(jnp.int32, (rows, PAIR), 1) < HEAD_DIM
    zero = jnp.zeros((rows, PAIR), F32)

    def stacked(parts):
        both = []
        for part in parts:
            both += [jnp.where(first, part, zero), jnp.where(first, zero, part)]
        return jnp.concatenate(both, axis=0).astype(BF16)

    query2, grad2 = stacked(queries), stacked(grads)
    keys = jnp.concatenate(keys, axis=0).astype(BF16)
    values = jnp.concatenate(values, axis=0).astype(BF16)
    scores = dot(keys, query2, ((1,), (1,))) * SCALE
    expo = jnp.exp(scores - jnp.max(scores, axis=0, keepdims=True))
    probs = expo * (1.0 / jnp.sum(expo, axis=0, keepdims=True))
    dprob = dot(values, grad2, ((1,), (1,)))
    delta = jnp.sum(probs * dprob, axis=0, keepdims=True)
    dscore = (probs * (dprob - delta)).astype(BF16)
    grad_values = dot(probs[:rows].astype(BF16), grad2, ((1,), (0,)))
    grad_keys = dot(dscore[:rows], query2, ((1,), (0,))) * SCALE
    both = dot(dscore[:, : 2 * rows], keys, ((0,), (0,))) * SCALE
    grad_query = jnp.where(first, both[:rows], both[rows:])
    return grad_query, grad_keys, grad_values


HBM = pl.BlockSpec(memory_space=pltpu.HBM)
SCALARS = pl.BlockSpec(memory_space=pltpu.SMEM)
BIG = pltpu.CompilerParams(vmem_limit_bytes=24 * 2**20)


def cost_of(microseconds):
    return pl.CostEstimate(flops=0, transcendentals=0, bytes_accessed=int(microseconds * 3_690_000))


def run_copies(sems, pairs):
    copies = [pltpu.make_async_copy(src, dst, sems.at[i]) for i, (src, dst) in enumerate(pairs)]
    for copy in copies:
        copy.start()
    return copies


def run_staged(pairs):
    count = len(pairs)

    def body(*scratch):
        stages, arrived, left = scratch[:count], scratch[count], scratch[count + 1]
        loads = run_copies(arrived, [(src, stage) for (src, _), stage in zip(pairs, stages)])
        stores = []
        for index, (load, (_, dst)) in enumerate(zip(loads, pairs)):
            load.wait()
            stores.append(pltpu.make_async_copy(stages[index], dst, left.at[index]))
            stores[-1].start()
        for store in stores:
            store.wait()

    sems = [pltpu.SemaphoreType.DMA((count,))] * 2
    pl.run_scoped(body, *[pltpu.VMEM(src.shape, BF16) for src, _ in pairs], *sems)


def moved(spots, parts, shapes, plan, name, after=(), kept=()):
    count = len(parts)

    def kernel(spots_ref, *refs):
        run_staged(plan(spots_ref, refs[:count], refs[len(refs) - len(shapes) :]))

    return pl.pallas_call(
        kernel,
        in_specs=[SCALARS] + [HBM] * (count + len(after) + len(kept)),
        out_specs=[HBM] * len(shapes),
        out_shape=[jax.ShapeDtypeStruct(shape, BF16) for shape in shapes],
        input_output_aliases={1 + count + len(after) + i: i for i in range(len(kept))},
        compiler_params=pltpu.CompilerParams(vmem_limit_bytes=2 * sum(math.prod(x) for x in shapes) + 2 * 2**20),
        name=name,
    )(spots, *parts, *after, *kept)


def weight_copies(gathered_ref, weights):
    space, groups, tm = gathered_ref.shape[:3]
    return [
        (gathered_ref.at[s, g, t], weights.at[(t * space + s) * groups + g])
        for t in range(tm)
        for s in range(space)
        for g in range(groups)
    ]


def attend_pair(held, results, patches, total):
    for patch in range(patches):
        rows = pl.ds(patch, total, stride=patches)
        done = pair_back(*[ref[rows, :] for ref in held])
        for ref, value in zip(results, done):
            ref[rows, :] = value


def time_chunk(frames, blocks, token_blocks, gathered, late_grad, name, after=()):
    blocks = [*blocks, *token_blocks]
    first = late_grad is None
    count = len(blocks) // 2 if first else len(blocks)
    patches, lanes = blocks[0].shape[1:]
    total, part = count * frames, frames * patches
    rows, width = total * patches, 2 * lanes
    wide = [pltpu.VMEM(block.shape, BF16) for block in blocks]
    scratch = wide + [pltpu.VMEM((3 * frames, patches, lanes), BF16)] * count
    scratch += [pltpu.VMEM((rows, PAIR), F32)] * 7
    if first:
        space, groups, tm, share = gathered.shape[:4]
        scratch += [pltpu.VMEM((rows, width), BF16), pltpu.VMEM((space * groups * tm, share, width), BF16)]
        operands = (gathered,)
        copied = len(blocks) + space * groups * tm
    else:
        scratch += [pltpu.VMEM((rows, lanes), BF16)]
        operands = (late_grad,)
        copied = count + 1
    scratch += [pltpu.SemaphoreType.DMA((copied,)), pltpu.SemaphoreType.DMA((count,))]

    def kernel(*refs):
        refs = list(refs)

        def take(number):
            taken, refs[:number] = refs[:number], []
            return taken

        block_refs, extra_ref, _ = take(len(blocks)), take(1)[0], take(len(after))
        out_refs = take(count)
        later_ref = take(1)[0] if first else None
        blocks_in, results_out = take(len(blocks)), take(count)
        blocks_in, tokens_in = blocks_in[:count], blocks_in[count:]
        held, results = take(4), take(3)
        grads = take(1)[0]
        weights = take(1)[0] if first else None
        arrived, left = refs
        pairs = list(zip(block_refs, [*blocks_in, *tokens_in]))
        pairs += weight_copies(extra_ref, weights) if first else [(extra_ref, grads)]
        for copy in run_copies(arrived, pairs):
            copy.wait()
        if first:
            for index, ref in enumerate(tokens_in):
                value = ref[:frames].astype(F32).reshape(part, width)
                grads[index * part : (index + 1) * part, :] = value.astype(BF16)

        def one_pair(pair, carry):
            columns = pl.ds(pl.multiple_of(pair * PAIR, PAIR), PAIR)
            for index, ref in enumerate(blocks_in):
                at = slice(index * part, (index + 1) * part)
                for kind in range(3):
                    value = ref[kind * frames : (kind + 1) * frames, :, columns]
                    held[kind][at, :] = value.astype(F32).reshape(part, PAIR)
            if first:
                pieces = weights[pl.ds(pair * (PAIR // share), PAIR // share)].reshape(PAIR, width)
                held[3][...] = dot(grads[...], pieces, ((1,), (1,))).astype(BF16).astype(F32)
            else:
                held[3][...] = grads[:, columns].astype(F32)
            attend_pair(held, results, patches, total)
            for index, ref in enumerate(results_out):
                at = slice(index * part, (index + 1) * part)
                for kind in range(3):
                    value = results[kind][at, :].reshape(frames, patches, PAIR)
                    ref[kind * frames : (kind + 1) * frames, :, columns] = value.astype(BF16)
            return carry

        lax.fori_loop(0, lanes // PAIR, one_pair, 0)
        stores = run_copies(left, list(zip(results_out, out_refs)))
        if first:
            half = weights.shape[0] // 2
            later = weights[half:].reshape(lanes, width)
            later_ref[...] = dot(grads[...], later, ((1,), (1,))).astype(BF16)
        for store in stores:
            store.wait()

    out_shapes = [jax.ShapeDtypeStruct((3 * frames, patches, lanes), BF16)] * count
    out_specs = [HBM] * count
    if first:
        out_shapes = out_shapes + [jax.ShapeDtypeStruct((rows, lanes), BF16)]
        out_specs = out_specs + [pl.BlockSpec(memory_space=pltpu.VMEM)]
    return pl.pallas_call(
        kernel,
        in_specs=[HBM] * (len(blocks) + 1 + len(after)),
        out_specs=out_specs,
        out_shape=out_shapes,
        scratch_shapes=scratch,
        compiler_params=BIG,
        cost_estimate=cost_of(16 if first else 10),
        name=name,
    )(*blocks, *operands, *after)


def space_attention(own, far, own_tokens, weights_of, after=()):
    frames, rows, width = own_tokens.shape
    space, groups, tm, share = weights_of.shape[:4]
    pieces = space * groups * tm

    def kernel(*refs):
        own_refs, far_ref, own_token_ref, far_token_ref, gathered_ref = refs[:3], *refs[3:7]
        outs = refs[7 + len(after) : 10 + len(after)]
        weights, grads, sems = refs[10 + len(after) :]

        @pl.when(pl.program_id(0) == 0)
        def _():
            for copy in run_copies(sems, weight_copies(gathered_ref, weights)):
                copy.wait()
            whole = weights[...].reshape(width, width)
            for side in range(2):
                flat = (far_token_ref[0] if side else own_token_ref[...]).reshape(frames * rows, width)
                made = dot(flat, whole, ((1,), (1,))).astype(BF16)
                grads[side] = made.reshape(frames, rows, width)

        frame = pl.program_id(0)
        for pair in range(width // PAIR):
            columns = slice(pair * PAIR, (pair + 1) * PAIR)
            operands = [
                (near[0, :, columns].astype(F32), far_ref[index, 0, :, columns].astype(F32))
                for index, near in enumerate(own_refs)
            ]
            operands.append(tuple(grads[side, frame, :, columns].astype(F32) for side in range(2)))
            for out, value in zip(outs, own_back(*operands)):
                out[0, :, columns] = value.astype(BF16)

    near = pl.BlockSpec((1, rows, width), lambda f: (f, 0, 0))
    near_all = pl.BlockSpec((frames, rows, width), lambda f: (0, 0, 0))
    away = pl.BlockSpec((3, 1, rows, width), lambda f: (0, f, 0, 0))
    away_all = pl.BlockSpec((1, frames, rows, width), lambda f: (3, 0, 0, 0))
    return pl.pallas_call(
        kernel,
        grid_spec=pltpu.PrefetchScalarGridSpec(
            num_scalar_prefetch=0,
            grid=(frames,),
            in_specs=[near] * 3 + [away, near_all, away_all] + [HBM] * (1 + len(after)),
            out_specs=[near] * 3,
            scratch_shapes=[
                pltpu.VMEM((pieces, share, width), BF16),
                pltpu.VMEM((2, frames, rows, width), BF16),
                pltpu.SemaphoreType.DMA((pieces,)),
            ],
        ),
        out_shape=[jax.ShapeDtypeStruct((frames, rows, width), BF16)] * 3,
        compiler_params=BIG,
        cost_estimate=cost_of(20),
        name="space_attention",
    )(*own, far, own_tokens, far, weights_of, *after)


def per_device(sizes, grad_out, time_q, time_k, time_v, space_q, space_k, space_v, time_wo, space_wo):
    frames, rows, width = grad_out.shape
    groups, tm, space = sizes
    patches, half = rows // tm, width // 2
    group, me = lax.axis_index("groups"), lax.axis_index("tm")
    share = time_wo.shape[0] // groups
    spots = jnp.concatenate([me ^ jnp.arange(tm, dtype=jnp.int32), group.reshape(1)]).astype(jnp.int32)
    order = []
    for low in range(tm // 2):
        order += [tm // 2 - 1 - low, tm - 1 - low]

    def to_partner(tensor, k):
        return lax.ppermute(tensor, "tm", [(i, i ^ k) for i in range(tm)]) if k else tensor

    def moved_one(parts, shape, plan, name, after=()):
        return moved(spots, parts, [shape], lambda at, refs, outs: plan(at, refs, outs[0]), name, after)[0]

    split = [t.reshape(frames, tm, patches, width) for t in (time_q, time_k, time_v, grad_out)]
    blocks = share // patches
    time_pieces, space_pieces = (t.reshape(groups, blocks, patches, width) for t in (time_wo, space_wo))

    def token_plan(at, parts, outs):
        pairs = []
        for k in order:
            pairs.append((parts[0].at[:, at[k]], outs[k].at[pl.ds(0, frames)]))
            pairs.append((parts[1].at[at[tm]], outs[k].at[pl.ds(frames, blocks)]))
        return pairs

    def payloads(chunk, more=(), after=()):
        def plan(at, parts, outs):
            columns = pl.ds(chunk * half, half)
            pairs = []
            for k in order:
                for i in range(3):
                    pairs.append((parts[i].at[:, at[k], :, columns], outs[k].at[pl.ds(i * frames, frames)]))
                for part in parts[3:]:
                    for side in range(2):
                        kept = outs[k].at[pl.ds(3 * frames + side * blocks, blocks)]
                        pairs.append((part.at[at[tm], :, :, pl.ds(side * half, half)], kept))
            return pairs

        shape = (3 * frames + 2 * blocks * len(more), patches, half)
        return moved(spots, [*split[:3], *more], [shape] * tm, plan, "payloads", after)

    def exchange(tensors):
        arrived = {k: to_partner(tensors[k], k) for k in order}
        return [arrived[k] for k in range(tm)]

    sent_tokens = moved(
        spots, [split[3], time_pieces], [(frames + blocks, patches, width)] * tm, token_plan, "token_payloads"
    )
    tokens = exchange(sent_tokens)
    first_sent = payloads(0, (space_pieces,), (sent_tokens[0],))
    early = exchange(first_sent)
    second_sent = payloads(1, (), (first_sent[0],))
    late = exchange(second_sent)

    both_cores = moved_one(
        [space_q, space_k, space_v, grad_out],
        (4, frames, rows, width),
        lambda at, refs, out: [(ref, out.at[i]) for i, ref in enumerate(refs)],
        "space_payload",
        (first_sent[0],),
    )
    far = lax.ppermute(both_cores, "space", [(0, 1), (1, 0)])

    def gathered(column):
        whole = lax.all_gather(column, ("space", "groups"), axis=0, tiled=True)
        return whole.reshape(space, groups, tm, share, width)

    time_weights = gathered(
        moved_one(
            tokens,
            (tm, blocks, patches, width),
            lambda at, refs, out: [
                (ref.at[pl.ds(frames, blocks)], out.at[at[k]]) for k, ref in enumerate(refs)
            ],
            "time_column",
            (first_sent[0], both_cores),
        )
    )
    space_weights = gathered(
        moved_one(
            early,
            (tm, blocks, patches, width),
            lambda at, refs, out: [
                (
                    ref.at[pl.ds(3 * frames + side * blocks, blocks)],
                    out.at[at[k], :, :, pl.ds(side * half, half)],
                )
                for k, ref in enumerate(refs)
                for side in range(2)
            ],
            "space_column",
            (second_sent[0],),
        )
    )

    *done, late_grad = time_chunk(frames, early, tokens, time_weights, None, "time_first", (far,))
    back = exchange(done)
    done = time_chunk(frames, late, (), None, late_grad, "time_second")
    back2 = exchange(done)

    def place(chunk):
        def plan(at, refs, outs):
            columns = pl.ds(chunk * half, half)
            return [
                (ref.at[pl.ds(kind * frames, frames)], outs[kind].at[:, at[k], :, columns])
                for k, ref in enumerate(refs)
                for kind in range(3)
            ]

        return plan

    shapes = [(frames, tm, patches, width)] * 3
    outs = moved(spots, back, shapes, place(0), "place_first")
    space_out = space_attention(
        (space_q, space_k, space_v),
        far,
        grad_out,
        space_weights,
        (outs[0],),
    )
    outs = moved(spots, back2, shapes, place(1), "place_second", space_out, outs)
    time_out = [out.reshape(frames, rows, width) for out in outs]
    return (*time_out, *space_out)


def per_device_plain(sizes, grad_out, time_q, time_k, time_v, space_q, space_k, space_v, time_wo, space_wo):
    frames, rows, width = grad_out.shape
    groups, tm, space = sizes
    patches = rows // tm

    def to_patches(tensor):
        split = tensor.reshape(tensor.shape[:-2] + (tm, patches, width))
        return jnp.moveaxis(split, -3, 0)

    def exchanged(tensor):
        return lax.all_to_all(tensor, "tm", split_axis=0, concat_axis=0, tiled=True)

    time_qkv = exchanged(to_patches(jnp.stack([time_q, time_k, time_v])))

    both_wo = jnp.concatenate([time_wo, space_wo], axis=1)
    share = both_wo.shape[0] // groups
    if share * groups == both_wo.shape[0]:
        piece = lax.dynamic_slice_in_dim(both_wo, lax.axis_index("groups") * share, share, 0)
        whole = lax.all_gather(piece, ("tm", "space", "groups"), axis=0, tiled=True)
    else:
        whole = lax.all_gather(both_wo, ("tm", "space"), axis=0, tiled=True)

    swap = [(0, 1), (1, 0)]
    far = lax.ppermute(jnp.stack([space_q, space_k, space_v, grad_out]), "space", swap)
    tokens = grad_out.reshape(frames * rows, width)
    time_grad = jnp.einsum("td,cd->tc", tokens, whole[:, :width], preferred_element_type=F32)
    time_grad = exchanged(to_patches(time_grad.astype(BF16).reshape(frames, rows, width)))
    pieces = whole[:, width:].reshape(tm, space, -1, 1, width)
    pieces = jnp.moveaxis(pieces.reshape(tm, space, 1, -1, width), 0, 2)
    space_out = space_attention((space_q, space_k, space_v), far, grad_out, pieces)

    back = exchanged(time_attention(time_qkv, time_grad))
    time_out = [jnp.moveaxis(back[:, index], 0, 1).reshape(frames, rows, width) for index in range(3)]
    return (*time_out, *space_out)


def solution(mesh):
    tokens = P(("groups", "tm"), "space", None)
    weights = P(("tm", "space"), None)
    sizes = tuple(mesh.shape[name] for name in ("groups", "tm", "space"))
    groups, tm, space = sizes
    paired = groups == 2 and space == 2 and tm % 2 == 0 and tm & (tm - 1) == 0

    def body(*tensors):
        patches, rows = tensors[0].shape[1] // tm, tensors[-1].shape[0]
        fits = paired and patches % 8 == 0 and rows % (16 * groups) == 0 and rows % (groups * patches) == 0
        return (per_device if fits else per_device_plain)(sizes, *tensors)

    return jax.shard_map(
        body,
        mesh=mesh,
        in_specs=(tokens,) * 7 + (weights,) * 2,
        out_specs=(tokens,) * 6,
        check_vma=False,
    )
```

```python
import functools
import math

import jax
import jax.numpy as jnp
from jax import lax
from jax.experimental import pallas as pl
from jax.experimental.pallas import tpu as pltpu
from jax.sharding import PartitionSpec as P

HEAD_DIM = 64
PAIR = 2 * HEAD_DIM
F32 = jnp.float32
BF16 = jnp.bfloat16
SCALE = 1.0 / math.sqrt(HEAD_DIM)


def dot(left, right, contract):
    return lax.dot_general(left, right, (contract, ((), ())), preferred_element_type=F32)


def pair_back(query, keys, values, out_grad):
    rows = query.shape[0]
    lane = lax.broadcasted_iota(jnp.int32, (rows, PAIR), 1)
    first = lane < HEAD_DIM

    def stacked(tensor):
        zero = jnp.zeros_like(tensor)
        both = [jnp.where(first, tensor, zero), jnp.where(first, zero, tensor)]
        return jnp.concatenate(both, axis=0).astype(BF16)

    query2 = stacked(query)
    grad2 = stacked(out_grad)
    keys = keys.astype(BF16)
    values = values.astype(BF16)
    scores = dot(keys, query2, ((1,), (1,))) * SCALE
    expo = jnp.exp(scores - jnp.max(scores, axis=0, keepdims=True))
    probs = expo * (1.0 / jnp.sum(expo, axis=0, keepdims=True))
    dprob = dot(values, grad2, ((1,), (1,)))
    delta = jnp.sum(probs * dprob, axis=0, keepdims=True)
    dscore = (probs * (dprob - delta)).astype(BF16)
    grad_values = dot(probs.astype(BF16), grad2, ((1,), (0,)))
    grad_keys = dot(dscore, query2, ((1,), (0,))) * SCALE
    both = dot(dscore, keys, ((0,), (0,))) * SCALE
    grad_query = jnp.where(first, both[:rows], both[rows:])
    return grad_query, grad_keys, grad_values


def time_kernel(qkv_ref, grad_ref, out_ref, *scratch):
    sources, frames, patches, lanes = grad_ref.shape
    total = sources * frames
    held, results = scratch[:4], scratch[4:]
    for pair in range(lanes // PAIR):
        columns = slice(pair * PAIR, (pair + 1) * PAIR)
        for index in range(4):
            part = qkv_ref[:, index, :, :, columns] if index < 3 else grad_ref[:, :, :, columns]
            held[index][pair] = part.astype(F32).reshape(total * patches, PAIR)
        for patch in range(patches):
            rows = pl.ds(patch, total, stride=patches)
            done = pair_back(*[ref[pair, rows, :] for ref in held])
            for ref, value in zip(results, done):
                ref[pair, rows, :] = value
        for index in range(3):
            value = results[index][pair].reshape(sources, frames, patches, PAIR)
            out_ref[:, index, :, :, columns] = value.astype(BF16)


def time_kernel_wide(qkv_ref, grad_ref, out_ref):
    done = pair_back(*[qkv_ref[index, 0].astype(F32) for index in range(3)], grad_ref[0].astype(F32))
    for index in range(3):
        out_ref[index, 0] = done[index].astype(BF16)


def time_attention(qkv, grad):
    sources, _, frames, patches, width = qkv.shape
    total = sources * frames
    if patches % 8 == 0:
        lanes = 2 * PAIR
        return pl.pallas_call(
            time_kernel,
            grid=(width // lanes,),
            in_specs=[
                pl.BlockSpec((sources, 3, frames, patches, lanes), lambda i: (0, 0, 0, 0, i)),
                pl.BlockSpec((sources, frames, patches, lanes), lambda i: (0, 0, 0, i)),
            ],
            out_specs=pl.BlockSpec((sources, 3, frames, patches, lanes), lambda i: (0, 0, 0, 0, i)),
            out_shape=jax.ShapeDtypeStruct(qkv.shape, BF16),
            scratch_shapes=[pltpu.VMEM((lanes // PAIR, total * patches, PAIR), F32)] * 7,
            compiler_params=pltpu.CompilerParams(vmem_limit_bytes=40 * 2**20),
            name="time_attention",
        )(qkv, grad)
    qkv = qkv.transpose(1, 3, 0, 2, 4).reshape(3, patches, total, width)
    grad = grad.transpose(2, 0, 1, 3).reshape(patches, total, width)
    done = pl.pallas_call(
        time_kernel_wide,
        grid=(patches, width // PAIR),
        in_specs=[
            pl.BlockSpec((3, 1, total, PAIR), lambda p, i: (0, p, 0, i)),
            pl.BlockSpec((1, total, PAIR), lambda p, i: (p, 0, i)),
        ],
        out_specs=pl.BlockSpec((3, 1, total, PAIR), lambda p, i: (0, p, 0, i)),
        out_shape=jax.ShapeDtypeStruct(qkv.shape, BF16),
        compiler_params=pltpu.CompilerParams(vmem_limit_bytes=40 * 2**20),
        name="time_attention_wide",
    )(qkv, grad)
    done = done.reshape(3, patches, sources, frames, width)
    return done.transpose(2, 0, 3, 1, 4)


def own_back(queries, keys, values, grads):
    rows = queries[0].shape[0]
    first = lax.broadcasted_iota(jnp.int32, (rows, PAIR), 1) < HEAD_DIM
    zero = jnp.zeros((rows, PAIR), F32)

    def stacked(parts):
        both = []
        for part in parts:
            both += [jnp.where(first, part, zero), jnp.where(first, zero, part)]
        return jnp.concatenate(both, axis=0).astype(BF16)

    query2, grad2 = stacked(queries), stacked(grads)
    keys = jnp.concatenate(keys, axis=0).astype(BF16)
    values = jnp.concatenate(values, axis=0).astype(BF16)
    scores = dot(keys, query2, ((1,), (1,))) * SCALE
    expo = jnp.exp(scores - jnp.max(scores, axis=0, keepdims=True))
    probs = expo * (1.0 / jnp.sum(expo, axis=0, keepdims=True))
    dprob = dot(values, grad2, ((1,), (1,)))
    delta = jnp.sum(probs * dprob, axis=0, keepdims=True)
    dscore = (probs * (dprob - delta)).astype(BF16)
    grad_values = dot(probs[:rows].astype(BF16), grad2, ((1,), (0,)))
    grad_keys = dot(dscore[:rows], query2, ((1,), (0,))) * SCALE
    both = dot(dscore[:, : 2 * rows], keys, ((0,), (0,))) * SCALE
    grad_query = jnp.where(first, both[:rows], both[rows:])
    return grad_query, grad_keys, grad_values


ANYWHERE = pl.BlockSpec(memory_space=pl.ANY)
SCALARS = pl.BlockSpec(memory_space=pltpu.SMEM)
BIG = pltpu.CompilerParams(vmem_limit_bytes=24 * 2**20)


def settled(tensors):
    return [
        tensor
        if jax.typeof(tensor).memory_space == pltpu.VMEM
        else pltpu.with_memory_space_constraint(tensor, pltpu.HBM)
        for tensor in tensors
    ]


def cost_of(microseconds):
    return pl.CostEstimate(flops=0, transcendentals=0, bytes_accessed=int(microseconds * 3_690_000))


def run_copies(sems, pairs):
    copies = [pltpu.make_async_copy(src, dst, sems.at[i]) for i, (src, dst) in enumerate(pairs)]
    for copy in copies:
        copy.start()
    return copies


def moved(spots, parts, shapes, plan, name, after=(), kept=(), space=pltpu.VMEM):
    count = len(parts)

    def kernel(spots_ref, *refs):
        pairs = plan(spots_ref, refs[:count], refs[len(refs) - len(shapes) :])

        def body(sems):
            for copy in run_copies(sems, pairs):
                copy.wait()

        pl.run_scoped(body, pltpu.SemaphoreType.DMA((len(pairs),)))

    return pl.pallas_call(
        kernel,
        in_specs=[SCALARS] + [ANYWHERE] * (count + len(after) + len(kept)),
        out_specs=[ANYWHERE] * len(shapes),
        out_shape=[space(shape, BF16) for shape in shapes],
        input_output_aliases={1 + count + len(after) + i: i for i in range(len(kept))},
        compiler_params=pltpu.CompilerParams(vmem_limit_bytes=4 * 2**20),
        name=name,
    )(spots, *settled(parts), *after, *settled(kept))


def weight_copies(gathered_ref, weights):
    space, groups, tm = gathered_ref.shape[:3]
    return [
        (gathered_ref.at[s, g, t], weights.at[(t * space + s) * groups + g])
        for t in range(tm)
        for s in range(space)
        for g in range(groups)
    ]


def attend_pair(held, results, patches, total):
    for patch in range(patches):
        rows = pl.ds(patch, total, stride=patches)
        done = pair_back(*[ref[rows, :] for ref in held])
        for ref, value in zip(results, done):
            ref[rows, :] = value


def time_chunk(frames, blocks, token_blocks, gathered, late_grad, name, after=()):
    blocks = [*blocks, *token_blocks]
    first = late_grad is None
    count = len(blocks) // 2 if first else len(blocks)
    patches, lanes = blocks[0].shape[1:]
    total, part = count * frames, frames * patches
    rows, width = total * patches, 2 * lanes
    wide = [pltpu.VMEM(block.shape, BF16) for block in blocks]
    scratch = wide + [pltpu.VMEM((3 * frames, patches, lanes), BF16)] * count
    scratch += [pltpu.VMEM((rows, PAIR), F32)] * 7
    if first:
        space, groups, tm, share = gathered.shape[:4]
        scratch += [pltpu.VMEM((rows, width), BF16), pltpu.VMEM((space * groups * tm, share, width), BF16)]
        operands = settled((gathered,))
        copied = len(blocks) + space * groups * tm
    else:
        scratch += [pltpu.VMEM((rows, lanes), BF16)]
        operands = (late_grad,)
        copied = count + 1
    scratch += [pltpu.SemaphoreType.DMA((copied,)), pltpu.SemaphoreType.DMA((count,))]

    def kernel(*refs):
        refs = list(refs)

        def take(number):
            taken, refs[:number] = refs[:number], []
            return taken

        block_refs, extra_ref, _ = take(len(blocks)), take(1)[0], take(len(after))
        out_refs = take(count)
        later_ref = take(1)[0] if first else None
        blocks_in, results_out = take(len(blocks)), take(count)
        blocks_in, tokens_in = blocks_in[:count], blocks_in[count:]
        held, results = take(4), take(3)
        grads = take(1)[0]
        weights = take(1)[0] if first else None
        arrived, left = refs
        pairs = list(zip(block_refs, [*blocks_in, *tokens_in]))
        pairs += weight_copies(extra_ref, weights) if first else [(extra_ref, grads)]
        for copy in run_copies(arrived, pairs):
            copy.wait()
        if first:
            for index, ref in enumerate(tokens_in):
                value = ref[:frames].astype(F32).reshape(part, width)
                grads[index * part : (index + 1) * part, :] = value.astype(BF16)

        def one_pair(pair, carry):
            columns = pl.ds(pl.multiple_of(pair * PAIR, PAIR), PAIR)
            for index, ref in enumerate(blocks_in):
                at = slice(index * part, (index + 1) * part)
                for kind in range(3):
                    value = ref[kind * frames : (kind + 1) * frames, :, columns]
                    held[kind][at, :] = value.astype(F32).reshape(part, PAIR)
            if first:
                pieces = weights[pl.ds(pair * (PAIR // share), PAIR // share)].reshape(PAIR, width)
                held[3][...] = dot(grads[...], pieces, ((1,), (1,))).astype(BF16).astype(F32)
            else:
                held[3][...] = grads[:, columns].astype(F32)
            attend_pair(held, results, patches, total)
            for index, ref in enumerate(results_out):
                at = slice(index * part, (index + 1) * part)
                for kind in range(3):
                    value = results[kind][at, :].reshape(frames, patches, PAIR)
                    ref[kind * frames : (kind + 1) * frames, :, columns] = value.astype(BF16)
            return carry

        lax.fori_loop(0, lanes // PAIR, one_pair, 0)
        stores = run_copies(left, list(zip(results_out, out_refs)))
        if first:
            half = weights.shape[0] // 2
            later = weights[half:].reshape(lanes, width)
            later_ref[...] = dot(grads[...], later, ((1,), (1,))).astype(BF16)
        for store in stores:
            store.wait()

    out_shapes = [pltpu.VMEM((3 * frames, patches, lanes), BF16)] * count
    out_specs = [ANYWHERE] * count
    if first:
        out_shapes = out_shapes + [jax.ShapeDtypeStruct((rows, lanes), BF16)]
        out_specs = out_specs + [pl.BlockSpec(memory_space=pltpu.VMEM)]
    return pl.pallas_call(
        kernel,
        in_specs=[ANYWHERE] * (len(blocks) + 1 + len(after)),
        out_specs=out_specs,
        out_shape=out_shapes,
        scratch_shapes=scratch,
        compiler_params=BIG,
        cost_estimate=cost_of(16 if first else 10),
        name=name,
    )(*blocks, *operands, *settled(after))


def space_attention(own, far, own_tokens, weights_of, after=()):
    frames, rows, width = own_tokens.shape
    space, groups, tm, share = weights_of.shape[:4]
    pieces = space * groups * tm

    def kernel(*refs):
        own_refs, far_ref, own_token_ref, far_token_ref, gathered_ref = refs[:3], *refs[3:7]
        outs = refs[7 + len(after) : 10 + len(after)]
        weights, grads, sems = refs[10 + len(after) :]

        @pl.when(pl.program_id(0) == 0)
        def _():
            for copy in run_copies(sems, weight_copies(gathered_ref, weights)):
                copy.wait()
            whole = weights[...].reshape(width, width)
            for side in range(2):
                flat = (far_token_ref[0] if side else own_token_ref[...]).reshape(frames * rows, width)
                made = dot(flat, whole, ((1,), (1,))).astype(BF16)
                grads[side] = made.reshape(frames, rows, width)

        frame = pl.program_id(0)
        for pair in range(width // PAIR):
            columns = slice(pair * PAIR, (pair + 1) * PAIR)
            operands = [
                (near[0, :, columns].astype(F32), far_ref[index, 0, :, columns].astype(F32))
                for index, near in enumerate(own_refs)
            ]
            operands.append(tuple(grads[side, frame, :, columns].astype(F32) for side in range(2)))
            for out, value in zip(outs, own_back(*operands)):
                out[0, :, columns] = value.astype(BF16)

    near = pl.BlockSpec((1, rows, width), lambda f: (f, 0, 0))
    near_all = pl.BlockSpec((frames, rows, width), lambda f: (0, 0, 0))
    away = pl.BlockSpec((3, 1, rows, width), lambda f: (0, f, 0, 0))
    away_all = pl.BlockSpec((1, frames, rows, width), lambda f: (3, 0, 0, 0))
    return pl.pallas_call(
        kernel,
        grid_spec=pltpu.PrefetchScalarGridSpec(
            num_scalar_prefetch=0,
            grid=(frames,),
            in_specs=[near] * 3 + [away, near_all, away_all] + [ANYWHERE] * (1 + len(after)),
            out_specs=[near] * 3,
            scratch_shapes=[
                pltpu.VMEM((pieces, share, width), BF16),
                pltpu.VMEM((2, frames, rows, width), BF16),
                pltpu.SemaphoreType.DMA((pieces,)),
            ],
        ),
        out_shape=[jax.ShapeDtypeStruct((frames, rows, width), BF16)] * 3,
        compiler_params=BIG,
        cost_estimate=cost_of(20),
        name="space_attention",
    )(*settled([*own, far, own_tokens, far, weights_of, *after]))


def per_device(sizes, grad_out, time_q, time_k, time_v, space_q, space_k, space_v, time_wo, space_wo):
    frames, rows, width = grad_out.shape
    groups, tm, space = sizes
    patches, half = rows // tm, width // 2
    group, me = lax.axis_index("groups"), lax.axis_index("tm")
    share = time_wo.shape[0] // groups
    spots = jnp.concatenate([me ^ jnp.arange(tm, dtype=jnp.int32), group.reshape(1)]).astype(jnp.int32)
    order = []
    for low in range(tm // 2):
        order += [tm // 2 - 1 - low, tm - 1 - low]

    def to_partner(tensor, k):
        return lax.ppermute(tensor, "tm", [(i, i ^ k) for i in range(tm)]) if k else tensor

    def moved_one(parts, shape, plan, name, after=(), space=pltpu.HBM):
        one = lambda at, refs, outs: plan(at, refs, outs[0])
        return moved(spots, parts, [shape], one, name, after, (), space)[0]

    split = [t.reshape(frames, tm, patches, width) for t in (time_q, time_k, time_v, grad_out)]
    blocks = share // patches
    time_pieces, space_pieces = (t.reshape(groups, blocks, patches, width) for t in (time_wo, space_wo))

    def token_plan(at, parts, outs):
        pairs = []
        for k in order:
            pairs.append((parts[0].at[:, at[k]], outs[k].at[pl.ds(0, frames)]))
            pairs.append((parts[1].at[at[tm]], outs[k].at[pl.ds(frames, blocks)]))
        return pairs

    def payloads(chunk, more=(), after=()):
        def plan(at, parts, outs):
            columns = pl.ds(chunk * half, half)
            pairs = []
            for k in order:
                for i in range(3):
                    pairs.append((parts[i].at[:, at[k], :, columns], outs[k].at[pl.ds(i * frames, frames)]))
                for part in parts[3:]:
                    for side in range(2):
                        kept = outs[k].at[pl.ds(3 * frames + side * blocks, blocks)]
                        pairs.append((part.at[at[tm], :, :, pl.ds(side * half, half)], kept))
            return pairs

        shape = (3 * frames + 2 * blocks * len(more), patches, half)
        return moved(spots, [*split[:3], *more], [shape] * tm, plan, "payloads", after)

    def exchange(tensors):
        arrived = {k: to_partner(tensors[k], k) for k in order}
        return [pltpu.with_memory_space_constraint(arrived[k], pltpu.VMEM) for k in range(tm)]

    sent_tokens = moved(
        spots, [split[3], time_pieces], [(frames + blocks, patches, width)] * tm, token_plan, "token_payloads"
    )
    tokens = exchange(sent_tokens)
    first_sent = payloads(0, (space_pieces,), (sent_tokens[0],))
    early = exchange(first_sent)
    second_sent = payloads(1, (), (first_sent[0],))
    late = exchange(second_sent)

    both_cores = moved_one(
        [space_q, space_k, space_v, grad_out],
        (4, frames, rows, width),
        lambda at, refs, out: [(ref, out.at[i]) for i, ref in enumerate(refs)],
        "space_payload",
        (first_sent[0],),
        pltpu.VMEM,
    )
    far = lax.ppermute(both_cores, "space", [(0, 1), (1, 0)])

    def gathered(column):
        whole = lax.all_gather(column, ("space", "groups"), axis=0, tiled=True)
        return whole.reshape(space, groups, tm, share, width)

    time_weights = gathered(
        moved_one(
            tokens,
            (tm, blocks, patches, width),
            lambda at, refs, out: [
                (ref.at[pl.ds(frames, blocks)], out.at[at[k]]) for k, ref in enumerate(refs)
            ],
            "time_column",
            (first_sent[0], both_cores),
        )
    )
    space_weights = gathered(
        moved_one(
            early,
            (tm, blocks, patches, width),
            lambda at, refs, out: [
                (
                    ref.at[pl.ds(3 * frames + side * blocks, blocks)],
                    out.at[at[k], :, :, pl.ds(side * half, half)],
                )
                for k, ref in enumerate(refs)
                for side in range(2)
            ],
            "space_column",
            (second_sent[0],),
        )
    )

    *done, late_grad = time_chunk(frames, early, tokens, time_weights, None, "time_first", (far,))
    back = exchange(done)
    done = time_chunk(frames, late, (), None, late_grad, "time_second")
    back2 = exchange(done)

    def place(chunk):
        def plan(at, refs, outs):
            columns = pl.ds(chunk * half, half)
            return [
                (ref.at[pl.ds(kind * frames, frames)], outs[kind].at[:, at[k], :, columns])
                for k, ref in enumerate(refs)
                for kind in range(3)
            ]

        return plan

    shapes = [(frames, tm, patches, width)] * 3
    outs = moved(spots, back, shapes, place(0), "place_first", (), (), pltpu.HBM)
    space_out = space_attention(
        (space_q, space_k, space_v),
        far,
        grad_out,
        space_weights,
        (outs[0],),
    )
    outs = moved(spots, back2, shapes, place(1), "place_second", settled(space_out), outs, pltpu.HBM)
    time_out = [out.reshape(frames, rows, width) for out in outs]
    return (*time_out, *space_out)


def per_device_plain(sizes, grad_out, time_q, time_k, time_v, space_q, space_k, space_v, time_wo, space_wo):
    frames, rows, width = grad_out.shape
    groups, tm, space = sizes
    patches = rows // tm

    def to_patches(tensor):
        split = tensor.reshape(tensor.shape[:-2] + (tm, patches, width))
        return jnp.moveaxis(split, -3, 0)

    def exchanged(tensor):
        return lax.all_to_all(tensor, "tm", split_axis=0, concat_axis=0, tiled=True)

    time_qkv = exchanged(to_patches(jnp.stack([time_q, time_k, time_v])))

    both_wo = jnp.concatenate([time_wo, space_wo], axis=1)
    share = both_wo.shape[0] // groups
    if share * groups == both_wo.shape[0]:
        piece = lax.dynamic_slice_in_dim(both_wo, lax.axis_index("groups") * share, share, 0)
        whole = lax.all_gather(piece, ("tm", "space", "groups"), axis=0, tiled=True)
    else:
        whole = lax.all_gather(both_wo, ("tm", "space"), axis=0, tiled=True)

    swap = [(0, 1), (1, 0)]
    far = lax.ppermute(jnp.stack([space_q, space_k, space_v, grad_out]), "space", swap)
    tokens = grad_out.reshape(frames * rows, width)
    time_grad = jnp.einsum("td,cd->tc", tokens, whole[:, :width], preferred_element_type=F32)
    time_grad = exchanged(to_patches(time_grad.astype(BF16).reshape(frames, rows, width)))
    pieces = whole[:, width:].reshape(tm, space, -1, 1, width)
    pieces = jnp.moveaxis(pieces.reshape(tm, space, 1, -1, width), 0, 2)
    space_out = space_attention((space_q, space_k, space_v), far, grad_out, pieces)

    back = exchanged(time_attention(time_qkv, time_grad))
    time_out = [jnp.moveaxis(back[:, index], 0, 1).reshape(frames, rows, width) for index in range(3)]
    return (*time_out, *space_out)


def solution(mesh):
    tokens = P(("groups", "tm"), "space", None)
    weights = P(("tm", "space"), None)
    sizes = tuple(mesh.shape[name] for name in ("groups", "tm", "space"))
    groups, tm, space = sizes
    paired = groups == 2 and space == 2 and tm % 2 == 0 and tm & (tm - 1) == 0

    def body(*tensors):
        patches, rows = tensors[0].shape[1] // tm, tensors[-1].shape[0]
        fits = paired and patches % 8 == 0 and rows % (16 * groups) == 0 and rows % (groups * patches) == 0
        return (per_device if fits else per_device_plain)(sizes, *tensors)

    return jax.shard_map(
        body,
        mesh=mesh,
        in_specs=(tokens,) * 7 + (weights,) * 2,
        out_specs=(tokens,) * 6,
        check_vma=False,
    )
```

```python
import functools
import math

import jax
import jax.numpy as jnp
from jax import lax
from jax.experimental import pallas as pl
from jax.experimental.pallas import tpu as pltpu
from jax.sharding import PartitionSpec as P

HEAD_DIM = 64
PAIR = 2 * HEAD_DIM
F32 = jnp.float32
BF16 = jnp.bfloat16
SCALE = 1.0 / math.sqrt(HEAD_DIM)


def dot(left, right, contract):
    return lax.dot_general(left, right, (contract, ((), ())), preferred_element_type=F32)


def pair_back(query, keys, values, out_grad):
    rows = query.shape[0]
    lane = lax.broadcasted_iota(jnp.int32, (rows, PAIR), 1)
    first = lane < HEAD_DIM

    def stacked(tensor):
        zero = jnp.zeros_like(tensor)
        both = [jnp.where(first, tensor, zero), jnp.where(first, zero, tensor)]
        return jnp.concatenate(both, axis=0).astype(BF16)

    query2 = stacked(query)
    grad2 = stacked(out_grad)
    keys = keys.astype(BF16)
    values = values.astype(BF16)
    scores = dot(keys, query2, ((1,), (1,))) * SCALE
    expo = jnp.exp(scores - jnp.max(scores, axis=0, keepdims=True))
    probs = expo * (1.0 / jnp.sum(expo, axis=0, keepdims=True))
    dprob = dot(values, grad2, ((1,), (1,)))
    delta = jnp.sum(probs * dprob, axis=0, keepdims=True)
    dscore = (probs * (dprob - delta)).astype(BF16)
    grad_values = dot(probs.astype(BF16), grad2, ((1,), (0,)))
    grad_keys = dot(dscore, query2, ((1,), (0,))) * SCALE
    both = dot(dscore, keys, ((0,), (0,))) * SCALE
    grad_query = jnp.where(first, both[:rows], both[rows:])
    return grad_query, grad_keys, grad_values


def time_kernel(qkv_ref, grad_ref, out_ref, *scratch):
    sources, frames, patches, lanes = grad_ref.shape
    total = sources * frames
    held, results = scratch[:4], scratch[4:]
    for pair in range(lanes // PAIR):
        columns = slice(pair * PAIR, (pair + 1) * PAIR)
        for index in range(4):
            part = qkv_ref[:, index, :, :, columns] if index < 3 else grad_ref[:, :, :, columns]
            held[index][pair] = part.astype(F32).reshape(total * patches, PAIR)
        for patch in range(patches):
            rows = pl.ds(patch, total, stride=patches)
            done = pair_back(*[ref[pair, rows, :] for ref in held])
            for ref, value in zip(results, done):
                ref[pair, rows, :] = value
        for index in range(3):
            value = results[index][pair].reshape(sources, frames, patches, PAIR)
            out_ref[:, index, :, :, columns] = value.astype(BF16)


def time_kernel_wide(qkv_ref, grad_ref, out_ref):
    done = pair_back(*[qkv_ref[index, 0].astype(F32) for index in range(3)], grad_ref[0].astype(F32))
    for index in range(3):
        out_ref[index, 0] = done[index].astype(BF16)


def time_attention(qkv, grad):
    sources, _, frames, patches, width = qkv.shape
    total = sources * frames
    if patches % 8 == 0:
        lanes = 2 * PAIR
        return pl.pallas_call(
            time_kernel,
            grid=(width // lanes,),
            in_specs=[
                pl.BlockSpec((sources, 3, frames, patches, lanes), lambda i: (0, 0, 0, 0, i)),
                pl.BlockSpec((sources, frames, patches, lanes), lambda i: (0, 0, 0, i)),
            ],
            out_specs=pl.BlockSpec((sources, 3, frames, patches, lanes), lambda i: (0, 0, 0, 0, i)),
            out_shape=jax.ShapeDtypeStruct(qkv.shape, BF16),
            scratch_shapes=[pltpu.VMEM((lanes // PAIR, total * patches, PAIR), F32)] * 7,
            compiler_params=pltpu.CompilerParams(vmem_limit_bytes=40 * 2**20),
            name="time_attention",
        )(qkv, grad)
    qkv = qkv.transpose(1, 3, 0, 2, 4).reshape(3, patches, total, width)
    grad = grad.transpose(2, 0, 1, 3).reshape(patches, total, width)
    done = pl.pallas_call(
        time_kernel_wide,
        grid=(patches, width // PAIR),
        in_specs=[
            pl.BlockSpec((3, 1, total, PAIR), lambda p, i: (0, p, 0, i)),
            pl.BlockSpec((1, total, PAIR), lambda p, i: (p, 0, i)),
        ],
        out_specs=pl.BlockSpec((3, 1, total, PAIR), lambda p, i: (0, p, 0, i)),
        out_shape=jax.ShapeDtypeStruct(qkv.shape, BF16),
        compiler_params=pltpu.CompilerParams(vmem_limit_bytes=40 * 2**20),
        name="time_attention_wide",
    )(qkv, grad)
    done = done.reshape(3, patches, sources, frames, width)
    return done.transpose(2, 0, 3, 1, 4)


def own_back(queries, keys, values, grads):
    rows = queries[0].shape[0]
    first = lax.broadcasted_iota(jnp.int32, (rows, PAIR), 1) < HEAD_DIM
    zero = jnp.zeros((rows, PAIR), F32)

    def stacked(parts):
        both = []
        for part in parts:
            both += [jnp.where(first, part, zero), jnp.where(first, zero, part)]
        return jnp.concatenate(both, axis=0).astype(BF16)

    query2, grad2 = stacked(queries), stacked(grads)
    keys = jnp.concatenate(keys, axis=0).astype(BF16)
    values = jnp.concatenate(values, axis=0).astype(BF16)
    scores = dot(keys, query2, ((1,), (1,))) * SCALE
    expo = jnp.exp(scores - jnp.max(scores, axis=0, keepdims=True))
    probs = expo * (1.0 / jnp.sum(expo, axis=0, keepdims=True))
    dprob = dot(values, grad2, ((1,), (1,)))
    delta = jnp.sum(probs * dprob, axis=0, keepdims=True)
    dscore = (probs * (dprob - delta)).astype(BF16)
    grad_values = dot(probs[:rows].astype(BF16), grad2, ((1,), (0,)))
    grad_keys = dot(dscore[:rows], query2, ((1,), (0,))) * SCALE
    both = dot(dscore[:, : 2 * rows], keys, ((0,), (0,))) * SCALE
    grad_query = jnp.where(first, both[:rows], both[rows:])
    return grad_query, grad_keys, grad_values


ANYWHERE = pl.BlockSpec(memory_space=pl.ANY)
SCALARS = pl.BlockSpec(memory_space=pltpu.SMEM)
BIG = pltpu.CompilerParams(vmem_limit_bytes=24 * 2**20)


def settled(tensors):
    return [
        tensor
        if jax.typeof(tensor).memory_space == pltpu.VMEM
        else pltpu.with_memory_space_constraint(tensor, pltpu.HBM)
        for tensor in tensors
    ]


def cost_of(microseconds):
    return pl.CostEstimate(flops=0, transcendentals=0, bytes_accessed=int(microseconds * 3_690_000))


def run_copies(sems, pairs):
    copies = [pltpu.make_async_copy(src, dst, sems.at[i]) for i, (src, dst) in enumerate(pairs)]
    for copy in copies:
        copy.start()
    return copies


def moved(spots, parts, shapes, plan, name, after=(), kept=(), space=pltpu.VMEM):
    count = len(parts)

    def kernel(spots_ref, *refs):
        pairs = plan(spots_ref, refs[:count], refs[len(refs) - len(shapes) :])

        def body(sems):
            for copy in run_copies(sems, pairs):
                copy.wait()

        pl.run_scoped(body, pltpu.SemaphoreType.DMA((len(pairs),)))

    return pl.pallas_call(
        kernel,
        in_specs=[SCALARS] + [ANYWHERE] * (count + len(after) + len(kept)),
        out_specs=[ANYWHERE] * len(shapes),
        out_shape=[space(shape, BF16) for shape in shapes],
        input_output_aliases={1 + count + len(after) + i: i for i in range(len(kept))},
        compiler_params=pltpu.CompilerParams(vmem_limit_bytes=4 * 2**20),
        name=name,
    )(spots, *settled(parts), *after, *settled(kept))


def weight_copies(gathered_ref, weights):
    space, groups, tm = gathered_ref.shape[:3]
    return [
        (gathered_ref.at[s, g, t], weights.at[(t * space + s) * groups + g])
        for t in range(tm)
        for s in range(space)
        for g in range(groups)
    ]


def attend_pair(held, results, patches, total):
    for patch in range(patches):
        rows = pl.ds(patch, total, stride=patches)
        done = pair_back(*[ref[rows, :] for ref in held])
        for ref, value in zip(results, done):
            ref[rows, :] = value


def time_chunk(frames, blocks, token_blocks, gathered, late_grad, name, after=()):
    blocks = [*blocks, *token_blocks]
    first = late_grad is None
    count = len(blocks) // 2 if first else len(blocks)
    patches, lanes = blocks[0].shape[1:]
    total, part = count * frames, frames * patches
    rows, width = total * patches, 2 * lanes
    wide = [pltpu.VMEM(block.shape, BF16) for block in blocks]
    scratch = wide + [pltpu.VMEM((3 * frames, patches, lanes), BF16)] * count
    scratch += [pltpu.VMEM((rows, PAIR), F32)] * 7
    if first:
        space, groups, tm, share = gathered.shape[:4]
        scratch += [pltpu.VMEM((rows, width), BF16), pltpu.VMEM((space * groups * tm, share, width), BF16)]
        operands = settled((gathered,))
        copied = len(blocks) + space * groups * tm
    else:
        scratch += [pltpu.VMEM((rows, lanes), BF16)]
        operands = (late_grad,)
        copied = count + 1
    scratch += [pltpu.SemaphoreType.DMA((copied,)), pltpu.SemaphoreType.DMA((count,))]

    def kernel(*refs):
        refs = list(refs)

        def take(number):
            taken, refs[:number] = refs[:number], []
            return taken

        block_refs, extra_ref, _ = take(len(blocks)), take(1)[0], take(len(after))
        out_refs = take(count)
        later_ref = take(1)[0] if first else None
        blocks_in, results_out = take(len(blocks)), take(count)
        blocks_in, tokens_in = blocks_in[:count], blocks_in[count:]
        held, results = take(4), take(3)
        grads = take(1)[0]
        weights = take(1)[0] if first else None
        arrived, left = refs
        pairs = list(zip(block_refs, [*blocks_in, *tokens_in]))
        pairs += weight_copies(extra_ref, weights) if first else [(extra_ref, grads)]
        for copy in run_copies(arrived, pairs):
            copy.wait()
        if first:
            for index, ref in enumerate(tokens_in):
                value = ref[:frames].astype(F32).reshape(part, width)
                grads[index * part : (index + 1) * part, :] = value.astype(BF16)

        def one_pair(pair, carry):
            columns = pl.ds(pl.multiple_of(pair * PAIR, PAIR), PAIR)
            for index, ref in enumerate(blocks_in):
                at = slice(index * part, (index + 1) * part)
                for kind in range(3):
                    value = ref[kind * frames : (kind + 1) * frames, :, columns]
                    held[kind][at, :] = value.astype(F32).reshape(part, PAIR)
            if first:
                pieces = weights[pl.ds(pair * (PAIR // share), PAIR // share)].reshape(PAIR, width)
                held[3][...] = dot(grads[...], pieces, ((1,), (1,))).astype(BF16).astype(F32)
            else:
                held[3][...] = grads[:, columns].astype(F32)
            attend_pair(held, results, patches, total)
            for index, ref in enumerate(results_out):
                at = slice(index * part, (index + 1) * part)
                for kind in range(3):
                    value = results[kind][at, :].reshape(frames, patches, PAIR)
                    ref[kind * frames : (kind + 1) * frames, :, columns] = value.astype(BF16)
            return carry

        lax.fori_loop(0, lanes // PAIR, one_pair, 0)
        stores = run_copies(left, list(zip(results_out, out_refs)))
        if first:
            half = weights.shape[0] // 2
            later = weights[half:].reshape(lanes, width)
            later_ref[...] = dot(grads[...], later, ((1,), (1,))).astype(BF16)
        for store in stores:
            store.wait()

    out_shapes = [pltpu.VMEM((3 * frames, patches, lanes), BF16)] * count
    out_specs = [ANYWHERE] * count
    if first:
        out_shapes = out_shapes + [jax.ShapeDtypeStruct((rows, lanes), BF16)]
        out_specs = out_specs + [pl.BlockSpec(memory_space=pltpu.VMEM)]
    return pl.pallas_call(
        kernel,
        in_specs=[ANYWHERE] * (len(blocks) + 1 + len(after)),
        out_specs=out_specs,
        out_shape=out_shapes,
        scratch_shapes=scratch,
        compiler_params=BIG,
        cost_estimate=cost_of(16 if first else 10),
        name=name,
    )(*blocks, *operands, *settled(after))


def space_attention(other_core, own, far, own_tokens, weights_of, after=()):
    frames, rows, width = own_tokens.shape
    space, groups, tm, share = weights_of.shape[:4]
    pieces = space * groups * tm

    def kernel(core_ref, *refs):
        own_refs, far_refs, own_token_ref, far_token_ref, gathered_ref = refs[:3], refs[3:6], *refs[6:9]
        outs = refs[9 + len(after) : 12 + len(after)]
        weights, grads, sems = refs[12 + len(after) :]

        @pl.when(pl.program_id(0) == 0)
        def _():
            for copy in run_copies(sems, weight_copies(gathered_ref, weights)):
                copy.wait()
            whole = weights[...].reshape(width, width)
            for side in range(2):
                flat = (far_token_ref[0] if side else own_token_ref[...]).reshape(frames * rows, width)
                made = dot(flat, whole, ((1,), (1,))).astype(BF16)
                grads[side] = made.reshape(frames, rows, width)

        frame = pl.program_id(0)
        for pair in range(width // PAIR):
            columns = slice(pair * PAIR, (pair + 1) * PAIR)
            operands = [
                (near[0, :, columns].astype(F32), away[0, 0, :, columns].astype(F32))
                for near, away in zip(own_refs, far_refs)
            ]
            operands.append(tuple(grads[side, frame, :, columns].astype(F32) for side in range(2)))
            for out, value in zip(outs, own_back(*operands)):
                out[0, :, columns] = value.astype(BF16)

    near = pl.BlockSpec((1, rows, width), lambda f, core_ref: (f, 0, 0))
    near_all = pl.BlockSpec((frames, rows, width), lambda f, core_ref: (0, 0, 0))
    away = pl.BlockSpec((1, 1, rows, width), lambda f, core_ref: (core_ref[0], f, 0, 0))
    away_all = pl.BlockSpec((1, frames, rows, width), lambda f, core_ref: (core_ref[0], 0, 0, 0))
    return pl.pallas_call(
        kernel,
        grid_spec=pltpu.PrefetchScalarGridSpec(
            num_scalar_prefetch=1,
            grid=(frames,),
            in_specs=[near] * 3 + [away] * 3 + [near_all, away_all] + [ANYWHERE] * (1 + len(after)),
            out_specs=[near] * 3,
            scratch_shapes=[
                pltpu.VMEM((pieces, share, width), BF16),
                pltpu.VMEM((2, frames, rows, width), BF16),
                pltpu.SemaphoreType.DMA((pieces,)),
            ],
        ),
        out_shape=[jax.ShapeDtypeStruct((frames, rows, width), BF16)] * 3,
        compiler_params=BIG,
        cost_estimate=cost_of(20),
        name="space_attention",
    )(other_core, *settled([*own, *far[:3], own_tokens, far[3], weights_of, *after]))


def per_device(sizes, grad_out, time_q, time_k, time_v, space_q, space_k, space_v, time_wo, space_wo):
    frames, rows, width = grad_out.shape
    groups, tm, space = sizes
    patches, half = rows // tm, width // 2
    group, me = lax.axis_index("groups"), lax.axis_index("tm")
    share = time_wo.shape[0] // groups
    spots = jnp.concatenate([me ^ jnp.arange(tm, dtype=jnp.int32), group.reshape(1)]).astype(jnp.int32)
    other_core = (1 - lax.axis_index("space")).reshape(1).astype(jnp.int32)
    order = []
    for low in range(tm // 2):
        order += [tm // 2 - 1 - low, tm - 1 - low]

    def to_partner(tensor, k):
        return lax.ppermute(tensor, "tm", [(i, i ^ k) for i in range(tm)]) if k else tensor

    def moved_one(parts, shape, plan, name, after=(), space=pltpu.HBM):
        one = lambda at, refs, outs: plan(at, refs, outs[0])
        return moved(spots, parts, [shape], one, name, after, (), space)[0]

    split = [t.reshape(frames, tm, patches, width) for t in (time_q, time_k, time_v, grad_out)]
    blocks = share // patches
    time_pieces, space_pieces = (t.reshape(groups, blocks, patches, width) for t in (time_wo, space_wo))

    def token_plan(at, parts, outs):
        pairs = []
        for k in order:
            pairs.append((parts[0].at[:, at[k]], outs[k].at[pl.ds(0, frames)]))
            pairs.append((parts[1].at[at[tm]], outs[k].at[pl.ds(frames, blocks)]))
        return pairs

    def payloads(chunk, more=(), after=()):
        def plan(at, parts, outs):
            columns = pl.ds(chunk * half, half)
            pairs = []
            for k in order:
                for i in range(3):
                    pairs.append((parts[i].at[:, at[k], :, columns], outs[k].at[pl.ds(i * frames, frames)]))
                for part in parts[3:]:
                    for side in range(2):
                        kept = outs[k].at[pl.ds(3 * frames + side * blocks, blocks)]
                        pairs.append((part.at[at[tm], :, :, pl.ds(side * half, half)], kept))
            return pairs

        shape = (3 * frames + 2 * blocks * len(more), patches, half)
        return moved(spots, [*split[:3], *more], [shape] * tm, plan, "payloads", after)

    def exchange(tensors):
        arrived = {k: to_partner(tensors[k], k) for k in order}
        return [pltpu.with_memory_space_constraint(arrived[k], pltpu.VMEM) for k in range(tm)]

    sent_tokens = moved(
        spots, [split[3], time_pieces], [(frames + blocks, patches, width)] * tm, token_plan, "token_payloads"
    )
    tokens = exchange(sent_tokens)
    first_sent = payloads(0, (space_pieces,), (sent_tokens[0],))
    early = exchange(first_sent)
    second_sent = payloads(1, (), (first_sent[0],))
    late = exchange(second_sent)

    far = [lax.all_gather(tensor, "space", axis=0) for tensor in (space_q, space_k, space_v, grad_out)]

    def gathered(column):
        whole = lax.all_gather(column, ("space", "groups"), axis=0, tiled=True)
        return whole.reshape(space, groups, tm, share, width)

    time_weights = gathered(
        moved_one(
            tokens,
            (tm, blocks, patches, width),
            lambda at, refs, out: [
                (ref.at[pl.ds(frames, blocks)], out.at[at[k]]) for k, ref in enumerate(refs)
            ],
            "time_column",
            (first_sent[0],),
        )
    )
    space_weights = gathered(
        moved_one(
            early,
            (tm, blocks, patches, width),
            lambda at, refs, out: [
                (
                    ref.at[pl.ds(3 * frames + side * blocks, blocks)],
                    out.at[at[k], :, :, pl.ds(side * half, half)],
                )
                for k, ref in enumerate(refs)
                for side in range(2)
            ],
            "space_column",
            (second_sent[0],),
        )
    )

    *done, late_grad = time_chunk(frames, early, tokens, time_weights, None, "time_first")
    back = exchange(done)
    done = time_chunk(frames, late, (), None, late_grad, "time_second")
    back2 = exchange(done)

    def place(chunk):
        def plan(at, refs, outs):
            columns = pl.ds(chunk * half, half)
            return [
                (ref.at[pl.ds(kind * frames, frames)], outs[kind].at[:, at[k], :, columns])
                for k, ref in enumerate(refs)
                for kind in range(3)
            ]

        return plan

    shapes = [(frames, tm, patches, width)] * 3
    outs = moved(spots, back, shapes, place(0), "place_first", (), (), pltpu.HBM)
    space_out = space_attention(
        other_core,
        (space_q, space_k, space_v),
        far,
        grad_out,
        space_weights,
        (outs[0],),
    )
    outs = moved(spots, back2, shapes, place(1), "place_second", settled(space_out), outs, pltpu.HBM)
    time_out = [out.reshape(frames, rows, width) for out in outs]
    return (*time_out, *space_out)


def per_device_plain(sizes, grad_out, time_q, time_k, time_v, space_q, space_k, space_v, time_wo, space_wo):
    frames, rows, width = grad_out.shape
    groups, tm, space = sizes
    patches = rows // tm

    def to_patches(tensor):
        split = tensor.reshape(tensor.shape[:-2] + (tm, patches, width))
        return jnp.moveaxis(split, -3, 0)

    def exchanged(tensor):
        return lax.all_to_all(tensor, "tm", split_axis=0, concat_axis=0, tiled=True)

    time_qkv = exchanged(to_patches(jnp.stack([time_q, time_k, time_v])))

    both_wo = jnp.concatenate([time_wo, space_wo], axis=1)
    share = both_wo.shape[0] // groups
    if share * groups == both_wo.shape[0]:
        piece = lax.dynamic_slice_in_dim(both_wo, lax.axis_index("groups") * share, share, 0)
        whole = lax.all_gather(piece, ("tm", "space", "groups"), axis=0, tiled=True)
    else:
        whole = lax.all_gather(both_wo, ("tm", "space"), axis=0, tiled=True)

    far = [lax.all_gather(tensor, "space", axis=0) for tensor in (space_q, space_k, space_v, grad_out)]
    tokens = grad_out.reshape(frames * rows, width)
    time_grad = jnp.einsum("td,cd->tc", tokens, whole[:, :width], preferred_element_type=F32)
    time_grad = exchanged(to_patches(time_grad.astype(BF16).reshape(frames, rows, width)))
    pieces = whole[:, width:].reshape(tm, space, -1, 1, width)
    pieces = jnp.moveaxis(pieces.reshape(tm, space, 1, -1, width), 0, 2)
    space_out = space_attention(
        (1 - lax.axis_index("space")).reshape(1).astype(jnp.int32), (space_q, space_k, space_v), far, grad_out, pieces
    )

    back = exchanged(time_attention(time_qkv, time_grad))
    time_out = [jnp.moveaxis(back[:, index], 0, 1).reshape(frames, rows, width) for index in range(3)]
    return (*time_out, *space_out)


def solution(mesh):
    tokens = P(("groups", "tm"), "space", None)
    weights = P(("tm", "space"), None)
    sizes = tuple(mesh.shape[name] for name in ("groups", "tm", "space"))
    groups, tm, space = sizes
    paired = groups == 2 and space == 2 and tm % 2 == 0 and tm & (tm - 1) == 0

    def body(*tensors):
        patches, rows = tensors[0].shape[1] // tm, tensors[-1].shape[0]
        fits = paired and patches % 8 == 0 and rows % (16 * groups) == 0 and rows % (groups * patches) == 0
        return (per_device if fits else per_device_plain)(sizes, *tensors)

    return jax.shard_map(
        body,
        mesh=mesh,
        in_specs=(tokens,) * 7 + (weights,) * 2,
        out_specs=(tokens,) * 6,
        check_vma=False,
    )
```

```python
import functools
import math

import jax
import jax.numpy as jnp
from jax import lax
from jax.experimental import pallas as pl
from jax.experimental.pallas import tpu as pltpu
from jax.sharding import PartitionSpec as P

HEAD_DIM = 64
PAIR = 2 * HEAD_DIM
F32 = jnp.float32
BF16 = jnp.bfloat16
SCALE = 1.0 / math.sqrt(HEAD_DIM)


def dot(left, right, contract):
    return lax.dot_general(left, right, (contract, ((), ())), preferred_element_type=F32)


def pair_back(query, keys, values, out_grad):
    rows = query.shape[0]
    lane = lax.broadcasted_iota(jnp.int32, (rows, PAIR), 1)
    first = lane < HEAD_DIM

    def stacked(tensor):
        zero = jnp.zeros_like(tensor)
        both = [jnp.where(first, tensor, zero), jnp.where(first, zero, tensor)]
        return jnp.concatenate(both, axis=0).astype(BF16)

    query2 = stacked(query)
    grad2 = stacked(out_grad)
    keys = keys.astype(BF16)
    values = values.astype(BF16)
    scores = dot(keys, query2, ((1,), (1,))) * SCALE
    expo = jnp.exp(scores - jnp.max(scores, axis=0, keepdims=True))
    probs = expo * (1.0 / jnp.sum(expo, axis=0, keepdims=True))
    dprob = dot(values, grad2, ((1,), (1,)))
    delta = jnp.sum(probs * dprob, axis=0, keepdims=True)
    dscore = (probs * (dprob - delta)).astype(BF16)
    grad_values = dot(probs.astype(BF16), grad2, ((1,), (0,)))
    grad_keys = dot(dscore, query2, ((1,), (0,))) * SCALE
    both = dot(dscore, keys, ((0,), (0,))) * SCALE
    grad_query = jnp.where(first, both[:rows], both[rows:])
    return grad_query, grad_keys, grad_values


def time_kernel(qkv_ref, grad_ref, out_ref, *scratch):
    sources, frames, patches, lanes = grad_ref.shape
    total = sources * frames
    held, results = scratch[:4], scratch[4:]
    for pair in range(lanes // PAIR):
        columns = slice(pair * PAIR, (pair + 1) * PAIR)
        for index in range(4):
            part = qkv_ref[:, index, :, :, columns] if index < 3 else grad_ref[:, :, :, columns]
            held[index][pair] = part.astype(F32).reshape(total * patches, PAIR)
        for patch in range(patches):
            rows = pl.ds(patch, total, stride=patches)
            done = pair_back(*[ref[pair, rows, :] for ref in held])
            for ref, value in zip(results, done):
                ref[pair, rows, :] = value
        for index in range(3):
            value = results[index][pair].reshape(sources, frames, patches, PAIR)
            out_ref[:, index, :, :, columns] = value.astype(BF16)


def time_kernel_wide(qkv_ref, grad_ref, out_ref):
    done = pair_back(*[qkv_ref[index, 0].astype(F32) for index in range(3)], grad_ref[0].astype(F32))
    for index in range(3):
        out_ref[index, 0] = done[index].astype(BF16)


def time_attention(qkv, grad):
    sources, _, frames, patches, width = qkv.shape
    total = sources * frames
    if patches % 8 == 0:
        lanes = 2 * PAIR
        return pl.pallas_call(
            time_kernel,
            grid=(width // lanes,),
            in_specs=[
                pl.BlockSpec((sources, 3, frames, patches, lanes), lambda i: (0, 0, 0, 0, i)),
                pl.BlockSpec((sources, frames, patches, lanes), lambda i: (0, 0, 0, i)),
            ],
            out_specs=pl.BlockSpec((sources, 3, frames, patches, lanes), lambda i: (0, 0, 0, 0, i)),
            out_shape=jax.ShapeDtypeStruct(qkv.shape, BF16),
            scratch_shapes=[pltpu.VMEM((lanes // PAIR, total * patches, PAIR), F32)] * 7,
            compiler_params=pltpu.CompilerParams(vmem_limit_bytes=40 * 2**20),
            name="time_attention",
        )(qkv, grad)
    qkv = qkv.transpose(1, 3, 0, 2, 4).reshape(3, patches, total, width)
    grad = grad.transpose(2, 0, 1, 3).reshape(patches, total, width)
    done = pl.pallas_call(
        time_kernel_wide,
        grid=(patches, width // PAIR),
        in_specs=[
            pl.BlockSpec((3, 1, total, PAIR), lambda p, i: (0, p, 0, i)),
            pl.BlockSpec((1, total, PAIR), lambda p, i: (p, 0, i)),
        ],
        out_specs=pl.BlockSpec((3, 1, total, PAIR), lambda p, i: (0, p, 0, i)),
        out_shape=jax.ShapeDtypeStruct(qkv.shape, BF16),
        compiler_params=pltpu.CompilerParams(vmem_limit_bytes=40 * 2**20),
        name="time_attention_wide",
    )(qkv, grad)
    done = done.reshape(3, patches, sources, frames, width)
    return done.transpose(2, 0, 3, 1, 4)


def own_back(queries, keys, values, grads):
    rows = queries[0].shape[0]
    first = lax.broadcasted_iota(jnp.int32, (rows, PAIR), 1) < HEAD_DIM
    zero = jnp.zeros((rows, PAIR), F32)

    def stacked(parts):
        both = []
        for part in parts:
            both += [jnp.where(first, part, zero), jnp.where(first, zero, part)]
        return jnp.concatenate(both, axis=0).astype(BF16)

    query2, grad2 = stacked(queries), stacked(grads)
    keys = jnp.concatenate(keys, axis=0).astype(BF16)
    values = jnp.concatenate(values, axis=0).astype(BF16)
    scores = dot(keys, query2, ((1,), (1,))) * SCALE
    expo = jnp.exp(scores - jnp.max(scores, axis=0, keepdims=True))
    probs = expo * (1.0 / jnp.sum(expo, axis=0, keepdims=True))
    dprob = dot(values, grad2, ((1,), (1,)))
    delta = jnp.sum(probs * dprob, axis=0, keepdims=True)
    dscore = (probs * (dprob - delta)).astype(BF16)
    grad_values = dot(probs[:rows].astype(BF16), grad2, ((1,), (0,)))
    grad_keys = dot(dscore[:rows], query2, ((1,), (0,))) * SCALE
    both = dot(dscore[:, : 2 * rows], keys, ((0,), (0,))) * SCALE
    grad_query = jnp.where(first, both[:rows], both[rows:])
    return grad_query, grad_keys, grad_values


ANYWHERE = pl.BlockSpec(memory_space=pl.ANY)
SCALARS = pl.BlockSpec(memory_space=pltpu.SMEM)
BIG = pltpu.CompilerParams(vmem_limit_bytes=24 * 2**20)


def settled(tensors):
    return [
        tensor
        if jax.typeof(tensor).memory_space == pltpu.VMEM
        else pltpu.with_memory_space_constraint(tensor, pltpu.HBM)
        for tensor in tensors
    ]


def cost_of(microseconds):
    return pl.CostEstimate(flops=0, transcendentals=0, bytes_accessed=int(microseconds * 3_690_000))


def run_copies(sems, pairs):
    copies = [pltpu.make_async_copy(src, dst, sems.at[i]) for i, (src, dst) in enumerate(pairs)]
    for copy in copies:
        copy.start()
    return copies


def moved(spots, parts, shapes, plan, name, after=(), kept=(), space=pltpu.VMEM):
    count = len(parts)

    def kernel(spots_ref, *refs):
        pairs = plan(spots_ref, refs[:count], refs[len(refs) - len(shapes) :])

        def body(sems):
            for copy in run_copies(sems, pairs):
                copy.wait()

        pl.run_scoped(body, pltpu.SemaphoreType.DMA((len(pairs),)))

    return pl.pallas_call(
        kernel,
        in_specs=[SCALARS] + [ANYWHERE] * (count + len(after) + len(kept)),
        out_specs=[ANYWHERE] * len(shapes),
        out_shape=[space(shape, BF16) for shape in shapes],
        input_output_aliases={1 + count + len(after) + i: i for i in range(len(kept))},
        compiler_params=pltpu.CompilerParams(vmem_limit_bytes=4 * 2**20),
        name=name,
    )(spots, *settled(parts), *after, *settled(kept))


def weight_copies(gathered_ref, weights):
    space, groups, tm = gathered_ref.shape[:3]
    return [
        (gathered_ref.at[s, g, t], weights.at[(t * space + s) * groups + g])
        for t in range(tm)
        for s in range(space)
        for g in range(groups)
    ]


def attend_pair(held, results, patches, total):
    for patch in range(patches):
        rows = pl.ds(patch, total, stride=patches)
        done = pair_back(*[ref[rows, :] for ref in held])
        for ref, value in zip(results, done):
            ref[rows, :] = value


def time_chunk(frames, blocks, token_blocks, gathered, late_grad, name, after=()):
    blocks = [*blocks, *token_blocks]
    first = late_grad is None
    count = len(blocks) // 2 if first else len(blocks)
    patches, lanes = blocks[0].shape[1:]
    total, part = count * frames, frames * patches
    rows, width = total * patches, 2 * lanes
    wide = [pltpu.VMEM(block.shape, BF16) for block in blocks]
    scratch = wide + [pltpu.VMEM((3 * frames, patches, lanes), BF16)] * count
    scratch += [pltpu.VMEM((rows, PAIR), F32)] * 7
    if first:
        space, groups, tm, share = gathered.shape[:4]
        scratch += [pltpu.VMEM((rows, width), BF16), pltpu.VMEM((space * groups * tm, share, width), BF16)]
        operands = settled((gathered,))
        copied = len(blocks) + space * groups * tm
    else:
        scratch += [pltpu.VMEM((rows, lanes), BF16)]
        operands = (late_grad,)
        copied = count + 1
    scratch += [pltpu.SemaphoreType.DMA((copied,)), pltpu.SemaphoreType.DMA((count,))]

    def kernel(*refs):
        refs = list(refs)

        def take(number):
            taken, refs[:number] = refs[:number], []
            return taken

        block_refs, extra_ref, _ = take(len(blocks)), take(1)[0], take(len(after))
        out_refs = take(count)
        later_ref = take(1)[0] if first else None
        blocks_in, results_out = take(len(blocks)), take(count)
        blocks_in, tokens_in = blocks_in[:count], blocks_in[count:]
        held, results = take(4), take(3)
        grads = take(1)[0]
        weights = take(1)[0] if first else None
        arrived, left = refs
        pairs = list(zip(block_refs, [*blocks_in, *tokens_in]))
        pairs += weight_copies(extra_ref, weights) if first else [(extra_ref, grads)]
        for copy in run_copies(arrived, pairs):
            copy.wait()
        if first:
            for index, ref in enumerate(tokens_in):
                value = ref[:frames].astype(F32).reshape(part, width)
                grads[index * part : (index + 1) * part, :] = value.astype(BF16)

        def one_pair(pair, carry):
            columns = pl.ds(pl.multiple_of(pair * PAIR, PAIR), PAIR)
            for index, ref in enumerate(blocks_in):
                at = slice(index * part, (index + 1) * part)
                for kind in range(3):
                    value = ref[kind * frames : (kind + 1) * frames, :, columns]
                    held[kind][at, :] = value.astype(F32).reshape(part, PAIR)
            if first:
                pieces = weights[pl.ds(pair * (PAIR // share), PAIR // share)].reshape(PAIR, width)
                held[3][...] = dot(grads[...], pieces, ((1,), (1,))).astype(BF16).astype(F32)
            else:
                held[3][...] = grads[:, columns].astype(F32)
            attend_pair(held, results, patches, total)
            for index, ref in enumerate(results_out):
                at = slice(index * part, (index + 1) * part)
                for kind in range(3):
                    value = results[kind][at, :].reshape(frames, patches, PAIR)
                    ref[kind * frames : (kind + 1) * frames, :, columns] = value.astype(BF16)
            return carry

        lax.fori_loop(0, lanes // PAIR, one_pair, 0)
        stores = run_copies(left, list(zip(results_out, out_refs)))
        if first:
            half = weights.shape[0] // 2
            later = weights[half:].reshape(lanes, width)
            later_ref[...] = dot(grads[...], later, ((1,), (1,))).astype(BF16)
        for store in stores:
            store.wait()

    out_shapes = [pltpu.VMEM((3 * frames, patches, lanes), BF16)] * count
    out_specs = [ANYWHERE] * count
    if first:
        out_shapes = out_shapes + [jax.ShapeDtypeStruct((rows, lanes), BF16)]
        out_specs = out_specs + [pl.BlockSpec(memory_space=pltpu.VMEM)]
    return pl.pallas_call(
        kernel,
        in_specs=[ANYWHERE] * (len(blocks) + 1 + len(after)),
        out_specs=out_specs,
        out_shape=out_shapes,
        scratch_shapes=scratch,
        compiler_params=BIG,
        cost_estimate=cost_of(16 if first else 10),
        name=name,
    )(*blocks, *operands, *settled(after))


def space_attention(other_core, own, far, own_tokens, weights_of, after=()):
    frames, rows, width = own_tokens.shape
    space, groups, tm, share = weights_of.shape[:4]
    pieces = space * groups * tm

    def kernel(core_ref, *refs):
        own_refs, far_refs, own_token_ref, far_token_ref, gathered_ref = refs[:3], refs[3:6], *refs[6:9]
        outs = refs[9 + len(after) : 12 + len(after)]
        weights, grads, sems = refs[12 + len(after) :]

        @pl.when(pl.program_id(0) == 0)
        def _():
            for copy in run_copies(sems, weight_copies(gathered_ref, weights)):
                copy.wait()
            whole = weights[...].reshape(width, width)
            for side in range(2):
                flat = (far_token_ref[0] if side else own_token_ref[...]).reshape(frames * rows, width)
                made = dot(flat, whole, ((1,), (1,))).astype(BF16)
                grads[side] = made.reshape(frames, rows, width)

        frame = pl.program_id(0)
        for pair in range(width // PAIR):
            columns = slice(pair * PAIR, (pair + 1) * PAIR)
            operands = [
                (near[0, :, columns].astype(F32), away[0, 0, :, columns].astype(F32))
                for near, away in zip(own_refs, far_refs)
            ]
            operands.append(tuple(grads[side, frame, :, columns].astype(F32) for side in range(2)))
            for out, value in zip(outs, own_back(*operands)):
                out[0, :, columns] = value.astype(BF16)

    near = pl.BlockSpec((1, rows, width), lambda f, core_ref: (f, 0, 0))
    near_all = pl.BlockSpec((frames, rows, width), lambda f, core_ref: (0, 0, 0))
    away = pl.BlockSpec((1, 1, rows, width), lambda f, core_ref: (core_ref[0], f, 0, 0))
    away_all = pl.BlockSpec((1, frames, rows, width), lambda f, core_ref: (core_ref[0], 0, 0, 0))
    return pl.pallas_call(
        kernel,
        grid_spec=pltpu.PrefetchScalarGridSpec(
            num_scalar_prefetch=1,
            grid=(frames,),
            in_specs=[near] * 3 + [away] * 3 + [near_all, away_all] + [ANYWHERE] * (1 + len(after)),
            out_specs=[near] * 3,
            scratch_shapes=[
                pltpu.VMEM((pieces, share, width), BF16),
                pltpu.VMEM((2, frames, rows, width), BF16),
                pltpu.SemaphoreType.DMA((pieces,)),
            ],
        ),
        out_shape=[jax.ShapeDtypeStruct((frames, rows, width), BF16)] * 3,
        compiler_params=BIG,
        cost_estimate=cost_of(20),
        name="space_attention",
    )(other_core, *settled([*own, *far[:3], own_tokens, far[3], weights_of, *after]))


def per_device(sizes, grad_out, time_q, time_k, time_v, space_q, space_k, space_v, time_wo, space_wo):
    frames, rows, width = grad_out.shape
    groups, tm, space = sizes
    patches, half = rows // tm, width // 2
    group, me = lax.axis_index("groups"), lax.axis_index("tm")
    share = time_wo.shape[0] // groups
    spots = jnp.concatenate([me ^ jnp.arange(tm, dtype=jnp.int32), group.reshape(1)]).astype(jnp.int32)
    other_core = (1 - lax.axis_index("space")).reshape(1).astype(jnp.int32)
    order = [0]
    for k in range(1, tm // 2):
        order += [k, k + tm // 2 - 1]
    order.append(tm - 1)

    def to_partner(tensor, k):
        return lax.ppermute(tensor, "tm", [(i, i ^ k) for i in range(tm)]) if k else tensor

    def moved_one(parts, shape, plan, name, after=(), space=pltpu.HBM):
        one = lambda at, refs, outs: plan(at, refs, outs[0])
        return moved(spots, parts, [shape], one, name, after, (), space)[0]

    split = [t.reshape(frames, tm, patches, width) for t in (time_q, time_k, time_v, grad_out)]
    blocks = share // patches
    time_pieces, space_pieces = (t.reshape(groups, blocks, patches, width) for t in (time_wo, space_wo))

    def token_plan(at, parts, outs):
        pairs = []
        for k, out in zip(order, outs):
            pairs.append((parts[0].at[:, at[k]], out.at[pl.ds(0, frames)]))
            pairs.append((parts[1].at[at[tm]], out.at[pl.ds(frames, blocks)]))
        return pairs

    def chunk_plan(chunk, at, parts, outs):
        columns = pl.ds(chunk * half, half)
        pairs = []
        for k, out in zip(order, outs):
            for i in range(3):
                pairs.append((parts[i].at[:, at[k], :, columns], out.at[pl.ds(i * frames, frames)]))
            for part in parts[3:]:
                for side in range(2):
                    kept = out.at[pl.ds(3 * frames + side * blocks, blocks)]
                    pairs.append((part.at[at[tm], :, :, pl.ds(side * half, half)], kept))
        return pairs

    def first_plan(at, parts, outs):
        return token_plan(at, parts[:2], outs[:tm]) + chunk_plan(0, at, parts[2:], outs[tm:])

    def exchange(tensors):
        arrived = [to_partner(tensor, k) for k, tensor in zip(order, tensors)]
        return [pltpu.with_memory_space_constraint(tensor, pltpu.VMEM) for tensor in arrived]

    first_sent = moved(
        spots,
        [split[3], time_pieces, *split[:3], space_pieces],
        [(frames + blocks, patches, width)] * tm + [(3 * frames + 2 * blocks, patches, half)] * tm,
        first_plan,
        "first_payloads",
    )
    tokens = exchange(first_sent[:tm])
    early = exchange(first_sent[tm:])
    second_plan = functools.partial(chunk_plan, 1)
    shapes = [(3 * frames, patches, half)] * tm
    second_sent = moved(spots, split[:3], shapes, second_plan, "second_payloads", (first_sent[0],))
    late = exchange(second_sent)

    far = [lax.all_gather(tensor, "space", axis=0) for tensor in (space_q, space_k, space_v, grad_out)]

    def gathered(column):
        whole = lax.all_gather(column, ("space", "groups"), axis=0, tiled=True)
        return whole.reshape(space, groups, tm, share, width)

    time_weights = gathered(
        moved_one(
            tokens,
            (tm, blocks, patches, width),
            lambda at, refs, out: [
                (ref.at[pl.ds(frames, blocks)], out.at[at[k]]) for k, ref in zip(order, refs)
            ],
            "time_column",
        )
    )
    space_weights = gathered(
        moved_one(
            early,
            (tm, blocks, patches, width),
            lambda at, refs, out: [
                (
                    ref.at[pl.ds(3 * frames + side * blocks, blocks)],
                    out.at[at[k], :, :, pl.ds(side * half, half)],
                )
                for k, ref in zip(order, refs)
                for side in range(2)
            ],
            "space_column",
            (second_sent[0],),
        )
    )

    *done, late_grad = time_chunk(frames, early, tokens, time_weights, None, "time_first")
    back = exchange(done)
    done = time_chunk(frames, late, (), None, late_grad, "time_second")
    back2 = exchange(done)

    def place(chunk):
        def plan(at, refs, outs):
            columns = pl.ds(chunk * half, half)
            return [
                (ref.at[pl.ds(kind * frames, frames)], outs[kind].at[:, at[k], :, columns])
                for k, ref in zip(order, refs)
                for kind in range(3)
            ]

        return plan

    shapes = [(frames, tm, patches, width)] * 3
    outs = moved(spots, back, shapes, place(0), "place_first", (), (), pltpu.HBM)
    space_out = space_attention(
        other_core,
        (space_q, space_k, space_v),
        far,
        grad_out,
        space_weights,
        (outs[0],),
    )
    outs = moved(spots, back2, shapes, place(1), "place_second", settled(space_out), outs, pltpu.HBM)
    time_out = [out.reshape(frames, rows, width) for out in outs]
    return (*time_out, *space_out)


def per_device_plain(sizes, grad_out, time_q, time_k, time_v, space_q, space_k, space_v, time_wo, space_wo):
    frames, rows, width = grad_out.shape
    groups, tm, space = sizes
    patches = rows // tm

    def to_patches(tensor):
        split = tensor.reshape(tensor.shape[:-2] + (tm, patches, width))
        return jnp.moveaxis(split, -3, 0)

    def exchanged(tensor):
        return lax.all_to_all(tensor, "tm", split_axis=0, concat_axis=0, tiled=True)

    time_qkv = exchanged(to_patches(jnp.stack([time_q, time_k, time_v])))

    both_wo = jnp.concatenate([time_wo, space_wo], axis=1)
    share = both_wo.shape[0] // groups
    if share * groups == both_wo.shape[0]:
        piece = lax.dynamic_slice_in_dim(both_wo, lax.axis_index("groups") * share, share, 0)
        whole = lax.all_gather(piece, ("tm", "space", "groups"), axis=0, tiled=True)
    else:
        whole = lax.all_gather(both_wo, ("tm", "space"), axis=0, tiled=True)

    far = [lax.all_gather(tensor, "space", axis=0) for tensor in (space_q, space_k, space_v, grad_out)]
    tokens = grad_out.reshape(frames * rows, width)
    time_grad = jnp.einsum("td,cd->tc", tokens, whole[:, :width], preferred_element_type=F32)
    time_grad = exchanged(to_patches(time_grad.astype(BF16).reshape(frames, rows, width)))
    pieces = whole[:, width:].reshape(tm, space, -1, 1, width)
    pieces = jnp.moveaxis(pieces.reshape(tm, space, 1, -1, width), 0, 2)
    space_out = space_attention(
        (1 - lax.axis_index("space")).reshape(1).astype(jnp.int32), (space_q, space_k, space_v), far, grad_out, pieces
    )

    back = exchanged(time_attention(time_qkv, time_grad))
    time_out = [jnp.moveaxis(back[:, index], 0, 1).reshape(frames, rows, width) for index in range(3)]
    return (*time_out, *space_out)


def solution(mesh):
    tokens = P(("groups", "tm"), "space", None)
    weights = P(("tm", "space"), None)
    sizes = tuple(mesh.shape[name] for name in ("groups", "tm", "space"))
    groups, tm, space = sizes
    paired = groups == 2 and space == 2 and tm % 2 == 0 and tm & (tm - 1) == 0

    def body(*tensors):
        patches, rows = tensors[0].shape[1] // tm, tensors[-1].shape[0]
        fits = paired and patches % 8 == 0 and rows % (16 * groups) == 0 and rows % (groups * patches) == 0
        return (per_device if fits else per_device_plain)(sizes, *tensors)

    return jax.shard_map(
        body,
        mesh=mesh,
        in_specs=(tokens,) * 7 + (weights,) * 2,
        out_specs=(tokens,) * 6,
        check_vma=False,
    )
```

```python
import functools
import math

import jax
import jax.numpy as jnp
from jax import lax
from jax.experimental import pallas as pl
from jax.experimental.pallas import tpu as pltpu
from jax.sharding import PartitionSpec as P

HEAD_DIM = 64
PAIR = 2 * HEAD_DIM
F32 = jnp.float32
BF16 = jnp.bfloat16
SCALE = 1.0 / math.sqrt(HEAD_DIM)


def dot(left, right, contract):
    return lax.dot_general(left, right, (contract, ((), ())), preferred_element_type=F32)


def pair_back(query, keys, values, out_grad):
    rows = query.shape[0]
    lane = lax.broadcasted_iota(jnp.int32, (rows, PAIR), 1)
    first = lane < HEAD_DIM

    def stacked(tensor):
        zero = jnp.zeros_like(tensor)
        both = [jnp.where(first, tensor, zero), jnp.where(first, zero, tensor)]
        return jnp.concatenate(both, axis=0).astype(BF16)

    query2 = stacked(query)
    grad2 = stacked(out_grad)
    keys = keys.astype(BF16)
    values = values.astype(BF16)
    scores = dot(keys, query2, ((1,), (1,))) * SCALE
    expo = jnp.exp(scores - jnp.max(scores, axis=0, keepdims=True))
    probs = expo * (1.0 / jnp.sum(expo, axis=0, keepdims=True))
    dprob = dot(values, grad2, ((1,), (1,)))
    delta = jnp.sum(probs * dprob, axis=0, keepdims=True)
    dscore = (probs * (dprob - delta)).astype(BF16)
    grad_values = dot(probs.astype(BF16), grad2, ((1,), (0,)))
    grad_keys = dot(dscore, query2, ((1,), (0,))) * SCALE
    both = dot(dscore, keys, ((0,), (0,))) * SCALE
    grad_query = jnp.where(first, both[:rows], both[rows:])
    return grad_query, grad_keys, grad_values


def time_kernel(qkv_ref, grad_ref, out_ref, *scratch):
    sources, frames, patches, lanes = grad_ref.shape
    total = sources * frames
    held, results = scratch[:4], scratch[4:]
    for pair in range(lanes // PAIR):
        columns = slice(pair * PAIR, (pair + 1) * PAIR)
        for index in range(4):
            part = qkv_ref[:, index, :, :, columns] if index < 3 else grad_ref[:, :, :, columns]
            held[index][pair] = part.astype(F32).reshape(total * patches, PAIR)
        for patch in range(patches):
            rows = pl.ds(patch, total, stride=patches)
            done = pair_back(*[ref[pair, rows, :] for ref in held])
            for ref, value in zip(results, done):
                ref[pair, rows, :] = value
        for index in range(3):
            value = results[index][pair].reshape(sources, frames, patches, PAIR)
            out_ref[:, index, :, :, columns] = value.astype(BF16)


def time_kernel_wide(qkv_ref, grad_ref, out_ref):
    done = pair_back(*[qkv_ref[index, 0].astype(F32) for index in range(3)], grad_ref[0].astype(F32))
    for index in range(3):
        out_ref[index, 0] = done[index].astype(BF16)


def time_attention(qkv, grad):
    sources, _, frames, patches, width = qkv.shape
    total = sources * frames
    if patches % 8 == 0:
        lanes = 2 * PAIR
        return pl.pallas_call(
            time_kernel,
            grid=(width // lanes,),
            in_specs=[
                pl.BlockSpec((sources, 3, frames, patches, lanes), lambda i: (0, 0, 0, 0, i)),
                pl.BlockSpec((sources, frames, patches, lanes), lambda i: (0, 0, 0, i)),
            ],
            out_specs=pl.BlockSpec((sources, 3, frames, patches, lanes), lambda i: (0, 0, 0, 0, i)),
            out_shape=jax.ShapeDtypeStruct(qkv.shape, BF16),
            scratch_shapes=[pltpu.VMEM((lanes // PAIR, total * patches, PAIR), F32)] * 7,
            compiler_params=pltpu.CompilerParams(vmem_limit_bytes=40 * 2**20),
            name="time_attention",
        )(qkv, grad)
    qkv = qkv.transpose(1, 3, 0, 2, 4).reshape(3, patches, total, width)
    grad = grad.transpose(2, 0, 1, 3).reshape(patches, total, width)
    done = pl.pallas_call(
        time_kernel_wide,
        grid=(patches, width // PAIR),
        in_specs=[
            pl.BlockSpec((3, 1, total, PAIR), lambda p, i: (0, p, 0, i)),
            pl.BlockSpec((1, total, PAIR), lambda p, i: (p, 0, i)),
        ],
        out_specs=pl.BlockSpec((3, 1, total, PAIR), lambda p, i: (0, p, 0, i)),
        out_shape=jax.ShapeDtypeStruct(qkv.shape, BF16),
        compiler_params=pltpu.CompilerParams(vmem_limit_bytes=40 * 2**20),
        name="time_attention_wide",
    )(qkv, grad)
    done = done.reshape(3, patches, sources, frames, width)
    return done.transpose(2, 0, 3, 1, 4)


def own_back(queries, keys, values, grads):
    rows = queries[0].shape[0]
    first = lax.broadcasted_iota(jnp.int32, (rows, PAIR), 1) < HEAD_DIM
    zero = jnp.zeros((rows, PAIR), F32)

    def stacked(parts):
        both = []
        for part in parts:
            both += [jnp.where(first, part, zero), jnp.where(first, zero, part)]
        return jnp.concatenate(both, axis=0).astype(BF16)

    query2, grad2 = stacked(queries), stacked(grads)
    keys = jnp.concatenate(keys, axis=0).astype(BF16)
    values = jnp.concatenate(values, axis=0).astype(BF16)
    scores = dot(keys, query2, ((1,), (1,))) * SCALE
    expo = jnp.exp(scores - jnp.max(scores, axis=0, keepdims=True))
    probs = expo * (1.0 / jnp.sum(expo, axis=0, keepdims=True))
    dprob = dot(values, grad2, ((1,), (1,)))
    delta = jnp.sum(probs * dprob, axis=0, keepdims=True)
    dscore = (probs * (dprob - delta)).astype(BF16)
    grad_values = dot(probs[:rows].astype(BF16), grad2, ((1,), (0,)))
    grad_keys = dot(dscore[:rows], query2, ((1,), (0,))) * SCALE
    both = dot(dscore[:, : 2 * rows], keys, ((0,), (0,))) * SCALE
    grad_query = jnp.where(first, both[:rows], both[rows:])
    return grad_query, grad_keys, grad_values


ANYWHERE = pl.BlockSpec(memory_space=pl.ANY)
SCALARS = pl.BlockSpec(memory_space=pltpu.SMEM)
BIG = pltpu.CompilerParams(vmem_limit_bytes=24 * 2**20)


def settled(tensors):
    return [
        tensor
        if jax.typeof(tensor).memory_space == pltpu.VMEM
        else pltpu.with_memory_space_constraint(tensor, pltpu.HBM)
        for tensor in tensors
    ]


def cost_of(microseconds):
    return pl.CostEstimate(flops=0, transcendentals=0, bytes_accessed=int(microseconds * 3_690_000))


def run_copies(sems, pairs):
    copies = [pltpu.make_async_copy(src, dst, sems.at[i]) for i, (src, dst) in enumerate(pairs)]
    for copy in copies:
        copy.start()
    return copies


def moved(spots, parts, shapes, plan, name, after=(), kept=(), space=pltpu.VMEM):
    count = len(parts)

    def kernel(spots_ref, *refs):
        pairs = plan(spots_ref, refs[:count], refs[len(refs) - len(shapes) :])

        def body(sems):
            for copy in run_copies(sems, pairs):
                copy.wait()

        pl.run_scoped(body, pltpu.SemaphoreType.DMA((len(pairs),)))

    return pl.pallas_call(
        kernel,
        in_specs=[SCALARS] + [ANYWHERE] * (count + len(after) + len(kept)),
        out_specs=[ANYWHERE] * len(shapes),
        out_shape=[space(shape, BF16) for shape in shapes],
        input_output_aliases={1 + count + len(after) + i: i for i in range(len(kept))},
        compiler_params=pltpu.CompilerParams(vmem_limit_bytes=4 * 2**20),
        name=name,
    )(spots, *settled(parts), *after, *settled(kept))


def weight_copies(gathered_ref, weights):
    space, groups, tm = gathered_ref.shape[:3]
    return [
        (gathered_ref.at[s, g, t], weights.at[(t * space + s) * groups + g])
        for t in range(tm)
        for s in range(space)
        for g in range(groups)
    ]


def attend_pair(held, results, patches, total):
    for patch in range(patches):
        rows = pl.ds(patch, total, stride=patches)
        done = pair_back(*[ref[rows, :] for ref in held])
        for ref, value in zip(results, done):
            ref[rows, :] = value


def time_chunk(frames, blocks, token_blocks, gathered, late_grad, name, after=()):
    blocks = [*blocks, *token_blocks]
    first = late_grad is None
    count = len(blocks) // 2 if first else len(blocks)
    patches, lanes = blocks[0].shape[1:]
    total, part = count * frames, frames * patches
    rows, width = total * patches, 2 * lanes
    wide = [pltpu.VMEM(block.shape, BF16) for block in blocks]
    scratch = wide + [pltpu.VMEM((3 * frames, patches, lanes), BF16)] * count
    scratch += [pltpu.VMEM((rows, PAIR), F32)] * 7
    if first:
        space, groups, tm, share = gathered.shape[:4]
        scratch += [pltpu.VMEM((rows, width), BF16), pltpu.VMEM((space * groups * tm, share, width), BF16)]
        operands = settled((gathered,))
        copied = len(blocks) + space * groups * tm
    else:
        scratch += [pltpu.VMEM((rows, lanes), BF16)]
        operands = (late_grad,)
        copied = count + 1
    scratch += [pltpu.SemaphoreType.DMA((copied,)), pltpu.SemaphoreType.DMA((count,))]

    def kernel(*refs):
        refs = list(refs)

        def take(number):
            taken, refs[:number] = refs[:number], []
            return taken

        block_refs, extra_ref, _ = take(len(blocks)), take(1)[0], take(len(after))
        out_refs = take(count)
        later_ref = take(1)[0] if first else None
        blocks_in, results_out = take(len(blocks)), take(count)
        blocks_in, tokens_in = blocks_in[:count], blocks_in[count:]
        held, results = take(4), take(3)
        grads = take(1)[0]
        weights = take(1)[0] if first else None
        arrived, left = refs
        pairs = list(zip(block_refs, [*blocks_in, *tokens_in]))
        pairs += weight_copies(extra_ref, weights) if first else [(extra_ref, grads)]
        for copy in run_copies(arrived, pairs):
            copy.wait()
        if first:
            for index, ref in enumerate(tokens_in):
                value = ref[:frames].astype(F32).reshape(part, width)
                grads[index * part : (index + 1) * part, :] = value.astype(BF16)

        def one_pair(pair, carry):
            columns = pl.ds(pl.multiple_of(pair * PAIR, PAIR), PAIR)
            for index, ref in enumerate(blocks_in):
                at = slice(index * part, (index + 1) * part)
                for kind in range(3):
                    value = ref[kind * frames : (kind + 1) * frames, :, columns]
                    held[kind][at, :] = value.astype(F32).reshape(part, PAIR)
            if first:
                pieces = weights[pl.ds(pair * (PAIR // share), PAIR // share)].reshape(PAIR, width)
                held[3][...] = dot(grads[...], pieces, ((1,), (1,))).astype(BF16).astype(F32)
            else:
                held[3][...] = grads[:, columns].astype(F32)
            attend_pair(held, results, patches, total)
            for index, ref in enumerate(results_out):
                at = slice(index * part, (index + 1) * part)
                for kind in range(3):
                    value = results[kind][at, :].reshape(frames, patches, PAIR)
                    ref[kind * frames : (kind + 1) * frames, :, columns] = value.astype(BF16)
            return carry

        lax.fori_loop(0, lanes // PAIR, one_pair, 0)
        stores = run_copies(left, list(zip(results_out, out_refs)))
        if first:
            half = weights.shape[0] // 2
            later = weights[half:].reshape(lanes, width)
            later_ref[...] = dot(grads[...], later, ((1,), (1,))).astype(BF16)
        for store in stores:
            store.wait()

    out_shapes = [pltpu.VMEM((3 * frames, patches, lanes), BF16)] * count
    out_specs = [ANYWHERE] * count
    if first:
        out_shapes = out_shapes + [jax.ShapeDtypeStruct((rows, lanes), BF16)]
        out_specs = out_specs + [pl.BlockSpec(memory_space=pltpu.VMEM)]
    return pl.pallas_call(
        kernel,
        in_specs=[ANYWHERE] * (len(blocks) + 1 + len(after)),
        out_specs=out_specs,
        out_shape=out_shapes,
        scratch_shapes=scratch,
        compiler_params=BIG,
        cost_estimate=cost_of(16 if first else 10),
        name=name,
    )(*blocks, *operands, *settled(after))


def space_attention(other_core, own, far, own_tokens, weights_of, after=()):
    frames, rows, width = own_tokens.shape
    space, groups, tm, share = weights_of.shape[:4]
    pieces = space * groups * tm

    def kernel(core_ref, *refs):
        own_refs, far_refs, own_token_ref, far_token_ref, gathered_ref = refs[:3], refs[3:6], *refs[6:9]
        outs = refs[9 + len(after) : 12 + len(after)]
        weights, grads, sems = refs[12 + len(after) :]

        @pl.when(pl.program_id(0) == 0)
        def _():
            for copy in run_copies(sems, weight_copies(gathered_ref, weights)):
                copy.wait()
            whole = weights[...].reshape(width, width)
            for side in range(2):
                flat = (far_token_ref[0] if side else own_token_ref[...]).reshape(frames * rows, width)
                made = dot(flat, whole, ((1,), (1,))).astype(BF16)
                grads[side] = made.reshape(frames, rows, width)

        frame = pl.program_id(0)
        for pair in range(width // PAIR):
            columns = slice(pair * PAIR, (pair + 1) * PAIR)
            operands = [
                (near[0, :, columns].astype(F32), away[0, 0, :, columns].astype(F32))
                for near, away in zip(own_refs, far_refs)
            ]
            operands.append(tuple(grads[side, frame, :, columns].astype(F32) for side in range(2)))
            for out, value in zip(outs, own_back(*operands)):
                out[0, :, columns] = value.astype(BF16)

    near = pl.BlockSpec((1, rows, width), lambda f, core_ref: (f, 0, 0))
    near_all = pl.BlockSpec((frames, rows, width), lambda f, core_ref: (0, 0, 0))
    away = pl.BlockSpec((1, 1, rows, width), lambda f, core_ref: (core_ref[0], f, 0, 0))
    away_all = pl.BlockSpec((1, frames, rows, width), lambda f, core_ref: (core_ref[0], 0, 0, 0))
    return pl.pallas_call(
        kernel,
        grid_spec=pltpu.PrefetchScalarGridSpec(
            num_scalar_prefetch=1,
            grid=(frames,),
            in_specs=[near] * 3 + [away] * 3 + [near_all, away_all] + [ANYWHERE] * (1 + len(after)),
            out_specs=[near] * 3,
            scratch_shapes=[
                pltpu.VMEM((pieces, share, width), BF16),
                pltpu.VMEM((2, frames, rows, width), BF16),
                pltpu.SemaphoreType.DMA((pieces,)),
            ],
        ),
        out_shape=[jax.ShapeDtypeStruct((frames, rows, width), BF16)] * 3,
        compiler_params=BIG,
        cost_estimate=cost_of(20),
        name="space_attention",
    )(other_core, *settled([*own, *far[:3], own_tokens, far[3], weights_of, *after]))


def per_device(sizes, grad_out, time_q, time_k, time_v, space_q, space_k, space_v, time_wo, space_wo):
    frames, rows, width = grad_out.shape
    groups, tm, space = sizes
    patches, half = rows // tm, width // 2
    group, me = lax.axis_index("groups"), lax.axis_index("tm")
    share = time_wo.shape[0] // groups
    spots = jnp.concatenate([me ^ jnp.arange(tm, dtype=jnp.int32), group.reshape(1)]).astype(jnp.int32)
    other_core = (1 - lax.axis_index("space")).reshape(1).astype(jnp.int32)
    order = [0]
    for k in range(1, tm // 2):
        order += [k, k + tm // 2 - 1]
    order.append(tm - 1)

    def to_partner(tensor, k):
        return lax.ppermute(tensor, "tm", [(i, i ^ k) for i in range(tm)]) if k else tensor

    split = [t.reshape(frames, tm, patches, width) for t in (time_q, time_k, time_v, grad_out)]
    blocks = share // patches
    time_pieces, space_pieces = (t.reshape(groups, blocks, patches, width) for t in (time_wo, space_wo))

    def token_plan(at, parts, outs):
        pairs = []
        for k, out in zip(order, outs):
            pairs.append((parts[0].at[:, at[k]], out.at[pl.ds(0, frames)]))
            for i, part in enumerate(parts[1:]):
                pairs.append((part.at[at[tm]], out.at[pl.ds(frames + i * blocks, blocks)]))
        return pairs

    def chunk_payloads(chunk, name, after):
        def plan(at, parts, outs):
            columns = pl.ds(chunk * half, half)
            return [
                (part.at[:, at[k], :, columns], out.at[pl.ds(i * frames, frames)])
                for k, out in zip(order, outs)
                for i, part in enumerate(parts)
            ]

        return moved(spots, split[:3], [(3 * frames, patches, half)] * tm, plan, name, after)

    def exchange(tensors):
        arrived = [to_partner(tensor, k) for k, tensor in zip(order, tensors)]
        return [pltpu.with_memory_space_constraint(tensor, pltpu.VMEM) for tensor in arrived]

    sent = moved(
        spots,
        [split[3], time_pieces, space_pieces],
        [(frames + 2 * blocks, patches, width)] * tm,
        token_plan,
        "token_payloads",
    )
    tokens = exchange(sent)
    first_sent = chunk_payloads(0, "first_payloads", (sent[0],))
    early = exchange(first_sent)
    late = exchange(chunk_payloads(1, "second_payloads", (first_sent[0],)))

    far = [lax.all_gather(tensor, "space", axis=0) for tensor in (space_q, space_k, space_v, grad_out)]

    def gathered(column):
        whole = lax.all_gather(column, ("space", "groups"), axis=0, tiled=True)
        return whole.reshape(space, groups, tm, share, width)

    columns = moved(
        spots,
        tokens,
        [(tm, blocks, patches, width)] * 2,
        lambda at, refs, outs: [
            (ref.at[pl.ds(frames + i * blocks, blocks)], out.at[at[k]])
            for k, ref in zip(order, refs)
            for i, out in enumerate(outs)
        ],
        "columns",
        (first_sent[0],),
        (),
        pltpu.HBM,
    )
    time_weights, space_weights = (gathered(column) for column in columns)

    *done, late_grad = time_chunk(frames, early, tokens, time_weights, None, "time_first")
    back = exchange(done)
    done = time_chunk(frames, late, (), None, late_grad, "time_second")
    back2 = exchange(done)

    def place(chunk):
        def plan(at, refs, outs):
            columns = pl.ds(chunk * half, half)
            return [
                (ref.at[pl.ds(kind * frames, frames)], outs[kind].at[:, at[k], :, columns])
                for k, ref in zip(order, refs)
                for kind in range(3)
            ]

        return plan

    shapes = [(frames, tm, patches, width)] * 3
    outs = moved(spots, back, shapes, place(0), "place_first", (), (), pltpu.HBM)
    space_out = space_attention(
        other_core,
        (space_q, space_k, space_v),
        far,
        grad_out,
        space_weights,
        (outs[0],),
    )
    outs = moved(spots, back2, shapes, place(1), "place_second", settled(space_out), outs, pltpu.HBM)
    time_out = [out.reshape(frames, rows, width) for out in outs]
    return (*time_out, *space_out)


def per_device_plain(sizes, grad_out, time_q, time_k, time_v, space_q, space_k, space_v, time_wo, space_wo):
    frames, rows, width = grad_out.shape
    groups, tm, space = sizes
    patches = rows // tm

    def to_patches(tensor):
        split = tensor.reshape(tensor.shape[:-2] + (tm, patches, width))
        return jnp.moveaxis(split, -3, 0)

    def exchanged(tensor):
        return lax.all_to_all(tensor, "tm", split_axis=0, concat_axis=0, tiled=True)

    time_qkv = exchanged(to_patches(jnp.stack([time_q, time_k, time_v])))

    both_wo = jnp.concatenate([time_wo, space_wo], axis=1)
    share = both_wo.shape[0] // groups
    if share * groups == both_wo.shape[0]:
        piece = lax.dynamic_slice_in_dim(both_wo, lax.axis_index("groups") * share, share, 0)
        whole = lax.all_gather(piece, ("tm", "space", "groups"), axis=0, tiled=True)
    else:
        whole = lax.all_gather(both_wo, ("tm", "space"), axis=0, tiled=True)

    far = [lax.all_gather(tensor, "space", axis=0) for tensor in (space_q, space_k, space_v, grad_out)]
    tokens = grad_out.reshape(frames * rows, width)
    time_grad = jnp.einsum("td,cd->tc", tokens, whole[:, :width], preferred_element_type=F32)
    time_grad = exchanged(to_patches(time_grad.astype(BF16).reshape(frames, rows, width)))
    pieces = whole[:, width:].reshape(tm, space, -1, 1, width)
    pieces = jnp.moveaxis(pieces.reshape(tm, space, 1, -1, width), 0, 2)
    space_out = space_attention(
        (1 - lax.axis_index("space")).reshape(1).astype(jnp.int32), (space_q, space_k, space_v), far, grad_out, pieces
    )

    back = exchanged(time_attention(time_qkv, time_grad))
    time_out = [jnp.moveaxis(back[:, index], 0, 1).reshape(frames, rows, width) for index in range(3)]
    return (*time_out, *space_out)


def solution(mesh):
    tokens = P(("groups", "tm"), "space", None)
    weights = P(("tm", "space"), None)
    sizes = tuple(mesh.shape[name] for name in ("groups", "tm", "space"))
    groups, tm, space = sizes
    paired = groups == 2 and space == 2 and tm % 2 == 0 and tm & (tm - 1) == 0

    def body(*tensors):
        patches, rows = tensors[0].shape[1] // tm, tensors[-1].shape[0]
        fits = paired and patches % 8 == 0 and rows % (16 * groups) == 0 and rows % (groups * patches) == 0
        return (per_device if fits else per_device_plain)(sizes, *tensors)

    return jax.shard_map(
        body,
        mesh=mesh,
        in_specs=(tokens,) * 7 + (weights,) * 2,
        out_specs=(tokens,) * 6,
        check_vma=False,
    )
```

```python
import functools
import math

import jax
import jax.numpy as jnp
from jax import lax
from jax.experimental import pallas as pl
from jax.experimental.pallas import tpu as pltpu
from jax.sharding import PartitionSpec as P

HEAD_DIM = 64
PAIR = 2 * HEAD_DIM
F32 = jnp.float32
BF16 = jnp.bfloat16
SCALE = 1.0 / math.sqrt(HEAD_DIM)


def dot(left, right, contract):
    return lax.dot_general(left, right, (contract, ((), ())), preferred_element_type=F32)


def pair_back(query, keys, values, out_grad):
    rows = query.shape[0]
    lane = lax.broadcasted_iota(jnp.int32, (rows, PAIR), 1)
    first = lane < HEAD_DIM

    def stacked(tensor):
        zero = jnp.zeros_like(tensor)
        both = [jnp.where(first, tensor, zero), jnp.where(first, zero, tensor)]
        return jnp.concatenate(both, axis=0).astype(BF16)

    query2 = stacked(query)
    grad2 = stacked(out_grad)
    keys = keys.astype(BF16)
    values = values.astype(BF16)
    scores = dot(keys, query2, ((1,), (1,))) * SCALE
    expo = jnp.exp(scores - jnp.max(scores, axis=0, keepdims=True))
    probs = expo * (1.0 / jnp.sum(expo, axis=0, keepdims=True))
    dprob = dot(values, grad2, ((1,), (1,)))
    delta = jnp.sum(probs * dprob, axis=0, keepdims=True)
    dscore = (probs * (dprob - delta)).astype(BF16)
    grad_values = dot(probs.astype(BF16), grad2, ((1,), (0,)))
    grad_keys = dot(dscore, query2, ((1,), (0,))) * SCALE
    both = dot(dscore, keys, ((0,), (0,))) * SCALE
    grad_query = jnp.where(first, both[:rows], both[rows:])
    return grad_query, grad_keys, grad_values


def time_kernel(qkv_ref, grad_ref, out_ref, *scratch):
    sources, frames, patches, lanes = grad_ref.shape
    total = sources * frames
    held, results = scratch[:4], scratch[4:]
    for pair in range(lanes // PAIR):
        columns = slice(pair * PAIR, (pair + 1) * PAIR)
        for index in range(4):
            part = qkv_ref[:, index, :, :, columns] if index < 3 else grad_ref[:, :, :, columns]
            held[index][pair] = part.astype(F32).reshape(total * patches, PAIR)
        for patch in range(patches):
            rows = pl.ds(patch, total, stride=patches)
            done = pair_back(*[ref[pair, rows, :] for ref in held])
            for ref, value in zip(results, done):
                ref[pair, rows, :] = value
        for index in range(3):
            value = results[index][pair].reshape(sources, frames, patches, PAIR)
            out_ref[:, index, :, :, columns] = value.astype(BF16)


def time_kernel_wide(qkv_ref, grad_ref, out_ref):
    done = pair_back(*[qkv_ref[index, 0].astype(F32) for index in range(3)], grad_ref[0].astype(F32))
    for index in range(3):
        out_ref[index, 0] = done[index].astype(BF16)


def time_attention(qkv, grad):
    sources, _, frames, patches, width = qkv.shape
    total = sources * frames
    if patches % 8 == 0:
        lanes = 2 * PAIR
        return pl.pallas_call(
            time_kernel,
            grid=(width // lanes,),
            in_specs=[
                pl.BlockSpec((sources, 3, frames, patches, lanes), lambda i: (0, 0, 0, 0, i)),
                pl.BlockSpec((sources, frames, patches, lanes), lambda i: (0, 0, 0, i)),
            ],
            out_specs=pl.BlockSpec((sources, 3, frames, patches, lanes), lambda i: (0, 0, 0, 0, i)),
            out_shape=jax.ShapeDtypeStruct(qkv.shape, BF16),
            scratch_shapes=[pltpu.VMEM((lanes // PAIR, total * patches, PAIR), F32)] * 7,
            compiler_params=pltpu.CompilerParams(vmem_limit_bytes=40 * 2**20),
            name="time_attention",
        )(qkv, grad)
    qkv = qkv.transpose(1, 3, 0, 2, 4).reshape(3, patches, total, width)
    grad = grad.transpose(2, 0, 1, 3).reshape(patches, total, width)
    done = pl.pallas_call(
        time_kernel_wide,
        grid=(patches, width // PAIR),
        in_specs=[
            pl.BlockSpec((3, 1, total, PAIR), lambda p, i: (0, p, 0, i)),
            pl.BlockSpec((1, total, PAIR), lambda p, i: (p, 0, i)),
        ],
        out_specs=pl.BlockSpec((3, 1, total, PAIR), lambda p, i: (0, p, 0, i)),
        out_shape=jax.ShapeDtypeStruct(qkv.shape, BF16),
        compiler_params=pltpu.CompilerParams(vmem_limit_bytes=40 * 2**20),
        name="time_attention_wide",
    )(qkv, grad)
    done = done.reshape(3, patches, sources, frames, width)
    return done.transpose(2, 0, 3, 1, 4)


def own_back(queries, keys, values, grads):
    rows = queries[0].shape[0]
    first = lax.broadcasted_iota(jnp.int32, (rows, PAIR), 1) < HEAD_DIM
    zero = jnp.zeros((rows, PAIR), F32)

    def stacked(parts):
        both = []
        for part in parts:
            both += [jnp.where(first, part, zero), jnp.where(first, zero, part)]
        return jnp.concatenate(both, axis=0).astype(BF16)

    query2, grad2 = stacked(queries), stacked(grads)
    keys = jnp.concatenate(keys, axis=0).astype(BF16)
    values = jnp.concatenate(values, axis=0).astype(BF16)
    scores = dot(keys, query2, ((1,), (1,))) * SCALE
    expo = jnp.exp(scores - jnp.max(scores, axis=0, keepdims=True))
    probs = expo * (1.0 / jnp.sum(expo, axis=0, keepdims=True))
    dprob = dot(values, grad2, ((1,), (1,)))
    delta = jnp.sum(probs * dprob, axis=0, keepdims=True)
    dscore = (probs * (dprob - delta)).astype(BF16)
    grad_values = dot(probs[:rows].astype(BF16), grad2, ((1,), (0,)))
    grad_keys = dot(dscore[:rows], query2, ((1,), (0,))) * SCALE
    both = dot(dscore[:, : 2 * rows], keys, ((0,), (0,))) * SCALE
    grad_query = jnp.where(first, both[:rows], both[rows:])
    return grad_query, grad_keys, grad_values


ANYWHERE = pl.BlockSpec(memory_space=pl.ANY)
SCALARS = pl.BlockSpec(memory_space=pltpu.SMEM)
BIG = pltpu.CompilerParams(vmem_limit_bytes=24 * 2**20)


def settled(tensors):
    return [
        tensor
        if jax.typeof(tensor).memory_space == pltpu.VMEM
        else pltpu.with_memory_space_constraint(tensor, pltpu.HBM)
        for tensor in tensors
    ]


def cost_of(microseconds):
    return pl.CostEstimate(flops=0, transcendentals=0, bytes_accessed=int(microseconds * 3_690_000))


def run_copies(sems, pairs):
    copies = [pltpu.make_async_copy(src, dst, sems.at[i]) for i, (src, dst) in enumerate(pairs)]
    for copy in copies:
        copy.start()
    return copies


def moved(spots, parts, shapes, plan, name, after=(), kept=(), space=pltpu.VMEM):
    count = len(parts)

    def kernel(spots_ref, *refs):
        pairs = plan(spots_ref, refs[:count], refs[len(refs) - len(shapes) :])

        def body(sems):
            for copy in run_copies(sems, pairs):
                copy.wait()

        pl.run_scoped(body, pltpu.SemaphoreType.DMA((len(pairs),)))

    return pl.pallas_call(
        kernel,
        in_specs=[SCALARS] + [ANYWHERE] * (count + len(after) + len(kept)),
        out_specs=[ANYWHERE] * len(shapes),
        out_shape=[space(shape, BF16) for shape in shapes],
        input_output_aliases={1 + count + len(after) + i: i for i in range(len(kept))},
        compiler_params=pltpu.CompilerParams(vmem_limit_bytes=4 * 2**20),
        name=name,
    )(spots, *settled(parts), *after, *settled(kept))


def weight_copies(gathered_ref, weights):
    space, groups, tm = gathered_ref.shape[:3]
    return [
        (gathered_ref.at[s, g, t], weights.at[(t * space + s) * groups + g])
        for t in range(tm)
        for s in range(space)
        for g in range(groups)
    ]


def attend_pair(held, results, patches, total):
    for patch in range(patches):
        rows = pl.ds(patch, total, stride=patches)
        done = pair_back(*[ref[rows, :] for ref in held])
        for ref, value in zip(results, done):
            ref[rows, :] = value


def time_chunk(frames, blocks, token_blocks, gathered, late_grad, name, after=()):
    blocks = [*blocks, *token_blocks]
    first = late_grad is None
    count = len(blocks) // 2 if first else len(blocks)
    patches, lanes = blocks[0].shape[1:]
    total, part = count * frames, frames * patches
    rows, width = total * patches, 2 * lanes
    wide = [pltpu.VMEM(block.shape, BF16) for block in blocks]
    scratch = wide + [pltpu.VMEM((3 * frames, patches, lanes), BF16)] * count
    scratch += [pltpu.VMEM((rows, PAIR), F32)] * 7
    if first:
        space, groups, tm, share = gathered.shape[:4]
        scratch += [pltpu.VMEM((rows, width), BF16), pltpu.VMEM((space * groups * tm, share, width), BF16)]
        operands = settled((gathered,))
        copied = len(blocks) + space * groups * tm
    else:
        scratch += [pltpu.VMEM((rows, lanes), BF16)]
        operands = (late_grad,)
        copied = count + 1
    scratch += [pltpu.SemaphoreType.DMA((copied,)), pltpu.SemaphoreType.DMA((count,))]

    def kernel(*refs):
        refs = list(refs)

        def take(number):
            taken, refs[:number] = refs[:number], []
            return taken

        block_refs, extra_ref, _ = take(len(blocks)), take(1)[0], take(len(after))
        out_refs = take(count)
        later_ref = take(1)[0] if first else None
        blocks_in, results_out = take(len(blocks)), take(count)
        blocks_in, tokens_in = blocks_in[:count], blocks_in[count:]
        held, results = take(4), take(3)
        grads = take(1)[0]
        weights = take(1)[0] if first else None
        arrived, left = refs
        pairs = list(zip(block_refs, [*blocks_in, *tokens_in]))
        pairs += weight_copies(extra_ref, weights) if first else [(extra_ref, grads)]
        for copy in run_copies(arrived, pairs):
            copy.wait()
        if first:
            for index, ref in enumerate(tokens_in):
                value = ref[:frames].astype(F32).reshape(part, width)
                grads[index * part : (index + 1) * part, :] = value.astype(BF16)

        def one_pair(pair, carry):
            columns = pl.ds(pl.multiple_of(pair * PAIR, PAIR), PAIR)
            for index, ref in enumerate(blocks_in):
                at = slice(index * part, (index + 1) * part)
                for kind in range(3):
                    value = ref[kind * frames : (kind + 1) * frames, :, columns]
                    held[kind][at, :] = value.astype(F32).reshape(part, PAIR)
            if first:
                pieces = weights[pl.ds(pair * (PAIR // share), PAIR // share)].reshape(PAIR, width)
                held[3][...] = dot(grads[...], pieces, ((1,), (1,))).astype(BF16).astype(F32)
            else:
                held[3][...] = grads[:, columns].astype(F32)
            attend_pair(held, results, patches, total)
            for index, ref in enumerate(results_out):
                at = slice(index * part, (index + 1) * part)
                for kind in range(3):
                    value = results[kind][at, :].reshape(frames, patches, PAIR)
                    ref[kind * frames : (kind + 1) * frames, :, columns] = value.astype(BF16)
            return carry

        lax.fori_loop(0, lanes // PAIR, one_pair, 0)
        stores = run_copies(left, list(zip(results_out, out_refs)))
        if first:
            half = weights.shape[0] // 2
            later = weights[half:].reshape(lanes, width)
            later_ref[...] = dot(grads[...], later, ((1,), (1,))).astype(BF16)
        for store in stores:
            store.wait()

    out_shapes = [pltpu.VMEM((3 * frames, patches, lanes), BF16)] * count
    out_specs = [ANYWHERE] * count
    if first:
        out_shapes = out_shapes + [jax.ShapeDtypeStruct((rows, lanes), BF16)]
        out_specs = out_specs + [pl.BlockSpec(memory_space=pltpu.VMEM)]
    return pl.pallas_call(
        kernel,
        in_specs=[ANYWHERE] * (len(blocks) + 1 + len(after)),
        out_specs=out_specs,
        out_shape=out_shapes,
        scratch_shapes=scratch,
        compiler_params=BIG,
        cost_estimate=cost_of(16 if first else 10),
        name=name,
    )(*blocks, *operands, *settled(after))


def space_attention(other_core, own, far, own_tokens, weights_of, after=()):
    frames, rows, width = own_tokens.shape
    space, groups, tm, share = weights_of.shape[:4]
    pieces = space * groups * tm

    def kernel(core_ref, *refs):
        own_refs, far_refs, own_token_ref, far_token_ref, gathered_ref = refs[:3], refs[3:6], *refs[6:9]
        outs = refs[9 + len(after) : 12 + len(after)]
        weights, grads, sems = refs[12 + len(after) :]

        @pl.when(pl.program_id(0) == 0)
        def _():
            for copy in run_copies(sems, weight_copies(gathered_ref, weights)):
                copy.wait()
            whole = weights[...].reshape(width, width)
            for side in range(2):
                flat = (far_token_ref[0] if side else own_token_ref[...]).reshape(frames * rows, width)
                made = dot(flat, whole, ((1,), (1,))).astype(BF16)
                grads[side] = made.reshape(frames, rows, width)

        frame = pl.program_id(0)
        for pair in range(width // PAIR):
            columns = slice(pair * PAIR, (pair + 1) * PAIR)
            operands = [
                (near[0, :, columns].astype(F32), away[0, 0, :, columns].astype(F32))
                for near, away in zip(own_refs, far_refs)
            ]
            operands.append(tuple(grads[side, frame, :, columns].astype(F32) for side in range(2)))
            for out, value in zip(outs, own_back(*operands)):
                out[0, :, columns] = value.astype(BF16)

    near = pl.BlockSpec((1, rows, width), lambda f, core_ref: (f, 0, 0))
    near_all = pl.BlockSpec((frames, rows, width), lambda f, core_ref: (0, 0, 0))
    away = pl.BlockSpec((1, 1, rows, width), lambda f, core_ref: (core_ref[0], f, 0, 0))
    away_all = pl.BlockSpec((1, frames, rows, width), lambda f, core_ref: (core_ref[0], 0, 0, 0))
    return pl.pallas_call(
        kernel,
        grid_spec=pltpu.PrefetchScalarGridSpec(
            num_scalar_prefetch=1,
            grid=(frames,),
            in_specs=[near] * 3 + [away] * 3 + [near_all, away_all] + [ANYWHERE] * (1 + len(after)),
            out_specs=[near] * 3,
            scratch_shapes=[
                pltpu.VMEM((pieces, share, width), BF16),
                pltpu.VMEM((2, frames, rows, width), BF16),
                pltpu.SemaphoreType.DMA((pieces,)),
            ],
        ),
        out_shape=[jax.ShapeDtypeStruct((frames, rows, width), BF16)] * 3,
        compiler_params=BIG,
        cost_estimate=cost_of(20),
        name="space_attention",
    )(other_core, *settled([*own, *far[:3], own_tokens, far[3], weights_of, *after]))


def per_device(sizes, grad_out, time_q, time_k, time_v, space_q, space_k, space_v, time_wo, space_wo):
    frames, rows, width = grad_out.shape
    groups, tm, space = sizes
    patches, half = rows // tm, width // 2
    group, me = lax.axis_index("groups"), lax.axis_index("tm")
    share = time_wo.shape[0] // groups
    spots = jnp.concatenate([me ^ jnp.arange(tm, dtype=jnp.int32), group.reshape(1)]).astype(jnp.int32)
    other_core = (1 - lax.axis_index("space")).reshape(1).astype(jnp.int32)
    order = [0]
    for k in range(1, tm // 2):
        order += [k, k + tm // 2 - 1]
    order.append(tm - 1)

    def to_partner(tensor, k):
        return lax.ppermute(tensor, "tm", [(i, i ^ k) for i in range(tm)]) if k else tensor

    def moved_one(parts, shape, plan, name, after=(), space=pltpu.HBM):
        one = lambda at, refs, outs: plan(at, refs, outs[0])
        return moved(spots, parts, [shape], one, name, after, (), space)[0]

    split = [t.reshape(frames, tm, patches, width) for t in (time_q, time_k, time_v, grad_out)]
    blocks = share // patches
    time_pieces, space_pieces = (t.reshape(groups, blocks, patches, width) for t in (time_wo, space_wo))

    def token_plan(at, parts, outs):
        pairs = []
        for k, out in zip(order, outs):
            pairs.append((parts[0].at[:, at[k]], out.at[pl.ds(0, frames)]))
            pairs.append((parts[1].at[at[tm]], out.at[pl.ds(frames, blocks)]))
        return pairs

    def chunk_plan(chunk, at, parts, outs):
        columns = pl.ds(chunk * half, half)
        pairs = []
        for k, out in zip(order, outs):
            for i in range(3):
                pairs.append((parts[i].at[:, at[k], :, columns], out.at[pl.ds(i * frames, frames)]))
            for part in parts[3:]:
                for side in range(2):
                    kept = out.at[pl.ds(3 * frames + side * blocks, blocks)]
                    pairs.append((part.at[at[tm], :, :, pl.ds(side * half, half)], kept))
        return pairs

    def exchange(tensors):
        arrived = [to_partner(tensor, k) for k, tensor in zip(order, tensors)]
        return [pltpu.with_memory_space_constraint(tensor, pltpu.VMEM) for tensor in arrived]

    sent_tokens = moved(
        spots, [split[3], time_pieces], [(frames + blocks, patches, width)] * tm, token_plan, "token_payloads"
    )
    tokens = exchange(sent_tokens)
    first_sent = moved(
        spots,
        [*split[:3], space_pieces],
        [(3 * frames + 2 * blocks, patches, half)] * tm,
        functools.partial(chunk_plan, 0),
        "first_payloads",
        (sent_tokens[0],),
    )
    early = exchange(first_sent)
    second_plan = functools.partial(chunk_plan, 1)
    shapes = [(3 * frames, patches, half)] * tm
    second_sent = moved(spots, split[:3], shapes, second_plan, "second_payloads", (first_sent[0],))
    late = exchange(second_sent)

    far = [lax.all_gather(tensor, "space", axis=0) for tensor in (space_q, space_k, space_v, grad_out)]

    def gathered(column):
        whole = lax.all_gather(column, ("space", "groups"), axis=0, tiled=True)
        return whole.reshape(space, groups, tm, share, width)

    time_weights = gathered(
        moved_one(
            tokens,
            (tm, blocks, patches, width),
            lambda at, refs, out: [
                (ref.at[pl.ds(frames, blocks)], out.at[at[k]]) for k, ref in zip(order, refs)
            ],
            "time_column",
            (first_sent[0],),
        )
    )
    space_weights = gathered(
        moved_one(
            early,
            (tm, blocks, patches, width),
            lambda at, refs, out: [
                (
                    ref.at[pl.ds(3 * frames + side * blocks, blocks)],
                    out.at[at[k], :, :, pl.ds(side * half, half)],
                )
                for k, ref in zip(order, refs)
                for side in range(2)
            ],
            "space_column",
            (second_sent[0],),
        )
    )

    *done, late_grad = time_chunk(frames, early, tokens, time_weights, None, "time_first")
    back = exchange(done)
    done = time_chunk(frames, late, (), None, late_grad, "time_second")
    back2 = exchange(done)

    def place(chunk):
        def plan(at, refs, outs):
            columns = pl.ds(chunk * half, half)
            return [
                (ref.at[pl.ds(kind * frames, frames)], outs[kind].at[:, at[k], :, columns])
                for k, ref in zip(order, refs)
                for kind in range(3)
            ]

        return plan

    shapes = [(frames, tm, patches, width)] * 3
    outs = moved(spots, back, shapes, place(0), "place_first", (), (), pltpu.HBM)
    space_out = space_attention(
        other_core,
        (space_q, space_k, space_v),
        far,
        grad_out,
        space_weights,
        (outs[0],),
    )
    outs = moved(spots, back2, shapes, place(1), "place_second", settled(space_out), outs, pltpu.HBM)
    time_out = [out.reshape(frames, rows, width) for out in outs]
    return (*time_out, *space_out)


def per_device_plain(sizes, grad_out, time_q, time_k, time_v, space_q, space_k, space_v, time_wo, space_wo):
    frames, rows, width = grad_out.shape
    groups, tm, space = sizes
    patches = rows // tm

    def to_patches(tensor):
        split = tensor.reshape(tensor.shape[:-2] + (tm, patches, width))
        return jnp.moveaxis(split, -3, 0)

    def exchanged(tensor):
        return lax.all_to_all(tensor, "tm", split_axis=0, concat_axis=0, tiled=True)

    time_qkv = exchanged(to_patches(jnp.stack([time_q, time_k, time_v])))

    both_wo = jnp.concatenate([time_wo, space_wo], axis=1)
    share = both_wo.shape[0] // groups
    if share * groups == both_wo.shape[0]:
        piece = lax.dynamic_slice_in_dim(both_wo, lax.axis_index("groups") * share, share, 0)
        whole = lax.all_gather(piece, ("tm", "space", "groups"), axis=0, tiled=True)
    else:
        whole = lax.all_gather(both_wo, ("tm", "space"), axis=0, tiled=True)

    far = [lax.all_gather(tensor, "space", axis=0) for tensor in (space_q, space_k, space_v, grad_out)]
    tokens = grad_out.reshape(frames * rows, width)
    time_grad = jnp.einsum("td,cd->tc", tokens, whole[:, :width], preferred_element_type=F32)
    time_grad = exchanged(to_patches(time_grad.astype(BF16).reshape(frames, rows, width)))
    pieces = whole[:, width:].reshape(tm, space, -1, 1, width)
    pieces = jnp.moveaxis(pieces.reshape(tm, space, 1, -1, width), 0, 2)
    space_out = space_attention(
        (1 - lax.axis_index("space")).reshape(1).astype(jnp.int32), (space_q, space_k, space_v), far, grad_out, pieces
    )

    back = exchanged(time_attention(time_qkv, time_grad))
    time_out = [jnp.moveaxis(back[:, index], 0, 1).reshape(frames, rows, width) for index in range(3)]
    return (*time_out, *space_out)


def solution(mesh):
    tokens = P(("groups", "tm"), "space", None)
    weights = P(("tm", "space"), None)
    sizes = tuple(mesh.shape[name] for name in ("groups", "tm", "space"))
    groups, tm, space = sizes
    paired = groups == 2 and space == 2 and tm % 2 == 0 and tm & (tm - 1) == 0

    def body(*tensors):
        patches, rows = tensors[0].shape[1] // tm, tensors[-1].shape[0]
        fits = paired and patches % 8 == 0 and rows % (16 * groups) == 0 and rows % (groups * patches) == 0
        return (per_device if fits else per_device_plain)(sizes, *tensors)

    return jax.shard_map(
        body,
        mesh=mesh,
        in_specs=(tokens,) * 7 + (weights,) * 2,
        out_specs=(tokens,) * 6,
        check_vma=False,
    )
```
